32 devices in a mesh: prow: 8 (over z, y), pcol: 4 (over x, core).
Axes of the slice: x: 2, y: 2, z: 4, core: 2. Of those that a mesh axis runs over, the one named last changes fastest.
Arguments:
- matrix: float32 [4096, 11, 4, 256], P('prow', None, 'pcol'), may hold values from -6 to 6
Outputs:
- r_factor: float32 [512, 11, 4, 256], P('prow', None, 'pcol')
- remainder: float32 [4096, 11, 4, 256], P('prow', None, 'pcol')
The draws below stay inside these ranges and needn't reach their ends.
All inputs are finite; a program needn't handle non-finite values.
Results may differ from the reference program's by a relative error of at most 0.0003.
Values sent between devices are 32-bit elements; how exact they have to be, the bound alone decides.
No kernel may reach another device: no remote copies, remote signals or barrier semaphores. Data moves between devices by JAX's collectives and lax.ppermute only.
A program may use at most 192 MiB of HBM per device.

```python
import jax
import jax.numpy as jnp
from jax import lax

PW = 256
CPD = 11
ROWS = 4096
COLS = 11264
N_PCOL = 4


def draw_matrix(key, part):
    key = jax.random.fold_in(key, 11)
    dims = (ROWS, CPD, N_PCOL, PW)
    position = jnp.arange(PW, dtype=jnp.float32) / (PW - 1)
    entries = jax.random.truncated_normal(key, -6.0, 6.0, dims, jnp.float32)
    exponent = position
    grading = jnp.power(10.0, -1.0 * exponent)
    first_block = jnp.arange(CPD)[:, None, None] == 0
    panel_block = jnp.arange(N_PCOL)[None, :, None] < 2
    scaling = jnp.where(first_block & panel_block, grading[None, None, :], 1.0)
    return (entries * scaling[None]).astype(jnp.float32)


def setup_inputs(seed: int = 0) -> dict:
    streams_of = jax.random.split(jax.random.key(seed), 2)
    return {
        "matrix": draw_matrix(jax.random.fold_in(streams_of[1], 71), 0),
    }


def reference(matrix):
    full = matrix.reshape(ROWS, COLS)
    blocks = []
    for section in range(2):
        panel = full[:, section * PW:(section + 1) * PW]
        ortho, upper = jnp.linalg.qr(panel)
        signs = jnp.sign(jnp.diagonal(upper))
        ortho = ortho * signs[None, :]
        inner = jnp.dot(ortho.T, full, precision=lax.Precision.HIGHEST)
        full = full - jnp.dot(ortho, inner, precision=lax.Precision.HIGHEST)
        blocks.append(inner)
    r_factor = jnp.concatenate(blocks, axis=0).reshape(2 * PW, CPD, N_PCOL, PW)
    return (r_factor, full.reshape(ROWS, CPD, N_PCOL, PW))
```

```python
import jax
import jax.numpy as jnp
from jax import lax
from jax.sharding import PartitionSpec as P

highest = lax.Precision.HIGHEST


def dot(a, b):
    return jnp.dot(a, b, precision=highest, preferred_element_type=jnp.float32)


def flip(value, axis, bit):
    n = lax.axis_size(axis)
    return lax.ppermute(value, axis, [(i, i ^ bit) for i in range(n)])


def both_panels(own):
    n = lax.axis_size("pcol")
    col = lax.axis_index("pcol")
    held = own
    reach = 2
    while reach < n:
        pairs = [(i, i + reach) for i in range(reach) if i + reach < n]
        came = lax.ppermute(held, "pcol", pairs)
        held = jnp.where((col >= reach) & (col < 2 * reach), came, held)
        reach *= 2
    other = flip(held, "pcol", 1)
    first = col % 2 == 0
    return jnp.where(first, held, other), jnp.where(first, other, held)


def sum_rows(value):
    n = lax.axis_size("prow")
    bit = 1
    while bit < n:
        value = value + flip(value, "prow", bit)
        bit *= 2
    return value


def gather_columns(value):
    n = lax.axis_size("pcol")
    col = lax.axis_index("pcol")
    held = value[None]
    order = [0]
    bit = n // 2
    while bit >= 1:
        came = flip(held, "pcol", bit)
        low = (col & bit) == 0
        held = jnp.concatenate([jnp.where(low, held, came), jnp.where(low, came, held)], 0)
        order = order + [o + bit for o in order]
        bit //= 2
    return jnp.concatenate([held[order.index(i)] for i in range(n)], 0)


def local(matrix):
    rows, blocks, _, width = matrix.shape
    a = matrix[:, :, 0, :]
    p0, p1 = both_panels(a[:, 0, :])
    panels = jnp.concatenate([p0, p1], 1)
    depth = 2 * width
    share = depth // lax.axis_size("pcol")
    mine = lax.dynamic_slice_in_dim(panels, lax.axis_index("pcol") * share, share, 1)
    gram = gather_columns(sum_rows(dot(mine.T, panels)))
    inner = lax.psum(jnp.einsum("rw,rcv->wcv", panels, a, precision=highest), "prow")
    low = jnp.linalg.cholesky(gram)
    low_inv = jax.scipy.linalg.solve_triangular(low, jnp.eye(depth, dtype=jnp.float32), lower=True)
    ortho = dot(panels, low_inv.T)
    weights = dot(ortho, low_inv)
    rest = a - jnp.einsum("rw,wcv->rcv", weights, inner, precision=highest)
    per_device = depth // lax.axis_size("prow")
    my_rows = lax.dynamic_slice_in_dim(low_inv, lax.axis_index("prow") * per_device, per_device, 0)
    factor = jnp.einsum("kw,wcv->kcv", my_rows, inner, precision=highest)
    return (factor[:, :, None, :], rest[:, :, None, :])


def solution(mesh):
    placed = P("prow", None, "pcol", None)
    return jax.shard_map(
        local, mesh=mesh, in_specs=(placed,), out_specs=(placed, placed), check_vma=False
    )
```

```python
import functools

import jax
import jax.numpy as jnp
from jax import lax
from jax.experimental import pallas as pl
from jax.experimental.pallas import tpu as pltpu
from jax.sharding import PartitionSpec as P

highest = lax.Precision.HIGHEST
f32 = jnp.float32
TILE = 128
CHUNKS = (1, 2, 2, 2, 2, 2)


def dot(a, b):
    return jnp.dot(a, b, precision=highest, preferred_element_type=f32)


def dot_t(a, b):
    return lax.dot_general(a, b, (((0,), (0,)), ((), ())), precision=highest, preferred_element_type=f32)


def dot_nt(a, b):
    return lax.dot_general(a, b, (((1,), (1,)), ((), ())), precision=highest, preferred_element_type=f32)


def flip(value, axis, bit):
    n = lax.axis_size(axis)
    return lax.ppermute(value, axis, [(i, i ^ bit) for i in range(n)])


def both_panels(own):
    n = lax.axis_size("pcol")
    col = lax.axis_index("pcol")
    held = own
    reach = 2
    while reach < n:
        pairs = [(i, i + reach) for i in range(reach) if i + reach < n]
        came = lax.ppermute(held, "pcol", pairs)
        held = jnp.where((col >= reach) & (col < 2 * reach), came, held)
        reach *= 2
    other = flip(held, "pcol", 1)
    first = col % 2 == 0
    return jnp.where(first, held, other), jnp.where(first, other, held)


def sum_line(value):
    n = lax.axis_size("prow")
    if n != 8:
        bit = 2
        while bit < n:
            value = value + flip(value, "prow", bit)
            bit *= 2
        return value
    place = lax.axis_index("prow") // 2
    inner = (place == 1) | (place == 2)
    value = value + lax.ppermute(value, "prow", [(0, 2), (1, 3), (6, 4), (7, 5)])
    value = value + lax.ppermute(value, "prow", [(2, 4), (3, 5), (4, 2), (5, 3)])
    came = lax.ppermute(value, "prow", [(2, 0), (3, 1), (4, 6), (5, 7)])
    return jnp.where(inner, value, came)


def sum_halves(send, keep):
    total = sum_line(keep + flip(send, "prow", 1))
    return total, flip(total, "prow", 1)


def gather_columns(value):
    n = lax.axis_size("pcol")
    col = lax.axis_index("pcol")
    held = value[None]
    order = [0]
    bit = n // 2
    while bit >= 1:
        came = flip(held, "pcol", bit)
        low = (col & bit) == 0
        held = jnp.concatenate([jnp.where(low, held, came), jnp.where(low, came, held)], 0)
        order = order + [o + bit for o in order]
        bit //= 2
    return jnp.concatenate([held[order.index(i)] for i in range(n)], 0)


def spread_kernel(parts, in_ref, out_ref):
    rows = out_ref.shape[0]
    for part in range(parts):
        out_ref[:, part * TILE:(part + 1) * TILE] = in_ref[pl.ds(part, rows, stride=parts), :]


def natural(flat, rows, parts):
    step = min(rows, 128)
    return pl.pallas_call(
        functools.partial(spread_kernel, parts),
        grid=(rows // step,),
        out_shape=jax.ShapeDtypeStruct((rows, parts * TILE), f32),
        in_specs=[pl.BlockSpec((step * parts, TILE), lambda i: (i, 0))],
        out_specs=pl.BlockSpec((step, parts * TILE), lambda i: (i, 0)),
        name="rows_to_tiles",
    )(flat)


def eliminate(block):
    size = block.shape[0]
    sub = lax.broadcasted_iota(jnp.int32, (size, size), 0)
    lane = lax.broadcasted_iota(jnp.int32, (size, size), 1)
    left = block
    right = jnp.where(sub == lane, 1.0, 0.0).astype(f32)
    rows = []
    for j in range(size):
        at = j % 8
        pivot = left[at:at + 1, :]
        other = right[at:at + 1, :]
        head = left[at:at + 1, j:j + 1]
        rows.append((other, head))
        if j % 8 == 7:
            left = left[8:]
            right = right[8:]
            base = 8
        else:
            base = 0
        if j == size - 1:
            break
        column = left[:, j:j + 1] * (1.0 / head)
        left = left - column * pivot
        right = right - column * other
    return rows


def factor_kernel(step, gram_ref, state_ref, inv_ref, out_state_ref, out_inv_ref, inv_rows):
    size = state_ref.shape[0]
    lo, hi = step * TILE, (step + 1) * TILE
    if step == 0:
        half = size // 2
        out_state_ref[:half, :half] = gram_ref[:half]
        out_state_ref[half:, :half] = gram_ref[half:size]
        out_state_ref[half:, half:] = gram_ref[size:]
        sub = lax.broadcasted_iota(jnp.int32, (size, size), 0)
        lane = lax.broadcasted_iota(jnp.int32, (size, size), 1)
        out_inv_ref[...] = jnp.where(sub == lane, 1.0, 0.0).astype(f32)
    else:
        out_state_ref[...] = state_ref[...]
        out_inv_ref[...] = inv_ref[...]
    rows = eliminate(out_state_ref[lo:hi, lo:hi])
    for j, (row, head) in enumerate(rows):
        inv_rows[j:j + 1, :] = row * lax.rsqrt(head)
    block_inv = inv_rows[...]
    done = dot(block_inv, out_inv_ref[lo:hi, :hi])
    out_inv_ref[lo:hi, :hi] = done
    if hi < size:
        below = dot_nt(out_state_ref[hi:, lo:hi], block_inv)
        out_state_ref[hi:, hi:] = out_state_ref[hi:, hi:] - dot_nt(below, below)
        out_inv_ref[hi:, :hi] = out_inv_ref[hi:, :hi] - dot(below, done)


def factor_inverse(gram):
    size = 2 * gram.shape[1]
    state = inverse = jnp.zeros((size, size), f32)
    full = pl.BlockSpec(memory_space=pltpu.VMEM)
    for step in range(size // TILE):
        state, inverse = pl.pallas_call(
            functools.partial(factor_kernel, step),
            out_shape=[jax.ShapeDtypeStruct((size, size), f32)] * 2,
            in_specs=[full] * 3,
            out_specs=[full] * 2,
            scratch_shapes=[pltpu.VMEM((TILE, TILE), f32)],
            name="factor_step",
            cost_estimate=pl.CostEstimate(flops=3 * 10**9, bytes_accessed=4 * 10**6, transcendentals=128),
        )(gram, state, inverse)
    return inverse


def finish_kernel(widths, parts, own_rows, a_ref, keep_ref, other_ref, mine_keep_ref, mine_other_ref, *refs):
    n = len(widths)
    totals, others = refs[:n], refs[n:2 * n]
    rest_ref, factor_ref = refs[2 * n:]
    rows = keep_ref.shape[0]
    keep, other = keep_ref[...], other_ref[...]
    part = 0
    for which, width in enumerate(widths):
        for piece in range(width):
            cut = slice(piece * 2 * TILE, (piece + 1) * 2 * TILE)
            first, second = totals[which][:, cut], others[which][:, cut]
            change = dot(keep, first) + dot(other, second)
            for side in range(2):
                at = pl.ds(part + side, rows, stride=parts)
                rest_ref[at, :] = a_ref[at, :] - change[:, side * TILE:(side + 1) * TILE]

            @pl.when(pl.program_id(0) == 0)
            def _():
                mine = dot(mine_keep_ref[...], first) + dot(mine_other_ref[...], second)
                for side in range(2):
                    at = pl.ds(part + side, own_rows, stride=parts)
                    factor_ref[at, :] = mine[:, side * TILE:(side + 1) * TILE]

            part += 2


def finish(flat, keep, other, mine_keep, mine_other, widths, totals, others, parts):
    rows = keep.shape[0]
    own_rows = mine_keep.shape[0]
    step = min(rows, 128)
    whole = lambda v: pl.BlockSpec(v.shape, lambda i: (0, 0))
    by_rows = lambda v: pl.BlockSpec((step, v.shape[1]), lambda i: (i, 0))
    flat_rows = pl.BlockSpec((step * parts, TILE), lambda i: (i, 0))
    small = [mine_keep, mine_other, *totals, *others]
    return pl.pallas_call(
        functools.partial(finish_kernel, widths, parts, own_rows),
        grid=(rows // step,),
        out_shape=[
            jax.ShapeDtypeStruct(flat.shape, f32),
            jax.ShapeDtypeStruct((own_rows * parts, TILE), f32),
        ],
        in_specs=[flat_rows, by_rows(keep), by_rows(other)] + [whole(v) for v in small],
        out_specs=[flat_rows, pl.BlockSpec((own_rows * parts, TILE), lambda i: (0, 0))],
        compiler_params=pltpu.CompilerParams(vmem_limit_bytes=48 * 2**20),
        name="finish",
    )(flat, keep, other, *small)


def local(matrix):
    rows, blocks, _, width = matrix.shape
    parts = blocks * width // TILE
    depth = 2 * width
    n_row, n_col = lax.axis_size("prow"), lax.axis_size("pcol")
    first = lax.axis_index("prow") % 2 == 0
    flat = matrix.reshape(rows * parts, TILE)
    p0, p1 = both_panels(matrix[:, 0, 0, :])
    a = natural(flat, rows, parts)

    stack = jnp.concatenate([dot_t(p0, p0), dot_t(p1, p0), dot_t(p1, p1)], 0)
    share = stack.shape[0] // n_col
    mine = lax.dynamic_slice_in_dim(stack, lax.axis_index("pcol") * share, share, 0)
    top, bottom = mine[:share // 2], mine[share // 2:]
    kept, came = sum_halves(jnp.where(first, bottom, top), jnp.where(first, top, bottom))
    gram = gather_columns(
        jnp.concatenate([jnp.where(first, kept, came), jnp.where(first, came, kept)], 0)
    )

    p_keep, p_send = jnp.where(first, p0, p1), jnp.where(first, p1, p0)
    totals, others = [], []
    at = 0
    for count in CHUNKS:
        cut = a[:, at * width:(at + count) * width]
        total, other = sum_halves(dot_t(p_send, cut), dot_t(p_keep, cut))
        totals.append(total)
        others.append(other)
        at += count

    inverse = factor_inverse(gram)
    ortho = dot_nt(jnp.concatenate([p0, p1], 1), inverse)
    inv0, inv1 = inverse[:, :width], inverse[:, width:]
    inv_keep, inv_other = jnp.where(first, inv0, inv1), jnp.where(first, inv1, inv0)
    per_device = depth // n_row
    start = lax.axis_index("prow") * per_device
    mine_keep = lax.dynamic_slice_in_dim(inv_keep, start, per_device, 0)
    mine_other = lax.dynamic_slice_in_dim(inv_other, start, per_device, 0)
    rest, factor = finish(
        flat, dot(ortho, inv_keep), dot(ortho, inv_other), mine_keep, mine_other,
        CHUNKS, totals, others, parts,
    )
    return (
        factor.reshape(per_device, blocks, 1, width),
        rest.reshape(rows, blocks, 1, width),
    )


def solution(mesh):
    placed = P("prow", None, "pcol", None)
    return jax.shard_map(
        local, mesh=mesh, in_specs=(placed,), out_specs=(placed, placed), check_vma=False
    )
```

```python
import functools

import jax
import jax.numpy as jnp
from jax import lax
from jax.experimental import pallas as pl
from jax.experimental.pallas import tpu as pltpu
from jax.sharding import PartitionSpec as P

highest = lax.Precision.HIGHEST
f32 = jnp.float32
TILE = 128
SIZES = (2, 2, 2, 2, 2, 1)
ORDER = (
    "gram g1 send0 g2", "send1 g3 keep0 send2", "g4 keep1 g5 ~keep0", "send3 zm0 ch0 ~keep1",
    "~send2 send4 zm1 keep2", "zo0 ~send3 ch1 send5", "zo1 ~keep2 ~send4 keep3", "ag0 zm2 ~send5 keep4",
    "ch2 ~ag0 ~keep3 ag1", "zo2 zm3 keep5 ch3", "~ag1 zm4 ~keep5 ag2", "zo3 weights zm5 fin0",
    "fin1 zo4 fin2 ag3", "zo5 ag4 fin3 ag5", "fin4 fin5",
)


def dot(a, b):
    return jnp.dot(a, b, precision=highest, preferred_element_type=f32)


def dot_t(a, b):
    return lax.dot_general(a, b, (((0,), (0,)), ((), ())), precision=highest, preferred_element_type=f32)


def dot_nt(a, b):
    return lax.dot_general(a, b, (((1,), (1,)), ((), ())), precision=highest, preferred_element_type=f32)


def flip(value, axis, bit):
    n = lax.axis_size(axis)
    return lax.ppermute(value, axis, [(i, i ^ bit) for i in range(n)])


class Chain:
    def __init__(self):
        self.last = []
        self.waits = []

    def __call__(self, kernel, name, outs, flags, *operands, scratch=()):
        after = self.last + self.waits
        n_in, n_after = len(operands), len(after)
        vmem = pl.BlockSpec(memory_space=pltpu.VMEM)

        def body(*refs):
            skip = 1 + n_in
            kernel(*refs[:skip], *refs[skip + n_after:])

        result = pl.pallas_call(
            body,
            out_shape=[jax.ShapeDtypeStruct(o, f32) for o in outs],
            in_specs=[pl.BlockSpec(memory_space=pltpu.SMEM)] + [vmem] * n_in
            + [pl.BlockSpec(memory_space=pl.ANY)] * n_after,
            out_specs=[vmem] * len(outs),
            scratch_shapes=list(scratch),
            name=name,
            compiler_params=pltpu.CompilerParams(vmem_limit_bytes=24 * 2**20),
            cost_estimate=pl.CostEstimate(flops=1000, bytes_accessed=1000, transcendentals=0),
        )(flags, *operands, *after)
        self.last = [result[0]]
        self.waits = []
        return result


def spread_kernel(parts, flags, in_ref, out_ref):
    rows = out_ref.shape[0]
    for part in range(parts):
        out_ref[:, part * TILE:(part + 1) * TILE] = in_ref[pl.ds(part, rows, stride=parts), :]


def pick_kernel(which, flags, a_ref, b_ref, out_ref):
    @pl.when(flags[which] != 0)
    def _():
        out_ref[...] = a_ref[...]

    @pl.when(flags[which] == 0)
    def _():
        out_ref[...] = b_ref[...]


def panels_kernel(flags, held_ref, other_ref, share_ref, both_ref, keep_ref, send_ref, stack):
    width = held_ref.shape[1]
    share = share_ref.shape[0]
    held, other = held_ref[...], other_ref[...]
    low = flags[1] != 0
    p0, p1 = jnp.where(low, held, other), jnp.where(low, other, held)
    both_ref[:, :width] = p0
    both_ref[:, width:] = p1
    t0, t1 = p0.T, p1.T
    first = flags[2] != 0
    keep_ref[...] = jnp.where(first, t0, t1)
    send_ref[...] = jnp.where(first, t1, t0)
    stack[:width] = dot(t0, p0)
    stack[width:2 * width] = dot(t1, p0)
    stack[2 * width:] = dot(t1, p1)
    share_ref[...] = stack[pl.ds(pl.multiple_of(flags[4] * share, 8), share), :]


def product_kernel(lo, hi, flags, panel_ref, a_ref, out_ref):
    out_ref[...] = dot(panel_ref[...], a_ref[:, lo:hi])


def product_add_kernel(lo, hi, flags, panel_ref, a_ref, more_ref, out_ref):
    out_ref[...] = dot(panel_ref[...], a_ref[:, lo:hi]) + more_ref[...]


def add_kernel(flags, a_ref, b_ref, out_ref):
    out_ref[...] = a_ref[...] + b_ref[...]


def eliminate(block, rows_ref, heads_ref):
    size = block.shape[0]
    group = 4
    sub = lax.broadcasted_iota(jnp.int32, (size, size), 0)
    lane = lax.broadcasted_iota(jnp.int32, (size, size), 1)
    left = block
    right = jnp.where(sub == lane, 1.0, 0.0).astype(f32)
    for j in range(0, size, group):
        at = j % 8
        n = left.shape[0]
        cols = [jnp.broadcast_to(left[:, j + p:j + p + 1], (n, size)) for p in range(group)]
        rows = [left[at + p:at + p + 1] for p in range(group)]
        others = [right[at + p:at + p + 1] for p in range(group)]
        factors = []
        for p in range(group):
            head = cols[p][at + p:at + p + 1]
            factor = cols[p] * (1.0 / head)
            factors.append(factor)
            heads_ref[j + p:j + p + 1, :] = head
            rows_ref[j + p:j + p + 1, :] = others[p]
            for q in range(p + 1, group):
                cols[q] = cols[q] - factor * cols[q][at + p:at + p + 1]
                low = factor[at + q:at + q + 1]
                rows[q] = rows[q] - low * rows[p]
                others[q] = others[q] - low * others[p]
        cut = 8 if at + group == 8 else 0
        if j + group == size:
            break
        left, right = left[cut:], right[cut:]
        for p in range(group):
            left = left - factors[p][cut:] * rows[p]
            right = right - factors[p][cut:] * others[p]


def factor_kernel(step, flags, *refs):
    if step == 0:
        gram_ref, out_state_ref, out_inv_ref, rows_ref, heads_ref = refs
    else:
        state_ref, inv_ref, out_state_ref, out_inv_ref, rows_ref, heads_ref = refs
    size = out_state_ref.shape[0]
    lo, hi = step * TILE, (step + 1) * TILE
    if step == 0:
        half = size // 2
        out_state_ref[:half, :half] = gram_ref[:half]
        out_state_ref[half:, :half] = gram_ref[half:size]
        out_state_ref[half:, half:] = gram_ref[size:]
        sub = lax.broadcasted_iota(jnp.int32, (size, size), 0)
        lane = lax.broadcasted_iota(jnp.int32, (size, size), 1)
        out_inv_ref[...] = jnp.where(sub == lane, 1.0, 0.0).astype(f32)
    else:
        out_state_ref[...] = state_ref[...]
        out_inv_ref[...] = inv_ref[...]
    eliminate(out_state_ref[lo:hi, lo:hi], rows_ref, heads_ref)
    block_inv = rows_ref[...] * lax.rsqrt(heads_ref[...])
    done = dot(block_inv, out_inv_ref[lo:hi, :hi])
    out_inv_ref[lo:hi, :hi] = done
    if hi < size:
        below = dot_nt(out_state_ref[hi:, lo:hi], block_inv)
        out_state_ref[hi:, hi:] = out_state_ref[hi:, hi:] - dot_nt(below, below)
        out_inv_ref[hi:, :hi] = out_inv_ref[hi:, :hi] - dot(below, done)


def weights_kernel(flags, both_ref, inv_ref, keep_ref, other_ref, mine_ref):
    width = keep_ref.shape[1]
    per_device = mine_ref.shape[0]
    ortho = dot_nt(both_ref[...], inv_ref[...])
    half0, half1 = dot(ortho, inv_ref[:, :width]), dot(ortho, inv_ref[:, width:])
    first = flags[2] != 0
    keep_ref[...] = jnp.where(first, half0, half1)
    other_ref[...] = jnp.where(first, half1, half0)
    mine = inv_ref[pl.ds(pl.multiple_of(flags[5] * per_device, 8), per_device), :]
    left, right = mine[:, :width], mine[:, width:]
    mine_ref[:, :width] = jnp.where(first, left, right)
    mine_ref[:, width:] = jnp.where(first, right, left)


def finish_kernel(lo, flags, a_ref, keep_ref, other_ref, mine_ref, first_ref, second_ref, rest_ref, factor_ref):
    width = keep_ref.shape[1]
    first, second = first_ref[...], second_ref[...]
    change = dot(keep_ref[...], first) + dot(other_ref[...], second)
    rest_ref[...] = a_ref[:, lo:lo + first.shape[1]] - change
    mine = mine_ref[...]
    factor_ref[...] = dot(mine[:, :width], first) + dot(mine[:, width:], second)


def rows_kernel(parts, n, *refs):
    rests, factors, (rest_ref, factor_ref) = refs[:n], refs[n:2 * n], refs[2 * n:]

    def lay(pieces, out_ref):
        part = 0
        for piece in pieces:
            rows = piece.shape[0]
            for at in range(0, piece.shape[1], TILE):
                out_ref[pl.ds(part, rows, stride=parts), :] = piece[:, at:at + TILE]
                part += 1

    lay(rests, rest_ref)

    @pl.when(pl.program_id(0) == 0)
    def _():
        lay(factors, factor_ref)


def in_rows(rests, factors, parts):
    rows, own_rows = rests[0].shape[0], factors[0].shape[0]
    step = min(rows, 128)
    return pl.pallas_call(
        functools.partial(rows_kernel, parts, len(rests)),
        grid=(rows // step,),
        out_shape=[
            jax.ShapeDtypeStruct((rows * parts, TILE), f32),
            jax.ShapeDtypeStruct((own_rows * parts, TILE), f32),
        ],
        in_specs=[pl.BlockSpec((step, v.shape[1]), lambda i: (i, 0)) for v in rests]
        + [pl.BlockSpec(v.shape, lambda i: (0, 0)) for v in factors],
        out_specs=[
            pl.BlockSpec((step * parts, TILE), lambda i: (i, 0)),
            pl.BlockSpec((own_rows * parts, TILE), lambda i: (0, 0)),
        ],
        name="tiles_to_rows",
        compiler_params=pltpu.CompilerParams(vmem_limit_bytes=24 * 2**20),
    )(*rests, *factors)


def local(matrix):
    rows, blocks, _, width = matrix.shape
    parts = blocks * width // TILE
    depth = 2 * width
    n_row, n_col = lax.axis_size("prow"), lax.axis_size("pcol")
    row, col = lax.axis_index("prow"), lax.axis_index("pcol")
    place = row // 2
    line = n_row == 8
    sizes = SIZES if sum(SIZES) == blocks else (blocks,)
    flags = jnp.stack([
        col >= 2, col % 2 == 0, row % 2 == 0, (place == 1) | (place == 2), col, row,
    ]).astype(jnp.int32)
    chain = Chain()
    flat = matrix.reshape(rows * parts, TILE)

    held = matrix[:, 0, 0, :]
    reach = 2
    came = lax.ppermute(held, "pcol", [(0, 2), (1, 3)]) if n_col > 2 else held
    a, = chain(functools.partial(spread_kernel, parts), "rows_to_tiles", [(rows, parts * TILE)], flags, flat)
    held, = chain(functools.partial(pick_kernel, 0), "pick", [held.shape], flags, came, held)
    reach = 4
    while reach < n_col:
        came = lax.ppermute(held, "pcol", [(i, i + reach) for i in range(reach) if i + reach < n_col])
        held = jnp.where((col >= reach) & (col < 2 * reach), came, held)
        reach *= 2
    beside = flip(held, "pcol", 1)

    state = {}
    starts = [sum(sizes[:k]) * width for k in range(len(sizes) + 1)]

    def in_hop(value):
        return lax.ppermute(value, "prow", [(0, 2), (1, 3), (6, 4), (7, 5)]) if line else None

    def mid_hop(value):
        return lax.ppermute(value, "prow", [(2, 4), (3, 5), (4, 2), (5, 3)]) if line else None

    def out_hop(value):
        return lax.ppermute(value, "prow", [(2, 0), (3, 1), (4, 6), (5, 7)]) if line else None

    def add(name, a, b):
        if b is None:
            return a
        return chain(add_kernel, name, [a.shape], flags, a, b)[0]

    def pick_inner(name, a, b):
        if b is None:
            bit = 2
            while bit < n_row:
                a = a + flip(a, "prow", bit)
                bit *= 2
            return a
        return chain(functools.partial(pick_kernel, 3), name, [a.shape], flags, a, b)[0]

    def run(task):
        if task == "gram":
            stack = 3 * width
            share, both, keep, send = chain(
                panels_kernel, "panels",
                [(stack // n_col, width), (rows, depth), (width, rows), (width, rows)],
                flags, held, beside, scratch=[pltpu.VMEM((stack, width), f32)],
            )
            state.update(both=both, keep=keep, send=send, g=share, gr=flip(share, "prow", 1))
        elif task == "g1":
            state["g"] = add(task, state["g"], state["gr"])
            state["gr"] = in_hop(state["g"])
        elif task == "g2":
            state["g"] = add(task, state["g"], state["gr"])
            state["gr"] = mid_hop(state["g"])
        elif task == "g3":
            state["g"] = add(task, state["g"], state["gr"])
            state["gr"] = out_hop(state["g"])
        elif task == "g4":
            state["g"] = pick_inner(task, state["g"], state["gr"])
            state["shares"] = [state["g"]]
            state["which"] = [0]
            bit = n_col // 2
            while bit > 1:
                state["shares"] += [flip(v, "pcol", bit) for v in state["shares"]]
                state["which"] += [w ^ bit for w in state["which"]]
                bit //= 2
        elif task == "g5":
            shares = state["shares"] + [flip(v, "pcol", 1) for v in state["shares"]]
            which = state["which"] + [w ^ 1 for w in state["which"]]
            share = shares[0].shape[0]

            def place_kernel(flags, *refs):
                for ref, w in zip(refs, which):
                    at = pl.multiple_of((flags[4] ^ w) * share, 8)
                    refs[-1][pl.ds(at, share), :] = ref[...]

            state["gram"], = chain(place_kernel, task, [(3 * width, width)], flags, *shares)
        elif task.startswith("ch"):
            step = int(task[2:])
            operands = [state["gram"]] if step == 0 else state["factor"]
            state["factor"] = chain(
                functools.partial(factor_kernel, step), f"factor{step}", [(depth, depth)] * 2, flags, *operands,
                scratch=[pltpu.VMEM((TILE, TILE), f32)] * 2,
            )
        elif task == "weights":
            state["weights"] = chain(
                weights_kernel, task, [(rows, width), (rows, width), (depth // n_row, depth)],
                flags, state["both"], state["factor"][1],
            )
        else:
            kind, k = task.rstrip("0123456789"), int(task.lstrip("abcdefghijklmnopqrstuvwxyz"))
            if k >= len(sizes):
                return
            lo, hi = starts[k], starts[k + 1]
            if kind == "send":
                out, = chain(functools.partial(product_kernel, lo, hi), task, [(width, hi - lo)],
                             flags, state["send"], a)
                state["r", k] = flip(out, "prow", 1)
            elif kind == "keep":
                out, = chain(functools.partial(product_add_kernel, lo, hi), task, [(width, hi - lo)],
                             flags, state["keep"], a, state["r", k])
                state["s", k], state["r", k] = out, in_hop(out)
            elif kind == "zm":
                out = add(task, state["s", k], state["r", k])
                state["s", k], state["r", k] = out, mid_hop(out)
            elif kind == "zo":
                out = add(task, state["s", k], state["r", k])
                state["s", k], state["r", k] = out, out_hop(out)
            elif kind == "ag":
                out = pick_inner(task, state["s", k], state["r", k])
                state["s", k], state["r", k] = out, flip(out, "prow", 1)
            elif kind == "fin":
                state["out", k] = chain(
                    functools.partial(finish_kernel, lo), task,
                    [(rows, hi - lo), (depth // n_row, hi - lo)],
                    flags, a, *state["weights"], state["s", k], state["r", k],
                )

    for task in " ".join(ORDER).split():
        if task[0] != "~":
            run(task)
        elif line and ("r", int(task[-1])) in state:
            chain.waits.append(state["r", int(task[-1])])
    outs = [state["out", k] for k in range(len(sizes))]
    rest, factor = in_rows([o[0] for o in outs], [o[1] for o in outs], parts)
    return (
        factor.reshape(depth // n_row, blocks, 1, width),
        rest.reshape(rows, blocks, 1, width),
    )


def solution(mesh):
    placed = P("prow", None, "pcol", None)
    return jax.shard_map(
        local, mesh=mesh, in_specs=(placed,), out_specs=(placed, placed), check_vma=False
    )
```

```python
import functools

import jax
import jax.numpy as jnp
from jax import lax
from jax.experimental import pallas as pl
from jax.experimental.pallas import tpu as pltpu
from jax.sharding import PartitionSpec as P

highest = lax.Precision.HIGHEST
f32 = jnp.float32
TILE = 128
SIZES = (1, 1, 2, 2, 2, 3)
ORDER = (
    "gram send0 send1 send2", "keep0 send3 keep1 send5", "zm0 ~send2 zm1 keep2", "keep3 send4 zo0 zo1",
    "zm2 keep5 ~keep3 ag0", "zm3 ~send4 ag1 zo2", "g4 keep4 ~ag1 ~zm3", "zm5 ~zo2 zo3 g6",
    "ag2 zm4 ch0 ~ag2", "~zm5 ag3 zo5 ch1", "~ag3 zo4 ch2 ag5", "ch3 ag4 weights fin0",
    "fin1 ~ag5 fin2 fin3", "fin5 fin4",
)


def dot(a, b):
    return jnp.dot(a, b, precision=highest, preferred_element_type=f32)


def dot_t(a, b):
    return lax.dot_general(a, b, (((0,), (0,)), ((), ())), precision=highest, preferred_element_type=f32)


def dot_nt(a, b):
    return lax.dot_general(a, b, (((1,), (1,)), ((), ())), precision=highest, preferred_element_type=f32)


def flip(value, axis, bit):
    n = lax.axis_size(axis)
    return lax.ppermute(value, axis, [(i, i ^ bit) for i in range(n)])


class Chain:
    def __init__(self):
        self.last = []
        self.waits = []

    def __call__(self, kernel, name, outs, flags, *operands, scratch=()):
        after = self.last + self.waits
        n_in, n_after = len(operands), len(after)
        vmem = pl.BlockSpec(memory_space=pltpu.VMEM)

        def body(*refs):
            skip = 1 + n_in
            kernel(*refs[:skip], *refs[skip + n_after:])

        result = pl.pallas_call(
            body,
            out_shape=[jax.ShapeDtypeStruct(o, f32) for o in outs],
            in_specs=[pl.BlockSpec(memory_space=pltpu.SMEM)] + [vmem] * n_in
            + [pl.BlockSpec(memory_space=pl.ANY)] * n_after,
            out_specs=[vmem] * len(outs),
            scratch_shapes=list(scratch),
            name=name,
            compiler_params=pltpu.CompilerParams(vmem_limit_bytes=24 * 2**20),
            cost_estimate=pl.CostEstimate(flops=1000, bytes_accessed=1000, transcendentals=0),
        )(flags, *operands, *after)
        self.last = [result[0]]
        self.waits = []
        return result


def spread_kernel(parts, flags, in_ref, out_ref):
    rows = out_ref.shape[0]
    for part in range(parts):
        out_ref[:, part * TILE:(part + 1) * TILE] = in_ref[pl.ds(part, rows, stride=parts), :]


def pick_kernel(which, flags, a_ref, b_ref, out_ref):
    @pl.when(flags[which] != 0)
    def _():
        out_ref[...] = a_ref[...]

    @pl.when(flags[which] == 0)
    def _():
        out_ref[...] = b_ref[...]


def panels_kernel(flags, held_ref, other_ref, both_ref, keep_ref, send_ref, share_ref):
    width = held_ref.shape[1]
    held, other = held_ref[...], other_ref[...]
    low = flags[1] != 0
    p0, p1 = jnp.where(low, held, other), jnp.where(low, other, held)
    both_ref[:, :width] = p0
    both_ref[:, width:] = p1
    t0, t1 = p0.T, p1.T
    first = flags[2] != 0
    keep_ref[...] = jnp.where(first, t0, t1)
    send_ref[...] = jnp.where(first, t1, t0)
    for part in range(2 * width // TILE):
        @pl.when(flags[4] == part)
        def _():
            share_ref[...] = both_ref[:, part * TILE:(part + 1) * TILE]


def product_kernel(lo, hi, flags, panel_ref, a_ref, *refs):
    more, out_ref = refs[:-1], refs[-1]
    panel = panel_ref[...]
    out_ref[:, :hi - lo] = dot(panel, a_ref[:, lo:hi])
    if more:
        out_ref[:, hi - lo:] = dot(panel, more[0][...])


def product_add_kernel(lo, hi, flags, panel_ref, a_ref, came_ref, *refs):
    more, out_ref = refs[:-1], refs[-1]
    panel = panel_ref[...]
    out_ref[:, :hi - lo] = dot(panel, a_ref[:, lo:hi]) + came_ref[:, :hi - lo]
    if more:
        out_ref[:, hi - lo:] = dot(panel, more[0][...]) + came_ref[:, hi - lo:]


def share_kernel(flags, keep_ref, other_ref, out_ref):
    width = keep_ref.shape[0]
    first = flags[2] != 0
    keep, other = keep_ref[:, -TILE:], other_ref[:, -TILE:]
    out_ref[:width] = jnp.where(first, keep, other)
    out_ref[width:] = jnp.where(first, other, keep)


def gather_kernel(which, flags, *refs):
    out_ref = refs[-1]
    for part in range(out_ref.shape[1] // TILE):
        for ref, w in zip(refs, which):
            @pl.when((flags[4] ^ w) == part)
            def _():
                out_ref[:, part * TILE:(part + 1) * TILE] = ref[...]


def add_kernel(flags, a_ref, b_ref, out_ref):
    out_ref[...] = a_ref[...] + b_ref[...]


def eliminate(block, rows_ref, heads_ref):
    size = block.shape[0]
    group = 4
    sub = lax.broadcasted_iota(jnp.int32, (size, size), 0)
    lane = lax.broadcasted_iota(jnp.int32, (size, size), 1)
    left = block
    right = jnp.where(sub == lane, 1.0, 0.0).astype(f32)
    for j in range(0, size, group):
        at = j % 8
        n = left.shape[0]
        cols = [jnp.broadcast_to(left[:, j + p:j + p + 1], (n, size)) for p in range(group)]
        rows = [left[at + p:at + p + 1] for p in range(group)]
        others = [right[at + p:at + p + 1] for p in range(group)]
        factors = []
        for p in range(group):
            head = cols[p][at + p:at + p + 1]
            factor = cols[p] * (1.0 / head)
            factors.append(factor)
            heads_ref[j + p:j + p + 1, :] = head
            rows_ref[j + p:j + p + 1, :] = others[p]
            for q in range(p + 1, group):
                cols[q] = cols[q] - factor * cols[q][at + p:at + p + 1]
                low = factor[at + q:at + q + 1]
                rows[q] = rows[q] - low * rows[p]
                others[q] = others[q] - low * others[p]
        cut = 8 if at + group == 8 else 0
        if j + group == size:
            break
        left, right = left[cut:], right[cut:]
        for p in range(group):
            left = left - factors[p][cut:] * rows[p]
            right = right - factors[p][cut:] * others[p]


def factor_kernel(step, flags, *refs):
    if step == 0:
        gram_ref, out_state_ref, out_inv_ref, rows_ref, heads_ref = refs
    else:
        state_ref, inv_ref, out_state_ref, out_inv_ref, rows_ref, heads_ref = refs
    size = out_state_ref.shape[0]
    lo, hi = step * TILE, (step + 1) * TILE
    if step == 0:
        out_state_ref[...] = gram_ref[...]
        sub = lax.broadcasted_iota(jnp.int32, (size, size), 0)
        lane = lax.broadcasted_iota(jnp.int32, (size, size), 1)
        out_inv_ref[...] = jnp.where(sub == lane, 1.0, 0.0).astype(f32)
    else:
        out_state_ref[...] = state_ref[...]
        out_inv_ref[...] = inv_ref[...]
    eliminate(out_state_ref[lo:hi, lo:hi], rows_ref, heads_ref)
    block_inv = rows_ref[...] * lax.rsqrt(heads_ref[...])
    done = dot(block_inv, out_inv_ref[lo:hi, :hi])
    out_inv_ref[lo:hi, :hi] = done
    if hi < size:
        below = dot_nt(out_state_ref[hi:, lo:hi], block_inv)
        out_state_ref[hi:, hi:] = out_state_ref[hi:, hi:] - dot_nt(below, below)
        out_inv_ref[hi:, :hi] = out_inv_ref[hi:, :hi] - dot(below, done)


def weights_kernel(flags, both_ref, inv_ref, keep_ref, other_ref, mine_ref):
    width = keep_ref.shape[1]
    per_device = mine_ref.shape[0]
    ortho = dot_nt(both_ref[...], inv_ref[...])
    half0, half1 = dot(ortho, inv_ref[:, :width]), dot(ortho, inv_ref[:, width:])
    first = flags[2] != 0
    keep_ref[...] = jnp.where(first, half0, half1)
    other_ref[...] = jnp.where(first, half1, half0)
    mine = inv_ref[pl.ds(pl.multiple_of(flags[5] * per_device, 8), per_device), :]
    left, right = mine[:, :width], mine[:, width:]
    mine_ref[:, :width] = jnp.where(first, left, right)
    mine_ref[:, width:] = jnp.where(first, right, left)


def finish_kernel(lo, hi, flags, a_ref, keep_ref, other_ref, mine_ref, first_ref, second_ref, rest_ref, factor_ref):
    width = keep_ref.shape[1]
    first, second = first_ref[:, :hi - lo], second_ref[:, :hi - lo]
    change = dot(keep_ref[...], first) + dot(other_ref[...], second)
    rest_ref[...] = a_ref[:, lo:hi] - change
    mine = mine_ref[...]
    factor_ref[...] = dot(mine[:, :width], first) + dot(mine[:, width:], second)


def rows_kernel(parts, n, *refs):
    rests, factors, (rest_ref, factor_ref) = refs[:n], refs[n:2 * n], refs[2 * n:]

    def lay(pieces, out_ref):
        part = 0
        for piece in pieces:
            rows = piece.shape[0]
            for at in range(0, piece.shape[1], TILE):
                out_ref[pl.ds(part, rows, stride=parts), :] = piece[:, at:at + TILE]
                part += 1

    lay(rests, rest_ref)

    @pl.when(pl.program_id(0) == 0)
    def _():
        lay(factors, factor_ref)


def in_rows(rests, factors, parts):
    rows, own_rows = rests[0].shape[0], factors[0].shape[0]
    step = min(rows, 128)
    return pl.pallas_call(
        functools.partial(rows_kernel, parts, len(rests)),
        grid=(rows // step,),
        out_shape=[
            jax.ShapeDtypeStruct((rows * parts, TILE), f32),
            jax.ShapeDtypeStruct((own_rows * parts, TILE), f32),
        ],
        in_specs=[pl.BlockSpec((step, v.shape[1]), lambda i: (i, 0)) for v in rests]
        + [pl.BlockSpec(v.shape, lambda i: (0, 0)) for v in factors],
        out_specs=[
            pl.BlockSpec((step * parts, TILE), lambda i: (i, 0)),
            pl.BlockSpec((own_rows * parts, TILE), lambda i: (0, 0)),
        ],
        name="tiles_to_rows",
        compiler_params=pltpu.CompilerParams(vmem_limit_bytes=24 * 2**20),
    )(*rests, *factors)


def local(matrix):
    rows, blocks, _, width = matrix.shape
    parts = blocks * width // TILE
    depth = 2 * width
    n_row, n_col = lax.axis_size("prow"), lax.axis_size("pcol")
    row, col = lax.axis_index("prow"), lax.axis_index("pcol")
    place = row // 2
    line = n_row == 8
    sizes = SIZES if sum(SIZES) == blocks else (blocks,)
    flags = jnp.stack([
        col >= 2, col % 2 == 0, row % 2 == 0, (place == 1) | (place == 2), col % 4, row,
    ]).astype(jnp.int32)
    chain = Chain()
    flat = matrix.reshape(rows * parts, TILE)

    held = matrix[:, 0, 0, :]
    reach = 2
    came = lax.ppermute(held, "pcol", [(0, 2), (1, 3)]) if n_col > 2 else held
    a, = chain(functools.partial(spread_kernel, parts), "rows_to_tiles", [(rows, parts * TILE)], flags, flat)
    held, = chain(functools.partial(pick_kernel, 0), "pick", [held.shape], flags, came, held)
    reach = 4
    while reach < n_col:
        came = lax.ppermute(held, "pcol", [(i, i + reach) for i in range(reach) if i + reach < n_col])
        held = jnp.where((col >= reach) & (col < 2 * reach), came, held)
        reach *= 2
    beside = flip(held, "pcol", 1)

    state = {}
    starts = [sum(sizes[:k]) * width for k in range(len(sizes) + 1)]

    def in_hop(value):
        return lax.ppermute(value, "prow", [(0, 2), (1, 3), (6, 4), (7, 5)]) if line else None

    def mid_hop(value):
        return lax.ppermute(value, "prow", [(2, 4), (3, 5), (4, 2), (5, 3)]) if line else None

    def out_hop(value):
        return lax.ppermute(value, "prow", [(2, 0), (3, 1), (4, 6), (5, 7)]) if line else None

    def add(name, a, b):
        if b is None:
            return a
        return chain(add_kernel, name, [a.shape], flags, a, b)[0]

    def pick_inner(name, a, b):
        if b is None:
            bit = 2
            while bit < n_row:
                a = a + flip(a, "prow", bit)
                bit *= 2
            return a
        return chain(functools.partial(pick_kernel, 3), name, [a.shape], flags, a, b)[0]

    def run(task):
        if task == "gram":
            both, keep, send, share = chain(
                panels_kernel, "panels", [(rows, depth), (width, rows), (width, rows), (rows, TILE)],
                flags, held, beside,
            )
            state.update(both=both, keep=keep, send=send, more=[share])
        elif task == "g4":
            share, = chain(share_kernel, task, [(depth, TILE)], flags, state["s", 0], state["r", 0])
            came = flip(share, "pcol", 2)
            state["shares"] = [share, came, flip(share, "pcol", 1), flip(came, "pcol", 1)]
        elif task == "g6":
            state["gram"], = chain(
                functools.partial(gather_kernel, (0, 2, 1, 3)), task, [(depth, depth)], flags, *state["shares"]
            )
        elif task.startswith("ch"):
            step = int(task[2:])
            operands = [state["gram"]] if step == 0 else state["factor"]
            state["factor"] = chain(
                functools.partial(factor_kernel, step), f"factor{step}", [(depth, depth)] * 2, flags, *operands,
                scratch=[pltpu.VMEM((TILE, TILE), f32)] * 2,
            )
        elif task == "weights":
            state["weights"] = chain(
                weights_kernel, task, [(rows, width), (rows, width), (depth // n_row, depth)],
                flags, state["both"], state["factor"][1],
            )
        else:
            kind, k = task.rstrip("0123456789"), int(task.lstrip("abcdefghijklmnopqrstuvwxyz"))
            if k >= len(sizes):
                return
            lo, hi = starts[k], starts[k + 1]
            more = state["more"] if k == 0 else []
            wide = hi - lo + len(more) * TILE
            if kind == "send":
                out, = chain(functools.partial(product_kernel, lo, hi), task, [(width, wide)],
                             flags, state["send"], a, *more)
                state["r", k] = flip(out, "prow", 1)
            elif kind == "keep":
                out, = chain(functools.partial(product_add_kernel, lo, hi), task, [(width, wide)],
                             flags, state["keep"], a, state["r", k], *more)
                state["s", k], state["r", k] = out, in_hop(out)
            elif kind == "zm":
                out = add(task, state["s", k], state["r", k])
                state["s", k], state["r", k] = out, mid_hop(out)
            elif kind == "zo":
                out = add(task, state["s", k], state["r", k])
                state["s", k], state["r", k] = out, out_hop(out)
            elif kind == "ag":
                out = pick_inner(task, state["s", k], state["r", k])
                state["s", k], state["r", k] = out, flip(out, "prow", 1)
            elif kind == "fin":
                state["out", k] = chain(
                    functools.partial(finish_kernel, lo, hi), task,
                    [(rows, hi - lo), (depth // n_row, hi - lo)],
                    flags, a, *state["weights"], state["s", k], state["r", k],
                )

    for task in " ".join(ORDER).split():
        if task[0] != "~":
            run(task)
        elif line and ("r", int(task[-1])) in state:
            chain.waits.append(state["r", int(task[-1])])
    outs = [state["out", k] for k in range(len(sizes))]
    rest, factor = in_rows([o[0] for o in outs], [o[1] for o in outs], parts)
    return (
        factor.reshape(depth // n_row, blocks, 1, width),
        rest.reshape(rows, blocks, 1, width),
    )


def solution(mesh):
    placed = P("prow", None, "pcol", None)
    return jax.shard_map(
        local, mesh=mesh, in_specs=(placed,), out_specs=(placed, placed), check_vma=False
    )
```

```python
import functools

import jax
import jax.numpy as jnp
from jax import lax
from jax.experimental import pallas as pl
from jax.experimental.pallas import tpu as pltpu
from jax.sharding import PartitionSpec as P

highest = lax.Precision.HIGHEST
f32 = jnp.float32
bf16 = jnp.bfloat16
TILE = 128
SIZES = (2, 3, 3, 3)
ORDER = (
    "gram send0 send1 g1", "send2 g2 keep0 send3", "g3 keep1 g4 g6", "ch0 keep2 ch1 keep3",
    "ag0 ch2 ~ag0 ch3", "ag1 weights ~ag1 fin0", "ag2 fin1 ~ag2 ag3", "fin2 fin3",
)


def dot(a, b):
    return jnp.dot(a, b, precision=highest, preferred_element_type=f32)


def dot_t(a, b):
    return lax.dot_general(a, b, (((0,), (0,)), ((), ())), precision=highest, preferred_element_type=f32)


def dot_nt(a, b):
    return lax.dot_general(a, b, (((1,), (1,)), ((), ())), precision=highest, preferred_element_type=f32)


def split(value):
    high = value.astype(bf16)
    return high, (value - high.astype(f32)).astype(bf16)


def dot3(a, b):
    def product(x, y):
        return jnp.dot(x, y, preferred_element_type=f32)

    return product(a[0], b[0]) + (product(a[0], b[1]) + product(a[1], b[0]))


def flip(value, axis, bit):
    n = lax.axis_size(axis)
    return lax.ppermute(value, axis, [(i, i ^ bit) for i in range(n)])


class Chain:
    def __init__(self):
        self.last = []
        self.waits = []

    def __call__(self, kernel, name, outs, flags, *operands, scratch=()):
        after = self.last + self.waits
        n_in, n_after = len(operands), len(after)
        vmem = pl.BlockSpec(memory_space=pltpu.VMEM)

        def body(*refs):
            skip = 1 + n_in
            kernel(*refs[:skip], *refs[skip + n_after:])

        result = pl.pallas_call(
            body,
            out_shape=[jax.ShapeDtypeStruct(*(o if isinstance(o[0], tuple) else (o, f32))) for o in outs],
            in_specs=[pl.BlockSpec(memory_space=pltpu.SMEM)] + [vmem] * n_in
            + [pl.BlockSpec(memory_space=pl.ANY)] * n_after,
            out_specs=[vmem] * len(outs),
            scratch_shapes=list(scratch),
            name=name,
            compiler_params=pltpu.CompilerParams(vmem_limit_bytes=24 * 2**20),
            cost_estimate=pl.CostEstimate(flops=1000, bytes_accessed=1000, transcendentals=0),
        )(flags, *operands, *after)
        self.last = [result[0]]
        self.waits = []
        return result


def spread_kernel(parts, flags, in_ref, out_ref, high_ref, low_ref):
    rows = out_ref.shape[0]
    for part in range(parts):
        cut = slice(part * TILE, (part + 1) * TILE)
        value = in_ref[pl.ds(part, rows, stride=parts), :]
        out_ref[:, cut] = value
        high_ref[:, cut], low_ref[:, cut] = split(value)


def pick_kernel(which, flags, a_ref, b_ref, out_ref):
    @pl.when(flags[which] != 0)
    def _():
        out_ref[...] = a_ref[...]

    @pl.when(flags[which] == 0)
    def _():
        out_ref[...] = b_ref[...]


def panels_kernel(
    flags, held_ref, other_ref, both_ref, keep_high, keep_low, send_high, send_low, share_ref, stack
):
    width = held_ref.shape[1]
    share = share_ref.shape[0]
    held, other = held_ref[...], other_ref[...]
    low = flags[1] != 0
    p0, p1 = jnp.where(low, held, other), jnp.where(low, other, held)
    both_ref[:, :width] = p0
    both_ref[:, width:] = p1
    t0, t1 = p0.T, p1.T
    first = flags[2] != 0
    keep_high[...], keep_low[...] = split(jnp.where(first, t0, t1))
    send_high[...], send_low[...] = split(jnp.where(first, t1, t0))
    stack[:width] = dot(t0, p0)
    stack[width:2 * width] = dot(t1, p0)
    stack[2 * width:] = dot(t1, p1)
    share_ref[...] = stack[pl.ds(pl.multiple_of(flags[4] * share, 8), share), :]


def product_kernel(lo, hi, flags, panel_high, panel_low, a_high, a_low, out_ref):
    panel = panel_high[...], panel_low[...]
    out_ref[...] = dot3(panel, (a_high[:, lo:hi], a_low[:, lo:hi]))


def product_add_kernel(lo, hi, flags, panel_high, panel_low, a_high, a_low, came_ref, out_ref):
    panel = panel_high[...], panel_low[...]
    out_ref[...] = dot3(panel, (a_high[:, lo:hi], a_low[:, lo:hi])) + came_ref[...]


def gather_kernel(which, flags, *refs):
    share = refs[0].shape[0]
    for ref, w in zip(refs, which):
        at = pl.multiple_of((flags[4] ^ w) * share, 8)
        refs[-1][pl.ds(at, share), :] = ref[...]


def add_kernel(flags, a_ref, b_ref, out_ref):
    out_ref[...] = a_ref[...] + b_ref[...]


def eliminate(block, rows_ref, heads_ref):
    size = block.shape[0]
    group = 4
    sub = lax.broadcasted_iota(jnp.int32, (size, size), 0)
    lane = lax.broadcasted_iota(jnp.int32, (size, size), 1)
    left = block
    right = jnp.where(sub == lane, 1.0, 0.0).astype(f32)
    for j in range(0, size, group):
        at = j % 8
        n = left.shape[0]
        cols = [jnp.broadcast_to(left[:, j + p:j + p + 1], (n, size)) for p in range(group)]
        rows = [left[at + p:at + p + 1] for p in range(group)]
        others = [right[at + p:at + p + 1] for p in range(group)]
        factors = []
        for p in range(group):
            head = cols[p][at + p:at + p + 1]
            factor = cols[p] * (1.0 / head)
            factors.append(factor)
            heads_ref[j + p:j + p + 1, :] = head
            rows_ref[j + p:j + p + 1, :] = others[p]
            for q in range(p + 1, group):
                cols[q] = cols[q] - factor * cols[q][at + p:at + p + 1]
                low = factor[at + q:at + q + 1]
                rows[q] = rows[q] - low * rows[p]
                others[q] = others[q] - low * others[p]
        cut = 8 if at + group == 8 else 0
        if j + group == size:
            break
        left, right = left[cut:], right[cut:]
        for p in range(group):
            left = left - factors[p][cut:] * rows[p]
            right = right - factors[p][cut:] * others[p]


def factor_kernel(step, flags, *refs):
    if step == 0:
        gram_ref, out_state_ref, out_inv_ref, rows_ref, heads_ref = refs
    else:
        state_ref, inv_ref, out_state_ref, out_inv_ref, rows_ref, heads_ref = refs
    size = out_state_ref.shape[0]
    lo, hi = step * TILE, (step + 1) * TILE
    if step == 0:
        half = size // 2
        out_state_ref[:half, :half] = gram_ref[:half]
        out_state_ref[half:, :half] = gram_ref[half:size]
        out_state_ref[half:, half:] = gram_ref[size:]
        sub = lax.broadcasted_iota(jnp.int32, (size, size), 0)
        lane = lax.broadcasted_iota(jnp.int32, (size, size), 1)
        out_inv_ref[...] = jnp.where(sub == lane, 1.0, 0.0).astype(f32)
    else:
        out_state_ref[...] = state_ref[...]
        out_inv_ref[...] = inv_ref[...]
    eliminate(out_state_ref[lo:hi, lo:hi], rows_ref, heads_ref)
    block_inv = rows_ref[...] * lax.rsqrt(heads_ref[...])
    done = dot(block_inv, out_inv_ref[lo:hi, :hi])
    out_inv_ref[lo:hi, :hi] = done
    if hi < size:
        below = dot_nt(out_state_ref[hi:, lo:hi], block_inv)
        out_state_ref[hi:, hi:] = out_state_ref[hi:, hi:] - dot_nt(below, below)
        out_inv_ref[hi:, :hi] = out_inv_ref[hi:, :hi] - dot(below, done)


def weights_kernel(flags, both_ref, inv_ref, high_ref, low_ref):
    rows = both_ref.shape[0]
    width = both_ref.shape[1] // 2
    per_device = high_ref.shape[0] - rows
    ortho = dot_nt(both_ref[...], inv_ref[...])
    first = flags[2] != 0
    mine = inv_ref[pl.ds(pl.multiple_of(flags[5] * per_device, 8), per_device), :]

    def put(place, left, right):
        high_ref[place, :width], low_ref[place, :width] = split(jnp.where(first, left, right))
        high_ref[place, width:], low_ref[place, width:] = split(jnp.where(first, right, left))

    put(slice(0, rows), dot(ortho, inv_ref[:, :width]), dot(ortho, inv_ref[:, width:]))
    put(slice(rows, rows + per_device), mine[:, :width], mine[:, width:])


def finish_kernel(lo, hi, flags, a_ref, high_ref, low_ref, first_ref, second_ref, rest_ref, factor_ref):
    rows, width = a_ref.shape[0], first_ref.shape[0]
    change = dot3((high_ref[:, :width], low_ref[:, :width]), split(first_ref[...]))
    change += dot3((high_ref[:, width:], low_ref[:, width:]), split(second_ref[...]))
    rest_ref[...] = a_ref[:, lo:hi] - change[:rows]
    factor_ref[...] = change[rows:]


def rows_kernel(parts, n, *refs):
    rests, factors, (rest_ref, factor_ref) = refs[:n], refs[n:2 * n], refs[2 * n:]

    def lay(pieces, out_ref):
        part = 0
        for piece in pieces:
            rows = piece.shape[0]
            for at in range(0, piece.shape[1], TILE):
                out_ref[pl.ds(part, rows, stride=parts), :] = piece[:, at:at + TILE]
                part += 1

    lay(rests, rest_ref)

    @pl.when(pl.program_id(0) == 0)
    def _():
        lay(factors, factor_ref)


def in_rows(rests, factors, parts):
    rows, own_rows = rests[0].shape[0], factors[0].shape[0]
    step = min(rows, 128)
    return pl.pallas_call(
        functools.partial(rows_kernel, parts, len(rests)),
        grid=(rows // step,),
        out_shape=[
            jax.ShapeDtypeStruct((rows * parts, TILE), f32),
            jax.ShapeDtypeStruct((own_rows * parts, TILE), f32),
        ],
        in_specs=[pl.BlockSpec((step, v.shape[1]), lambda i: (i, 0)) for v in rests]
        + [pl.BlockSpec(v.shape, lambda i: (0, 0)) for v in factors],
        out_specs=[
            pl.BlockSpec((step * parts, TILE), lambda i: (i, 0)),
            pl.BlockSpec((own_rows * parts, TILE), lambda i: (0, 0)),
        ],
        name="tiles_to_rows",
        compiler_params=pltpu.CompilerParams(vmem_limit_bytes=24 * 2**20),
    )(*rests, *factors)


def local(matrix):
    rows, blocks, _, width = matrix.shape
    parts = blocks * width // TILE
    depth = 2 * width
    n_row, n_col = lax.axis_size("prow"), lax.axis_size("pcol")
    row, col = lax.axis_index("prow"), lax.axis_index("pcol")
    place = row // 2
    line = n_row == 8
    sizes = SIZES if sum(SIZES) == blocks else (blocks,)
    flags = jnp.stack([
        col >= 2, col % 2 == 0, row % 2 == 0, (place == 1) | (place == 2), col, row,
    ]).astype(jnp.int32)
    chain = Chain()
    flat = matrix.reshape(rows * parts, TILE)

    held = matrix[:, 0, 0, :]
    reach = 2
    came = lax.ppermute(held, "pcol", [(0, 2), (1, 3)]) if n_col > 2 else held
    wide = (rows, parts * TILE)
    a, *a_split = chain(
        functools.partial(spread_kernel, parts), "rows_to_tiles", [wide, (wide, bf16), (wide, bf16)], flags, flat
    )
    held, = chain(functools.partial(pick_kernel, 0), "pick", [held.shape], flags, came, held)
    reach = 4
    while reach < n_col:
        came = lax.ppermute(held, "pcol", [(i, i + reach) for i in range(reach) if i + reach < n_col])
        held = jnp.where((col >= reach) & (col < 2 * reach), came, held)
        reach *= 2
    beside = flip(held, "pcol", 1)

    state = {}
    starts = [sum(sizes[:k]) * width for k in range(len(sizes) + 1)]

    def in_hop(value):
        return lax.ppermute(value, "prow", [(0, 2), (1, 3), (6, 4), (7, 5)]) if line else None

    def mid_hop(value):
        return lax.ppermute(value, "prow", [(2, 4), (3, 5), (4, 2), (5, 3)]) if line else None

    def out_hop(value):
        return lax.ppermute(value, "prow", [(2, 0), (3, 1), (4, 6), (5, 7)]) if line else None

    def add(name, a, b):
        if b is None:
            return a
        return chain(add_kernel, name, [a.shape], flags, a, b)[0]

    def pick_inner(name, a, b):
        if b is None:
            bit = 2
            while bit < n_row:
                a = a + flip(a, "prow", bit)
                bit *= 2
            return a
        return chain(functools.partial(pick_kernel, 3), name, [a.shape], flags, a, b)[0]

    def run(task):
        if task == "gram":
            cut = ((width, rows), bf16)
            both, *panels, share = chain(
                panels_kernel, "panels", [(rows, depth)] + [cut] * 4 + [(3 * width // n_col, width)],
                flags, held, beside, scratch=[pltpu.VMEM((3 * width, width), f32)],
            )
            state.update(both=both, keep=panels[:2], send=panels[2:], g=share, gr=flip(share, "prow", 1))
        elif task == "g1":
            state["g"] = add(task, state["g"], state["gr"])
            state["gr"] = in_hop(state["g"])
        elif task == "g2":
            state["g"] = add(task, state["g"], state["gr"])
            state["gr"] = mid_hop(state["g"])
        elif task == "g3":
            state["g"] = add(task, state["g"], state["gr"])
            state["gr"] = out_hop(state["g"])
        elif task == "g4":
            state["g"] = pick_inner(task, state["g"], state["gr"])
            state["shares"] = [state["g"]]
            state["which"] = [0]
            bit = n_col // 2
            while bit >= 1:
                state["shares"] += [flip(v, "pcol", bit) for v in state["shares"]]
                state["which"] += [w ^ bit for w in state["which"]]
                bit //= 2
        elif task == "g6":
            state["gram"], = chain(
                functools.partial(gather_kernel, state["which"]), task, [(3 * width, width)], flags, *state["shares"]
            )
        elif task.startswith("ch"):
            step = int(task[2:])
            operands = [state["gram"]] if step == 0 else state["factor"]
            state["factor"] = chain(
                functools.partial(factor_kernel, step), f"factor{step}", [(depth, depth)] * 2, flags, *operands,
                scratch=[pltpu.VMEM((TILE, TILE), f32)] * 2,
            )
        elif task == "weights":
            cut = ((rows + depth // n_row, depth), bf16)
            state["weights"] = chain(weights_kernel, task, [cut] * 2, flags, state["both"], state["factor"][1])
        else:
            kind, k = task.rstrip("0123456789"), int(task.lstrip("abcdefghijklmnopqrstuvwxyz"))
            if k >= len(sizes):
                return
            lo, hi = starts[k], starts[k + 1]
            if kind == "send":
                out, = chain(functools.partial(product_kernel, lo, hi), task, [(width, hi - lo)],
                             flags, *state["send"], *a_split)
                state["r", k] = flip(out, "prow", 1)
            elif kind == "keep":
                out, = chain(functools.partial(product_add_kernel, lo, hi), task, [(width, hi - lo)],
                             flags, *state["keep"], *a_split, state["r", k])
                groups = [[i for i in range(n_row) if i % 2 == half] for half in range(2)]
                groups = [g[::-1] if k & 2 else g for g in (groups[::-1] if k & 1 else groups)]
                state["s", k] = lax.psum(out, "prow", axis_index_groups=groups)
            elif kind == "ag":
                state["r", k] = flip(state["s", k], "prow", 1)
            elif kind == "fin":
                state["out", k] = chain(
                    functools.partial(finish_kernel, lo, hi), task,
                    [(rows, hi - lo), (depth // n_row, hi - lo)],
                    flags, a, *state["weights"], state["s", k], state["r", k],
                )

    for task in " ".join(ORDER).split():
        if task[0] != "~":
            run(task)
        elif ("r", int(task[-1])) in state:
            chain.waits.append(state["r", int(task[-1])])
    outs = [state["out", k] for k in range(len(sizes))]
    rest, factor = in_rows([o[0] for o in outs], [o[1] for o in outs], parts)
    return (
        factor.reshape(depth // n_row, blocks, 1, width),
        rest.reshape(rows, blocks, 1, width),
    )


def solution(mesh):
    placed = P("prow", None, "pcol", None)
    return jax.shard_map(
        local, mesh=mesh, in_specs=(placed,), out_specs=(placed, placed), check_vma=False
    )
```

```python
import functools

import jax
import jax.numpy as jnp
from jax import lax
from jax.experimental import pallas as pl
from jax.experimental.pallas import tpu as pltpu
from jax.sharding import PartitionSpec as P

highest = lax.Precision.HIGHEST
f32 = jnp.float32
bf16 = jnp.bfloat16
TILE = 128
SIZES = (2, 2, 2, 2, 2, 1)
ORDER = (
    "gram g1 send1 send0", "g2 send4 keep1 g3", "send3 keep0 g4 ~keep1", "send2 zm1 ~send4 keep4",
    "~keep0 send5 g6 zm0", "~zm1 keep3 zo1 zm4", "keep2 zo0 ~keep3 keep5", "ag1 zm3 zo4 zm2",
    "~keep5 ag0 ~ag1 zm5", "zo3 ag4 ch0 ~ag0", "zo2 ch1 ~zm5 ag3", "~ag4 zo5 ch2 ag2",
    "ch3 ~ag3 ag5 weights", "fin1 fin0 fin2 fin4", "fin3 fin5",
)


def dot(a, b):
    return jnp.dot(a, b, precision=highest, preferred_element_type=f32)


def dot_t(a, b):
    return lax.dot_general(a, b, (((0,), (0,)), ((), ())), precision=highest, preferred_element_type=f32)


def dot_nt(a, b):
    return lax.dot_general(a, b, (((1,), (1,)), ((), ())), precision=highest, preferred_element_type=f32)


def split(value):
    high = value.astype(bf16)
    return high, (value - high.astype(f32)).astype(bf16)


def dot3(a, b):
    def product(x, y):
        return jnp.dot(x, y, preferred_element_type=f32)

    return product(a[0], b[0]) + (product(a[0], b[1]) + product(a[1], b[0]))


def flip(value, axis, bit):
    n = lax.axis_size(axis)
    return lax.ppermute(value, axis, [(i, i ^ bit) for i in range(n)])


class Chain:
    def __init__(self):
        self.last = []
        self.waits = []

    def __call__(self, kernel, name, outs, flags, *operands, scratch=()):
        after = self.last + self.waits
        n_in, n_after = len(operands), len(after)
        vmem = pl.BlockSpec(memory_space=pltpu.VMEM)

        def body(*refs):
            skip = 1 + n_in
            kernel(*refs[:skip], *refs[skip + n_after:])

        result = pl.pallas_call(
            body,
            out_shape=[jax.ShapeDtypeStruct(*(o if isinstance(o[0], tuple) else (o, f32))) for o in outs],
            in_specs=[pl.BlockSpec(memory_space=pltpu.SMEM)] + [vmem] * n_in
            + [pl.BlockSpec(memory_space=pl.ANY)] * n_after,
            out_specs=[vmem] * len(outs),
            scratch_shapes=list(scratch),
            name=name,
            compiler_params=pltpu.CompilerParams(vmem_limit_bytes=24 * 2**20),
            cost_estimate=pl.CostEstimate(flops=1000, bytes_accessed=1000, transcendentals=0),
        )(flags, *operands, *after)
        self.last = [result[0]]
        self.waits = []
        return result


def spread_kernel(parts, flags, in_ref, out_ref, high_ref, low_ref):
    rows = out_ref.shape[0]
    for part in range(parts):
        cut = slice(part * TILE, (part + 1) * TILE)
        value = in_ref[pl.ds(part, rows, stride=parts), :]
        out_ref[:, cut] = value
        high_ref[:, cut], low_ref[:, cut] = split(value)


def pick_kernel(which, flags, a_ref, b_ref, out_ref):
    @pl.when(flags[which] != 0)
    def _():
        out_ref[...] = a_ref[...]

    @pl.when(flags[which] == 0)
    def _():
        out_ref[...] = b_ref[...]


def panels_kernel(
    flags, held_ref, other_ref, both_ref, keep_high, keep_low, send_high, send_low, share_ref, stack
):
    width = held_ref.shape[1]
    share = share_ref.shape[0]
    held, other = held_ref[...], other_ref[...]
    low = flags[1] != 0
    p0, p1 = jnp.where(low, held, other), jnp.where(low, other, held)
    both_ref[:, :width] = p0
    both_ref[:, width:] = p1
    t0, t1 = p0.T, p1.T
    first = flags[2] != 0
    keep_high[...], keep_low[...] = split(jnp.where(first, t0, t1))
    send_high[...], send_low[...] = split(jnp.where(first, t1, t0))
    stack[:width] = dot(t0, p0)
    stack[width:2 * width] = dot(t1, p0)
    stack[2 * width:] = dot(t1, p1)
    share_ref[...] = stack[pl.ds(pl.multiple_of(flags[4] * share, 8), share), :]


def product_kernel(lo, hi, flags, panel_high, panel_low, a_high, a_low, out_ref):
    panel = panel_high[...], panel_low[...]
    out_ref[...] = dot3(panel, (a_high[:, lo:hi], a_low[:, lo:hi]))


def product_add_kernel(lo, hi, flags, panel_high, panel_low, a_high, a_low, came_ref, out_ref):
    panel = panel_high[...], panel_low[...]
    out_ref[...] = dot3(panel, (a_high[:, lo:hi], a_low[:, lo:hi])) + came_ref[...]


def gather_kernel(which, flags, *refs):
    share = refs[0].shape[0]
    for ref, w in zip(refs, which):
        at = pl.multiple_of((flags[4] ^ w) * share, 8)
        refs[-1][pl.ds(at, share), :] = ref[...]


def add_kernel(flags, a_ref, b_ref, out_ref):
    out_ref[...] = a_ref[...] + b_ref[...]


def eliminate(block, rows_ref, heads_ref):
    size = block.shape[0]
    group = 4
    sub = lax.broadcasted_iota(jnp.int32, (size, size), 0)
    lane = lax.broadcasted_iota(jnp.int32, (size, size), 1)
    left = block
    right = jnp.where(sub == lane, 1.0, 0.0).astype(f32)

    def spread(j):
        return [jnp.broadcast_to(left[:, j + p:j + p + 1], left.shape) for p in range(group)]

    cols = spread(0)
    for j in range(0, size, group):
        at = j % 8
        last = j + group == size
        ahead = [] if last else spread(j + group)
        rows = [left[at + p:at + p + 1] for p in range(group)]
        others = [right[at + p:at + p + 1] for p in range(group)]
        factors = []
        for p in range(group):
            head = cols[p][at + p:at + p + 1]
            factor = cols[p] * (1.0 / head)
            factors.append(factor)
            heads_ref[j + p:j + p + 1, :] = head
            rows_ref[j + p:j + p + 1, :] = others[p]
            for q in range(p + 1, group):
                cols[q] = cols[q] - factor * cols[p][at + q:at + q + 1]
                low = factor[at + q:at + q + 1]
                rows[q] = rows[q] - low * rows[p]
                others[q] = others[q] - low * others[p]
            for q in range(len(ahead)):
                here = at + group + q
                ahead[q] = ahead[q] - factor * cols[p][here:here + 1]
        if last:
            break
        cut = 8 if at + group == 8 else 0
        left, right, cols = left[cut:], right[cut:], [c[cut:] for c in ahead]
        for p in range(group):
            left = left - factors[p][cut:] * rows[p]
            right = right - factors[p][cut:] * others[p]


def factor_kernel(step, flags, *refs):
    if step == 0:
        gram_ref, out_state_ref, out_inv_ref, rows_ref, heads_ref = refs
    else:
        state_ref, inv_ref, out_state_ref, out_inv_ref, rows_ref, heads_ref = refs
    size = out_state_ref.shape[0]
    lo, hi = step * TILE, (step + 1) * TILE
    if step == 0:
        half = size // 2
        out_state_ref[:half, :half] = gram_ref[:half]
        out_state_ref[half:, :half] = gram_ref[half:size]
        out_state_ref[half:, half:] = gram_ref[size:]
        sub = lax.broadcasted_iota(jnp.int32, (size, size), 0)
        lane = lax.broadcasted_iota(jnp.int32, (size, size), 1)
        out_inv_ref[...] = jnp.where(sub == lane, 1.0, 0.0).astype(f32)
    else:
        out_state_ref[...] = state_ref[...]
        out_inv_ref[...] = inv_ref[...]
    eliminate(out_state_ref[lo:hi, lo:hi], rows_ref, heads_ref)
    block_inv = rows_ref[...] * lax.rsqrt(heads_ref[...])
    done = dot(block_inv, out_inv_ref[lo:hi, :hi])
    out_inv_ref[lo:hi, :hi] = done
    if hi < size:
        below = dot_nt(out_state_ref[hi:, lo:hi], block_inv)
        out_state_ref[hi:, hi:] = out_state_ref[hi:, hi:] - dot_nt(below, below)
        out_inv_ref[hi:, :hi] = out_inv_ref[hi:, :hi] - dot(below, done)


def weights_kernel(flags, both_ref, inv_ref, high_ref, low_ref):
    rows = both_ref.shape[0]
    width = both_ref.shape[1] // 2
    per_device = high_ref.shape[0] - rows
    ortho = dot_nt(both_ref[...], inv_ref[...])
    first = flags[2] != 0
    mine = inv_ref[pl.ds(pl.multiple_of(flags[5] * per_device, 8), per_device), :]

    def put(place, left, right):
        high_ref[place, :width], low_ref[place, :width] = split(jnp.where(first, left, right))
        high_ref[place, width:], low_ref[place, width:] = split(jnp.where(first, right, left))

    put(slice(0, rows), dot(ortho, inv_ref[:, :width]), dot(ortho, inv_ref[:, width:]))
    put(slice(rows, rows + per_device), mine[:, :width], mine[:, width:])


def finish_kernel(lo, hi, flags, a_ref, high_ref, low_ref, first_ref, second_ref, rest_ref, factor_ref):
    rows, width = a_ref.shape[0], first_ref.shape[0]
    change = dot3((high_ref[:, :width], low_ref[:, :width]), split(first_ref[...]))
    change += dot3((high_ref[:, width:], low_ref[:, width:]), split(second_ref[...]))
    rest_ref[...] = a_ref[:, lo:hi] - change[:rows]
    factor_ref[...] = change[rows:]


def rows_kernel(parts, n, *refs):
    rests, factors, (rest_ref, factor_ref) = refs[:n], refs[n:2 * n], refs[2 * n:]

    def lay(pieces, out_ref):
        part = 0
        for piece in pieces:
            rows = piece.shape[0]
            for at in range(0, piece.shape[1], TILE):
                out_ref[pl.ds(part, rows, stride=parts), :] = piece[:, at:at + TILE]
                part += 1

    lay(rests, rest_ref)

    @pl.when(pl.program_id(0) == 0)
    def _():
        lay(factors, factor_ref)


def in_rows(rests, factors, parts):
    rows, own_rows = rests[0].shape[0], factors[0].shape[0]
    step = min(rows, 128)
    return pl.pallas_call(
        functools.partial(rows_kernel, parts, len(rests)),
        grid=(rows // step,),
        out_shape=[
            jax.ShapeDtypeStruct((rows * parts, TILE), f32),
            jax.ShapeDtypeStruct((own_rows * parts, TILE), f32),
        ],
        in_specs=[pl.BlockSpec((step, v.shape[1]), lambda i: (i, 0)) for v in rests]
        + [pl.BlockSpec(v.shape, lambda i: (0, 0)) for v in factors],
        out_specs=[
            pl.BlockSpec((step * parts, TILE), lambda i: (i, 0)),
            pl.BlockSpec((own_rows * parts, TILE), lambda i: (0, 0)),
        ],
        name="tiles_to_rows",
        compiler_params=pltpu.CompilerParams(vmem_limit_bytes=24 * 2**20),
    )(*rests, *factors)


def local(matrix):
    rows, blocks, _, width = matrix.shape
    parts = blocks * width // TILE
    depth = 2 * width
    n_row, n_col = lax.axis_size("prow"), lax.axis_size("pcol")
    row, col = lax.axis_index("prow"), lax.axis_index("pcol")
    place = row // 2
    line = n_row == 8
    sizes = SIZES if sum(SIZES) == blocks else (blocks,)
    flags = jnp.stack([
        col >= 2, col % 2 == 0, row % 2 == 0, (place == 1) | (place == 2), col, row,
    ]).astype(jnp.int32)
    chain = Chain()
    flat = matrix.reshape(rows * parts, TILE)

    held = matrix[:, 0, 0, :]
    reach = 2
    came = lax.ppermute(held, "pcol", [(0, 2), (1, 3)]) if n_col > 2 else held
    wide = (rows, parts * TILE)
    a, *a_split = chain(
        functools.partial(spread_kernel, parts), "rows_to_tiles", [wide, (wide, bf16), (wide, bf16)], flags, flat
    )
    held, = chain(functools.partial(pick_kernel, 0), "pick", [held.shape], flags, came, held)
    reach = 4
    while reach < n_col:
        came = lax.ppermute(held, "pcol", [(i, i + reach) for i in range(reach) if i + reach < n_col])
        held = jnp.where((col >= reach) & (col < 2 * reach), came, held)
        reach *= 2
    beside = flip(held, "pcol", 1)

    state = {}
    starts = [sum(sizes[:k]) * width for k in range(len(sizes) + 1)]

    def in_hop(value):
        return lax.ppermute(value, "prow", [(0, 2), (1, 3), (6, 4), (7, 5)]) if line else None

    def mid_hop(value):
        return lax.ppermute(value, "prow", [(2, 4), (3, 5), (4, 2), (5, 3)]) if line else None

    def out_hop(value):
        return lax.ppermute(value, "prow", [(2, 0), (3, 1), (4, 6), (5, 7)]) if line else None

    def add(name, a, b):
        if b is None:
            return a
        return chain(add_kernel, name, [a.shape], flags, a, b)[0]

    def pick_inner(name, a, b):
        if b is None:
            bit = 2
            while bit < n_row:
                a = a + flip(a, "prow", bit)
                bit *= 2
            return a
        return chain(functools.partial(pick_kernel, 3), name, [a.shape], flags, a, b)[0]

    def run(task):
        if task == "gram":
            cut = ((width, rows), bf16)
            both, *panels, share = chain(
                panels_kernel, "panels", [(rows, depth)] + [cut] * 4 + [(3 * width // n_col, width)],
                flags, held, beside, scratch=[pltpu.VMEM((3 * width, width), f32)],
            )
            state.update(both=both, keep=panels[:2], send=panels[2:], g=share, gr=flip(share, "prow", 1))
        elif task == "g1":
            state["g"] = add(task, state["g"], state["gr"])
            state["gr"] = in_hop(state["g"])
        elif task == "g2":
            state["g"] = add(task, state["g"], state["gr"])
            state["gr"] = mid_hop(state["g"])
        elif task == "g3":
            state["g"] = add(task, state["g"], state["gr"])
            state["gr"] = out_hop(state["g"])
        elif task == "g4":
            state["g"] = pick_inner(task, state["g"], state["gr"])
            state["shares"] = [state["g"]]
            state["which"] = [0]
            bit = n_col // 2
            while bit >= 1:
                state["shares"] += [flip(v, "pcol", bit) for v in state["shares"]]
                state["which"] += [w ^ bit for w in state["which"]]
                bit //= 2
        elif task == "g6":
            state["gram"], = chain(
                functools.partial(gather_kernel, state["which"]), task, [(3 * width, width)], flags, *state["shares"]
            )
        elif task.startswith("ch"):
            step = int(task[2:])
            operands = [state["gram"]] if step == 0 else state["factor"]
            state["factor"] = chain(
                functools.partial(factor_kernel, step), f"factor{step}", [(depth, depth)] * 2, flags, *operands,
                scratch=[pltpu.VMEM((TILE, TILE), f32)] * 2,
            )
        elif task == "weights":
            cut = ((rows + depth // n_row, depth), bf16)
            state["weights"] = chain(weights_kernel, task, [cut] * 2, flags, state["both"], state["factor"][1])
        else:
            kind, k = task.rstrip("0123456789"), int(task.lstrip("abcdefghijklmnopqrstuvwxyz"))
            if k >= len(sizes):
                return
            lo, hi = starts[k], starts[k + 1]
            if kind == "send":
                out, = chain(functools.partial(product_kernel, lo, hi), task, [(width, hi - lo)],
                             flags, *state["send"], *a_split)
                state["r", k] = flip(out, "prow", 1)
            elif kind == "keep":
                out, = chain(functools.partial(product_add_kernel, lo, hi), task, [(width, hi - lo)],
                             flags, *state["keep"], *a_split, state["r", k])
                state["s", k], state["r", k] = out, in_hop(out)
            elif kind == "zm":
                out = add(task, state["s", k], state["r", k])
                state["s", k], state["r", k] = out, mid_hop(out)
            elif kind == "zo":
                out = add(task, state["s", k], state["r", k])
                state["s", k], state["r", k] = out, out_hop(out)
            elif kind == "ag":
                out = pick_inner(task, state["s", k], state["r", k])
                state["s", k], state["r", k] = out, flip(out, "prow", 1)
            elif kind == "fin":
                state["out", k] = chain(
                    functools.partial(finish_kernel, lo, hi), task,
                    [(rows, hi - lo), (depth // n_row, hi - lo)],
                    flags, a, *state["weights"], state["s", k], state["r", k],
                )

    for task in " ".join(ORDER).split():
        if task[0] != "~":
            run(task)
        elif line and ("r", int(task[-1])) in state:
            chain.waits.append(state["r", int(task[-1])])
    outs = [state["out", k] for k in range(len(sizes))]
    rest, factor = in_rows([o[0] for o in outs], [o[1] for o in outs], parts)
    return (
        factor.reshape(depth // n_row, blocks, 1, width),
        rest.reshape(rows, blocks, 1, width),
    )


def solution(mesh):
    placed = P("prow", None, "pcol", None)
    return jax.shard_map(
        local, mesh=mesh, in_specs=(placed,), out_specs=(placed, placed), check_vma=False
    )
```

```python
import functools

import jax
import jax.numpy as jnp
from jax import lax
from jax.experimental import pallas as pl
from jax.experimental.pallas import tpu as pltpu
from jax.sharding import PartitionSpec as P

highest = lax.Precision.HIGHEST
f32 = jnp.float32
bf16 = jnp.bfloat16
TILE = 128
SIZES = (2, 1, 2, 2, 2, 2)
SENDS = ((0,), (1,), (2,), (3,), (4,), (5,))
ORDER = (
    "gram send1 send0 send4", "g1 ~g1 send5 keep1", "g2 send2 keep0 send3", "~keep1 zm1 keep2 g4",
    "keep4 ~zm1 zm0 zm2", "keep3 g5 zo0 keep5", "zm4 zo2 g6 ag0", "ch0 zm3 zo1 zo4",
    "ag2 ~zo1 zm5 ~ag2", "ch1 ag4 zo5 ag1", "~ag0 ch2 zo3 ch3", "ag5 weights fin4 ~zo3",
    "fin1 ag3 fin5 fin2", "fin0 fin3",
)


def dot(a, b):
    return jnp.dot(a, b, precision=highest, preferred_element_type=f32)


def dot_t(a, b):
    return lax.dot_general(a, b, (((0,), (0,)), ((), ())), precision=highest, preferred_element_type=f32)


def dot_nt(a, b):
    return lax.dot_general(a, b, (((1,), (1,)), ((), ())), precision=highest, preferred_element_type=f32)


def split(value):
    high = value.astype(bf16)
    return high, (value - high.astype(f32)).astype(bf16)


def dot3(a, b):
    def product(x, y):
        return jnp.dot(x, y, preferred_element_type=f32)

    return product(a[0], b[0]) + (product(a[0], b[1]) + product(a[1], b[0]))


def flip(value, axis, bit):
    n = lax.axis_size(axis)
    return lax.ppermute(value, axis, [(i, i ^ bit) for i in range(n)])


class Chain:
    def __init__(self):
        self.last = []
        self.waits = []

    def __call__(self, kernel, name, outs, flags, *operands, scratch=()):
        after = self.last + self.waits
        n_in, n_after = len(operands), len(after)
        vmem = pl.BlockSpec(memory_space=pltpu.VMEM)

        def body(*refs):
            skip = 1 + n_in
            kernel(*refs[:skip], *refs[skip + n_after:])

        result = pl.pallas_call(
            body,
            out_shape=[jax.ShapeDtypeStruct(*(o if isinstance(o[0], tuple) else (o, f32))) for o in outs],
            in_specs=[pl.BlockSpec(memory_space=pltpu.SMEM)] + [vmem] * n_in
            + [pl.BlockSpec(memory_space=pl.ANY)] * n_after,
            out_specs=[vmem] * len(outs),
            scratch_shapes=list(scratch),
            name=name,
            compiler_params=pltpu.CompilerParams(vmem_limit_bytes=24 * 2**20),
            cost_estimate=pl.CostEstimate(flops=1000, bytes_accessed=1000, transcendentals=0),
        )(flags, *operands, *after)
        self.last = [result[0]]
        self.waits = []
        return result


def spread_kernel(parts, flags, in_ref, *out_refs):
    part = 0
    for out_ref, high_ref, low_ref in zip(out_refs[::3], out_refs[1::3], out_refs[2::3]):
        rows, columns = out_ref.shape
        for at in range(0, columns, TILE):
            cut = slice(at, at + TILE)
            value = in_ref[pl.ds(part, rows, stride=parts), :]
            out_ref[:, cut] = value
            high_ref[:, cut], low_ref[:, cut] = split(value)
            part += 1


def pick_kernel(which, flags, a_ref, b_ref, out_ref):
    @pl.when(flags[which] != 0)
    def _():
        out_ref[...] = a_ref[...]

    @pl.when(flags[which] == 0)
    def _():
        out_ref[...] = b_ref[...]


def panels_kernel(
    flags, held_ref, other_ref, both_ref, keep_high, keep_low, send_high, send_low, share_ref, stack
):
    width = held_ref.shape[1]
    share = share_ref.shape[0]
    held, other = held_ref[...], other_ref[...]
    low = flags[1] != 0
    p0, p1 = jnp.where(low, held, other), jnp.where(low, other, held)
    both_ref[:, :width] = p0
    both_ref[:, width:] = p1
    t0, t1 = p0.T, p1.T
    first = flags[2] != 0
    keep_high[...], keep_low[...] = split(jnp.where(first, t0, t1))
    send_high[...], send_low[...] = split(jnp.where(first, t1, t0))
    stack[:width] = dot(t0, p0)
    stack[width:2 * width] = dot(t1, p0)
    stack[2 * width:] = dot(t1, p1)
    share_ref[...] = stack[pl.ds(pl.multiple_of(flags[4] * share, 8), share), :]


def product_kernel(flags, panel_high, panel_low, *refs):
    panel = panel_high[...], panel_low[...]
    at, out_ref = 0, refs[-1]
    for high, low in zip(refs[:-1:2], refs[1:-1:2]):
        columns = high.shape[1]
        out_ref[:, at:at + columns] = dot3(panel, (high[...], low[...]))
        at += columns


def product_add_kernel(skip, flags, panel_high, panel_low, a_high, a_low, came_ref, out_ref):
    panel = panel_high[...], panel_low[...]
    came = came_ref[:, skip:skip + out_ref.shape[1]]
    out_ref[...] = dot3(panel, (a_high[...], a_low[...])) + came


def stack_kernel(flags, a_ref, b_ref, out_ref):
    rows = a_ref.shape[0]
    out_ref[:rows] = a_ref[...]
    out_ref[rows:] = b_ref[...]


def gather_kernel(which, flags, a_ref, b_ref, out_ref):
    share = out_ref.shape[0] // len(which)
    half = len(which) // 2
    for place, w in enumerate(which):
        at = pl.multiple_of((flags[4] ^ w) * share, 8)
        ref, here = (a_ref, place) if place < half else (b_ref, place - half)
        out_ref[pl.ds(at, share), :] = ref[here * share:(here + 1) * share]


def add_kernel(flags, a_ref, b_ref, out_ref):
    out_ref[...] = a_ref[...] + b_ref[...]


def eliminate(block, rows_ref, heads_ref):
    size = block.shape[0]
    group = 4
    sub = lax.broadcasted_iota(jnp.int32, (size, size), 0)
    lane = lax.broadcasted_iota(jnp.int32, (size, size), 1)
    left = block
    right = jnp.where(sub == lane, 1.0, 0.0).astype(f32)

    def spread(j):
        return [jnp.broadcast_to(left[:, j + p:j + p + 1], left.shape) for p in range(group)]

    cols = spread(0)
    for j in range(0, size, group):
        at = j % 8
        last = j + group == size
        ahead = [] if last else spread(j + group)
        rows = [left[at + p:at + p + 1] for p in range(group)]
        others = [right[at + p:at + p + 1] for p in range(group)]
        factors = []
        for p in range(group):
            head = cols[p][at + p:at + p + 1]
            factor = cols[p] * (1.0 / head)
            factors.append(factor)
            heads_ref[j + p:j + p + 1, :] = head
            rows_ref[j + p:j + p + 1, :] = others[p]
            for q in range(p + 1, group):
                cols[q] = cols[q] - factor * cols[p][at + q:at + q + 1]
                low = factor[at + q:at + q + 1]
                rows[q] = rows[q] - low * rows[p]
                others[q] = others[q] - low * others[p]
            for q in range(len(ahead)):
                here = at + group + q
                ahead[q] = ahead[q] - factor * cols[p][here:here + 1]
        if last:
            break
        cut = 8 if at + group == 8 else 0
        left, right, cols = left[cut:], right[cut:], [c[cut:] for c in ahead]
        for p in range(group):
            left = left - factors[p][cut:] * rows[p]
            right = right - factors[p][cut:] * others[p]


def factor_kernel(step, flags, *refs):
    if step == 0:
        gram_ref, out_state_ref, out_inv_ref, rows_ref, heads_ref = refs
    else:
        state_ref, inv_ref, out_state_ref, out_inv_ref, rows_ref, heads_ref = refs
    size = out_state_ref.shape[0]
    lo, hi = step * TILE, (step + 1) * TILE
    if step == 0:
        half = size // 2
        out_state_ref[:half, :half] = gram_ref[:half]
        out_state_ref[half:, :half] = gram_ref[half:size]
        out_state_ref[half:, half:] = gram_ref[size:]
        sub = lax.broadcasted_iota(jnp.int32, (size, size), 0)
        lane = lax.broadcasted_iota(jnp.int32, (size, size), 1)
        out_inv_ref[...] = jnp.where(sub == lane, 1.0, 0.0).astype(f32)
    else:
        out_state_ref[...] = state_ref[...]
        out_inv_ref[...] = inv_ref[...]
    eliminate(out_state_ref[lo:hi, lo:hi], rows_ref, heads_ref)
    block_inv = rows_ref[...] * lax.rsqrt(heads_ref[...])
    done = dot(block_inv, out_inv_ref[lo:hi, :hi])
    out_inv_ref[lo:hi, :hi] = done
    if hi < size:
        below = dot_nt(out_state_ref[hi:, lo:hi], block_inv)
        out_state_ref[hi:, hi:] = out_state_ref[hi:, hi:] - dot_nt(below, below)
        out_inv_ref[hi:, :hi] = out_inv_ref[hi:, :hi] - dot(below, done)


def weights_kernel(flags, both_ref, inv_ref, high_ref, low_ref):
    rows = both_ref.shape[0]
    width = both_ref.shape[1] // 2
    per_device = high_ref.shape[0] - rows
    inverse = inv_ref[...]
    high, low = split(inverse)
    ortho = split(dot3(split(both_ref[...]), split(inverse.T)))
    first = flags[2] != 0
    mine = inv_ref[pl.ds(pl.multiple_of(flags[5] * per_device, 8), per_device), :]

    def put(place, left, right):
        high_ref[place, :width], low_ref[place, :width] = split(jnp.where(first, left, right))
        high_ref[place, width:], low_ref[place, width:] = split(jnp.where(first, right, left))

    both = dot3(ortho, (high, low))
    put(slice(0, rows), both[:, :width], both[:, width:])
    put(slice(rows, rows + per_device), mine[:, :width], mine[:, width:])


def finish_kernel(flags, a_ref, high_ref, low_ref, first_ref, second_ref, rest_ref, factor_ref):
    rows, width = a_ref.shape[0], first_ref.shape[0]
    change = dot3((high_ref[:, :width], low_ref[:, :width]), split(first_ref[...]))
    change += dot3((high_ref[:, width:], low_ref[:, width:]), split(second_ref[...]))
    rest_ref[...] = a_ref[...] - change[:rows]
    factor_ref[...] = change[rows:]


def rows_kernel(parts, n, *refs):
    rests, factors, (rest_ref, factor_ref) = refs[:n], refs[n:2 * n], refs[2 * n:]

    def lay(pieces, out_ref):
        part = 0
        for piece in pieces:
            rows = piece.shape[0]
            for at in range(0, piece.shape[1], TILE):
                out_ref[pl.ds(part, rows, stride=parts), :] = piece[:, at:at + TILE]
                part += 1

    lay(rests, rest_ref)

    @pl.when(pl.program_id(0) == 0)
    def _():
        lay(factors, factor_ref)


def in_rows(rests, factors, parts):
    rows, own_rows = rests[0].shape[0], factors[0].shape[0]
    step = min(rows, 64)
    return pl.pallas_call(
        functools.partial(rows_kernel, parts, len(rests)),
        grid=(rows // step,),
        out_shape=[
            jax.ShapeDtypeStruct((rows * parts, TILE), f32),
            jax.ShapeDtypeStruct((own_rows * parts, TILE), f32),
        ],
        in_specs=[pl.BlockSpec((step, v.shape[1]), lambda i: (i, 0)) for v in rests]
        + [pl.BlockSpec(v.shape, lambda i: (0, 0)) for v in factors],
        out_specs=[
            pl.BlockSpec((step * parts, TILE), lambda i: (i, 0)),
            pl.BlockSpec((own_rows * parts, TILE), lambda i: (0, 0)),
        ],
        name="tiles_to_rows",
        compiler_params=pltpu.CompilerParams(vmem_limit_bytes=24 * 2**20),
    )(*rests, *factors)


def local(matrix):
    rows, blocks, _, width = matrix.shape
    parts = blocks * width // TILE
    depth = 2 * width
    n_row, n_col = lax.axis_size("prow"), lax.axis_size("pcol")
    row, col = lax.axis_index("prow"), lax.axis_index("pcol")
    place = row // 2
    line = n_row == 8
    sizes, sends = (SIZES, SENDS) if sum(SIZES) == blocks else ((blocks,), ((0,),))
    flags = jnp.stack([
        col >= 2, col % 2 == 0, row % 2 == 0, (place == 1) | (place == 2), col, row,
    ]).astype(jnp.int32)
    chain = Chain()
    flat = matrix.reshape(rows * parts, TILE)

    held = matrix[:, 0, 0, :]
    reach = 2
    came = lax.ppermute(held, "pcol", [(0, 2), (1, 3)]) if n_col > 2 else held
    shapes = []
    for count in sizes:
        shape = (rows, count * width)
        shapes += [shape, (shape, bf16), (shape, bf16)]
    cuts = chain(functools.partial(spread_kernel, parts), "rows_to_tiles", shapes, flags, flat)
    cuts = [cuts[3 * k:3 * k + 3] for k in range(len(sizes))]
    held, = chain(functools.partial(pick_kernel, 0), "pick", [held.shape], flags, came, held)
    reach = 4
    while reach < n_col:
        came = lax.ppermute(held, "pcol", [(i, i + reach) for i in range(reach) if i + reach < n_col])
        held = jnp.where((col >= reach) & (col < 2 * reach), came, held)
        reach *= 2
    beside = flip(held, "pcol", 1)

    state = {}
    starts = [sum(sizes[:k]) * width for k in range(len(sizes) + 1)]

    def in_hop(value):
        return lax.ppermute(value, "prow", [(0, 2), (1, 3), (6, 4), (7, 5)]) if line else None

    def mid_hop(value):
        return lax.ppermute(value, "prow", [(2, 4), (3, 5), (4, 2), (5, 3)]) if line else None

    def out_hop(value):
        return lax.ppermute(value, "prow", [(2, 0), (3, 1), (4, 6), (5, 7)]) if line else None

    def add(name, a, b):
        if b is None:
            return a
        return chain(add_kernel, name, [a.shape], flags, a, b)[0]

    def pick_inner(name, a, b):
        if b is None:
            bit = 2
            while bit < n_row:
                a = a + flip(a, "prow", bit)
                bit *= 2
            return a
        return chain(functools.partial(pick_kernel, 3), name, [a.shape], flags, a, b)[0]

    def run(task):
        if task == "gram":
            cut = ((width, rows), bf16)
            both, *panels, share = chain(
                panels_kernel, "panels", [(rows, depth)] + [cut] * 4 + [(3 * width // n_col, width)],
                flags, held, beside, scratch=[pltpu.VMEM((3 * width, width), f32)],
            )
            state.update(both=both, keep=panels[:2], send=panels[2:], g=share, gr=flip(share, "prow", 1))
        elif task == "g1" or task == "g2":
            state["g"] = add(task, state["g"], state["gr"])
            state["gr"] = flip(state["g"], "prow", 2 * int(task[1]))
        elif task == "g4":
            state["g"] = add(task, state["g"], state["gr"])
            bit = 8
            while bit < n_row:
                state["g"] = state["g"] + flip(state["g"], "prow", bit)
                bit *= 2
            bit = n_col // 2
            state["gr"] = flip(state["g"], "pcol", bit)
        elif task == "g5":
            bit = n_col // 2
            which = [0, bit]
            joint, = chain(stack_kernel, task, [(2 * state["g"].shape[0], width)], flags, state["g"], state["gr"])
            bit //= 2
            while bit > 1:
                which += [w ^ bit for w in which]
                joint = jnp.concatenate([joint, flip(joint, "pcol", bit)], 0)
                bit //= 2
            state.update(held=joint, which=which + [w ^ 1 for w in which], gr=flip(joint, "pcol", 1))
        elif task == "g6":
            state["gram"], = chain(
                functools.partial(gather_kernel, state["which"]), task, [(3 * width, width)], flags, state["held"], state["gr"]
            )
        elif task.startswith("ch"):
            step = int(task[2:])
            operands = [state["gram"]] if step == 0 else state["factor"]
            state["factor"] = chain(
                functools.partial(factor_kernel, step), f"factor{step}", [(depth, depth)] * 2, flags, *operands,
                scratch=[pltpu.VMEM((TILE, TILE), f32)] * 2,
            )
        elif task == "weights":
            cut = ((rows + depth // n_row, depth), bf16)
            state["weights"] = chain(weights_kernel, task, [cut] * 2, flags, state["both"], state["factor"][1])
        else:
            kind, k = task.rstrip("0123456789"), int(task.lstrip("abcdefghijklmnopqrstuvwxyz"))
            if k >= (len(sends) if kind == "send" else len(sizes)):
                return
            if kind != "send":
                lo, hi = starts[k], starts[k + 1]
            if kind == "send":
                members = sends[k]
                lo, hi = starts[members[0]], starts[members[-1] + 1]
                pieces = [v for member in members for v in cuts[member][1:]]
                out, = chain(product_kernel, task, [(width, hi - lo)], flags, *state["send"], *pieces)
                came = flip(out, "prow", 1)
                for member in members:
                    state["r", member] = came
            elif kind == "keep":
                skip = lo - starts[next(m for m in sends if k in m)[0]]
                out, = chain(functools.partial(product_add_kernel, skip), task, [(width, hi - lo)],
                             flags, *state["keep"], *cuts[k][1:], state["r", k])
                state["s", k], state["r", k] = out, in_hop(out)
            elif kind == "zm":
                out = add(task, state["s", k], state["r", k])
                state["s", k], state["r", k] = out, mid_hop(out)
            elif kind == "zo":
                out = add(task, state["s", k], state["r", k])
                state["s", k], state["r", k] = out, out_hop(out)
            elif kind == "ag":
                out = pick_inner(task, state["s", k], state["r", k])
                state["s", k], state["r", k] = out, flip(out, "prow", 1)
            elif kind == "fin":
                state["out", k] = chain(
                    finish_kernel, task, [(rows, hi - lo), (depth // n_row, hi - lo)],
                    flags, cuts[k][0], *state["weights"], state["s", k], state["r", k],
                )

    for task in " ".join(ORDER).split():
        if task[0] != "~":
            run(task)
        elif task[1] == "g":
            chain.waits.append(state["gr"])
        elif line and ("r", int(task[-1])) in state:
            chain.waits.append(state["r", int(task[-1])])
    outs = [state["out", k] for k in range(len(sizes))]
    rest, factor = in_rows([o[0] for o in outs], [o[1] for o in outs], parts)
    return (
        factor.reshape(depth // n_row, blocks, 1, width),
        rest.reshape(rows, blocks, 1, width),
    )


def solution(mesh):
    placed = P("prow", None, "pcol", None)
    return jax.shard_map(
        local, mesh=mesh, in_specs=(placed,), out_specs=(placed, placed), check_vma=False
    )
```

```python
import functools

import jax
import jax.numpy as jnp
from jax import lax
from jax.experimental import pallas as pl
from jax.experimental.pallas import tpu as pltpu
from jax.sharding import PartitionSpec as P

highest = lax.Precision.HIGHEST
f32 = jnp.float32
bf16 = jnp.bfloat16
TILE = 128
SIZES = (1, 2, 2, 2, 2, 2)
ORDER = (
    "panels send0 send1 keep0", "send2 keep1 zm0 send3", "keep2 zm1 zo0 send4", "keep3 zm2 ~zo0 zo1",
    "send5 keep4 zm3 ~zo1", "zo2 ag0 keep5 zm4", "~zo2 zo3 ag1 zm5", "~ag0 g4 ~zo3 zo4",
    "g6 ag2 ch0 ~zo4", "zo5 ~ag1 ag3 ch1", "~ag2 ag4 ch2 ~zo5", "ag5 ch3 ~ag3 weights",
    "fin0 fin1 fin2 fin3", "fin4 fin5",
)


def dot(a, b):
    return jnp.dot(a, b, precision=highest, preferred_element_type=f32)


def dot_t(a, b):
    return lax.dot_general(a, b, (((0,), (0,)), ((), ())), precision=highest, preferred_element_type=f32)


def dot_nt(a, b):
    return lax.dot_general(a, b, (((1,), (1,)), ((), ())), precision=highest, preferred_element_type=f32)


def split(value):
    high = value.astype(bf16)
    return high, (value - high.astype(f32)).astype(bf16)


def dot3(a, b):
    def product(x, y):
        return jnp.dot(x, y, preferred_element_type=f32)

    return product(a[0], b[0]) + (product(a[0], b[1]) + product(a[1], b[0]))


def flip(value, axis, bit):
    n = lax.axis_size(axis)
    return lax.ppermute(value, axis, [(i, i ^ bit) for i in range(n)])


class Chain:
    def __init__(self):
        self.last = []
        self.waits = []

    def __call__(self, kernel, name, outs, flags, *operands, scratch=()):
        after = self.last + self.waits
        n_in, n_after = len(operands), len(after)
        vmem = pl.BlockSpec(memory_space=pltpu.VMEM)

        def body(*refs):
            skip = 1 + n_in
            kernel(*refs[:skip], *refs[skip + n_after:])

        result = pl.pallas_call(
            body,
            out_shape=[jax.ShapeDtypeStruct(*(o if isinstance(o[0], tuple) else (o, f32))) for o in outs],
            in_specs=[pl.BlockSpec(memory_space=pltpu.SMEM)] + [vmem] * n_in
            + [pl.BlockSpec(memory_space=pl.ANY)] * n_after,
            out_specs=[vmem] * len(outs),
            scratch_shapes=list(scratch),
            name=name,
            compiler_params=pltpu.CompilerParams(vmem_limit_bytes=24 * 2**20),
            cost_estimate=pl.CostEstimate(flops=1000, bytes_accessed=1000, transcendentals=0),
        )(flags, *operands, *after)
        self.last = [result[0]]
        self.waits = []
        return result


def spread_kernel(parts, flags, in_ref, *out_refs):
    part = 0
    for out_ref, high_ref, low_ref in zip(out_refs[::3], out_refs[1::3], out_refs[2::3]):
        rows, columns = out_ref.shape
        for at in range(0, columns, TILE):
            cut = slice(at, at + TILE)
            value = in_ref[pl.ds(part, rows, stride=parts), :]
            out_ref[:, cut] = value
            high_ref[:, cut], low_ref[:, cut] = split(value)
            part += 1


def pick_kernel(which, flags, a_ref, b_ref, out_ref):
    @pl.when(flags[which] != 0)
    def _():
        out_ref[...] = a_ref[...]

    @pl.when(flags[which] == 0)
    def _():
        out_ref[...] = b_ref[...]


def panels_kernel(
    flags, held_ref, other_ref, both_ref, keep_ref, send_ref, keep_high, keep_low, send_high, send_low
):
    width = held_ref.shape[1]
    held, other = held_ref[...], other_ref[...]
    low = flags[1] != 0
    p0, p1 = jnp.where(low, held, other), jnp.where(low, other, held)
    both_ref[:, :width] = p0
    both_ref[:, width:] = p1
    t0, t1 = p0.T, p1.T
    first = flags[2] != 0
    keep, send = jnp.where(first, t0, t1), jnp.where(first, t1, t0)
    keep_ref[...], send_ref[...] = keep, send
    keep_high[...], keep_low[...] = split(keep)
    send_high[...], send_low[...] = split(send)


def product_kernel(flags, panel_high, panel_low, a_high, a_low, *refs):
    columns, out_ref = a_high.shape[1], refs[-1]
    out_ref[:, :columns] = dot3((panel_high[...], panel_low[...]), (a_high[...], a_low[...]))
    if len(refs) > 1:
        out_ref[:, columns:] = dot(refs[0][...], refs[1][...])


def product_add_kernel(flags, panel_high, panel_low, a_high, a_low, came_ref, *refs):
    columns, out_ref = a_high.shape[1], refs[-1]
    product = dot3((panel_high[...], panel_low[...]), (a_high[...], a_low[...]))
    out_ref[:, :columns] = product + came_ref[:, :columns]
    if len(refs) > 1:
        out_ref[:, columns:] = dot(refs[0][...], refs[1][...]) + came_ref[:, columns:]


def share_kernel(flags, keep_ref, other_ref, out_ref):
    width = keep_ref.shape[0]
    first = flags[2] != 0
    keep, other = keep_ref[:, -width:], other_ref[:, -width:]
    out_ref[:width] = jnp.where(first, keep, other)
    out_ref[width:] = jnp.where(first, other, keep)


def gather_kernel(flags, own_ref, other_ref, out_ref):
    width = own_ref.shape[1]
    low = flags[1] != 0
    own, other = own_ref[...], other_ref[...]
    out_ref[:, :width] = jnp.where(low, own, other)
    out_ref[:, width:] = jnp.where(low, other, own)


def add_kernel(flags, a_ref, b_ref, out_ref):
    out_ref[...] = a_ref[...] + b_ref[...]


def eliminate(block, rows_ref, heads_ref):
    size = block.shape[0]
    group = 4
    sub = lax.broadcasted_iota(jnp.int32, (size, size), 0)
    lane = lax.broadcasted_iota(jnp.int32, (size, size), 1)
    left = block
    right = jnp.where(sub == lane, 1.0, 0.0).astype(f32)

    def spread(j):
        return [jnp.broadcast_to(left[:, j + p:j + p + 1], left.shape) for p in range(group)]

    cols = spread(0)
    for j in range(0, size, group):
        at = j % 8
        last = j + group == size
        ahead = [] if last else spread(j + group)
        rows = [left[at + p:at + p + 1] for p in range(group)]
        others = [right[at + p:at + p + 1] for p in range(group)]
        factors = []
        for p in range(group):
            head = cols[p][at + p:at + p + 1]
            factor = cols[p] * (1.0 / head)
            factors.append(factor)
            heads_ref[j + p:j + p + 1, :] = head
            rows_ref[j + p:j + p + 1, :] = others[p]
            for q in range(p + 1, group):
                cols[q] = cols[q] - factor * cols[p][at + q:at + q + 1]
                low = factor[at + q:at + q + 1]
                rows[q] = rows[q] - low * rows[p]
                others[q] = others[q] - low * others[p]
            for q in range(len(ahead)):
                here = at + group + q
                ahead[q] = ahead[q] - factor * cols[p][here:here + 1]
        if last:
            break
        cut = 8 if at + group == 8 else 0
        left, right, cols = left[cut:], right[cut:], [c[cut:] for c in ahead]
        for p in range(group):
            left = left - factors[p][cut:] * rows[p]
            right = right - factors[p][cut:] * others[p]


def factor_kernel(step, flags, *refs):
    if step == 0:
        gram_ref, out_state_ref, out_inv_ref, rows_ref, heads_ref = refs
    else:
        state_ref, inv_ref, out_state_ref, out_inv_ref, rows_ref, heads_ref = refs
    size = out_state_ref.shape[0]
    lo, hi = step * TILE, (step + 1) * TILE
    if step == 0:
        out_state_ref[...] = gram_ref[...]
        sub = lax.broadcasted_iota(jnp.int32, (size, size), 0)
        lane = lax.broadcasted_iota(jnp.int32, (size, size), 1)
        out_inv_ref[...] = jnp.where(sub == lane, 1.0, 0.0).astype(f32)
    else:
        out_state_ref[...] = state_ref[...]
        out_inv_ref[...] = inv_ref[...]
    eliminate(out_state_ref[lo:hi, lo:hi], rows_ref, heads_ref)
    block_inv = rows_ref[...] * lax.rsqrt(heads_ref[...])
    done = dot(block_inv, out_inv_ref[lo:hi, :hi])
    out_inv_ref[lo:hi, :hi] = done
    if hi < size:
        below = dot_nt(out_state_ref[hi:, lo:hi], block_inv)
        out_state_ref[hi:, hi:] = out_state_ref[hi:, hi:] - dot_nt(below, below)
        out_inv_ref[hi:, :hi] = out_inv_ref[hi:, :hi] - dot(below, done)


def weights_kernel(flags, both_ref, inv_ref, high_ref, low_ref):
    rows = both_ref.shape[0]
    width = both_ref.shape[1] // 2
    per_device = high_ref.shape[0] - rows
    inverse = inv_ref[...]
    high, low = split(inverse)
    ortho = split(dot3(split(both_ref[...]), split(inverse.T)))
    first = flags[2] != 0
    mine = inv_ref[pl.ds(pl.multiple_of(flags[5] * per_device, 8), per_device), :]

    def put(place, left, right):
        high_ref[place, :width], low_ref[place, :width] = split(jnp.where(first, left, right))
        high_ref[place, width:], low_ref[place, width:] = split(jnp.where(first, right, left))

    both = dot3(ortho, (high, low))
    put(slice(0, rows), both[:, :width], both[:, width:])
    put(slice(rows, rows + per_device), mine[:, :width], mine[:, width:])


def finish_kernel(flags, a_ref, high_ref, low_ref, first_ref, second_ref, rest_ref, factor_ref):
    rows, columns = a_ref.shape
    width = first_ref.shape[0]
    change = dot3((high_ref[:, :width], low_ref[:, :width]), split(first_ref[:, :columns]))
    change += dot3((high_ref[:, width:], low_ref[:, width:]), split(second_ref[:, :columns]))
    rest_ref[...] = a_ref[...] - change[:rows]
    factor_ref[...] = change[rows:]


def rows_kernel(parts, n, *refs):
    rests, factors, (rest_ref, factor_ref) = refs[:n], refs[n:2 * n], refs[2 * n:]

    def lay(pieces, out_ref):
        part = 0
        for piece in pieces:
            rows = piece.shape[0]
            for at in range(0, piece.shape[1], TILE):
                out_ref[pl.ds(part, rows, stride=parts), :] = piece[:, at:at + TILE]
                part += 1

    lay(rests, rest_ref)

    @pl.when(pl.program_id(0) == 0)
    def _():
        lay(factors, factor_ref)


def in_rows(rests, factors, parts):
    rows, own_rows = rests[0].shape[0], factors[0].shape[0]
    step = min(rows, 128)
    return pl.pallas_call(
        functools.partial(rows_kernel, parts, len(rests)),
        grid=(rows // step,),
        out_shape=[
            jax.ShapeDtypeStruct((rows * parts, TILE), f32),
            jax.ShapeDtypeStruct((own_rows * parts, TILE), f32),
        ],
        in_specs=[pl.BlockSpec((step, v.shape[1]), lambda i: (i, 0)) for v in rests]
        + [pl.BlockSpec(v.shape, lambda i: (0, 0)) for v in factors],
        out_specs=[
            pl.BlockSpec((step * parts, TILE), lambda i: (i, 0)),
            pl.BlockSpec((own_rows * parts, TILE), lambda i: (0, 0)),
        ],
        name="tiles_to_rows",
        compiler_params=pltpu.CompilerParams(vmem_limit_bytes=24 * 2**20),
    )(*rests, *factors)


def local(matrix):
    rows, blocks, _, width = matrix.shape
    parts = blocks * width // TILE
    depth = 2 * width
    n_row, n_col = lax.axis_size("prow"), lax.axis_size("pcol")
    row, col = lax.axis_index("prow"), lax.axis_index("pcol")
    place = row // 2
    line = n_row == 8
    sizes = SIZES if sum(SIZES) == blocks else (blocks,)
    flags = jnp.stack([
        col >= 2, col % 2 == 0, row % 2 == 0, (place == 1) | (place == 2), col, row,
    ]).astype(jnp.int32)
    chain = Chain()
    flat = matrix.reshape(rows * parts, TILE)

    held = matrix[:, 0, 0, :]
    reach = 2
    came = lax.ppermute(held, "pcol", [(0, 2), (1, 3)]) if n_col > 2 else held
    shapes = []
    for count in sizes:
        shape = (rows, count * width)
        shapes += [shape, (shape, bf16), (shape, bf16)]
    cuts = chain(functools.partial(spread_kernel, parts), "rows_to_tiles", shapes, flags, flat)
    cuts = [cuts[3 * k:3 * k + 3] for k in range(len(sizes))]
    held, = chain(functools.partial(pick_kernel, 0), "pick", [held.shape], flags, came, held)
    reach = 4
    while reach < n_col:
        came = lax.ppermute(held, "pcol", [(i, i + reach) for i in range(reach) if i + reach < n_col])
        held = jnp.where((col >= reach) & (col < 2 * reach), came, held)
        reach *= 2
    beside = flip(held, "pcol", 1)

    state = {}

    def in_hop(value):
        return lax.ppermute(value, "prow", [(0, 2), (1, 3), (6, 4), (7, 5)]) if line else None

    def mid_hop(value):
        return lax.ppermute(value, "prow", [(2, 4), (3, 5), (4, 2), (5, 3)]) if line else None

    def out_hop(value):
        return lax.ppermute(value, "prow", [(2, 0), (3, 1), (4, 6), (5, 7)]) if line else None

    def add(name, a, b):
        if b is None:
            return a
        return chain(add_kernel, name, [a.shape], flags, a, b)[0]

    def pick_inner(name, a, b):
        if b is None:
            bit = 2
            while bit < n_row:
                a = a + flip(a, "prow", bit)
                bit *= 2
            return a
        return chain(functools.partial(pick_kernel, 3), name, [a.shape], flags, a, b)[0]

    def run(task):
        if task == "panels":
            cut = (width, rows)
            both, keep, send, *parted = chain(
                panels_kernel, task, [(rows, depth), cut, cut] + [(cut, bf16)] * 4, flags, held, beside
            )
            state.update(both=both, keep=parted[:2], send=parted[2:], keep_more=[keep, held], send_more=[send, held])
        elif task == "g4":
            share, = chain(share_kernel, task, [(depth, width)], flags, state["s", 0], state["r", 0])
            state["gr"] = share, flip(share, "pcol", 1)
        elif task == "g6":
            state["gram"], = chain(gather_kernel, task, [(depth, depth)], flags, *state["gr"])
        elif task.startswith("ch"):
            step = int(task[2:])
            operands = [state["gram"]] if step == 0 else state["factor"]
            state["factor"] = chain(
                functools.partial(factor_kernel, step), f"factor{step}", [(depth, depth)] * 2, flags, *operands,
                scratch=[pltpu.VMEM((TILE, TILE), f32)] * 2,
            )
        elif task == "weights":
            cut = ((rows + depth // n_row, depth), bf16)
            state["weights"] = chain(weights_kernel, task, [cut] * 2, flags, state["both"], state["factor"][1])
        else:
            kind, k = task.rstrip("0123456789"), int(task.lstrip("abcdefghijklmnopqrstuvwxyz"))
            if k >= len(sizes):
                return
            count = (sizes[k] + (k == 0)) * width
            if kind == "send":
                more = state["send_more"] if k == 0 else []
                out, = chain(product_kernel, task, [(width, count)], flags, *state["send"], *cuts[k][1:], *more)
                state["r", k] = flip(out, "prow", 1)
            elif kind == "keep":
                more = state["keep_more"] if k == 0 else []
                out, = chain(product_add_kernel, task, [(width, count)],
                             flags, *state["keep"], *cuts[k][1:], state["r", k], *more)
                state["s", k], state["r", k] = out, in_hop(out)
            elif kind == "zm":
                out = add(task, state["s", k], state["r", k])
                state["s", k], state["r", k] = out, mid_hop(out)
            elif kind == "zo":
                out = add(task, state["s", k], state["r", k])
                state["s", k], state["r", k] = out, out_hop(out)
            elif kind == "ag":
                out = pick_inner(task, state["s", k], state["r", k])
                state["s", k], state["r", k] = out, flip(out, "prow", 1)
            elif kind == "fin":
                state["out", k] = chain(
                    finish_kernel, task, [(rows, sizes[k] * width), (depth // n_row, sizes[k] * width)],
                    flags, cuts[k][0], *state["weights"], state["s", k], state["r", k],
                )

    for task in " ".join(ORDER).split():
        if task[0] != "~":
            run(task)
        elif line and ("r", int(task[-1])) in state:
            chain.waits.append(state["r", int(task[-1])])
    outs = [state["out", k] for k in range(len(sizes))]
    rest, factor = in_rows([o[0] for o in outs], [o[1] for o in outs], parts)
    return (
        factor.reshape(depth // n_row, blocks, 1, width),
        rest.reshape(rows, blocks, 1, width),
    )


def solution(mesh):
    placed = P("prow", None, "pcol", None)
    return jax.shard_map(
        local, mesh=mesh, in_specs=(placed,), out_specs=(placed, placed), check_vma=False
    )
```

```python
import functools

import jax
import jax.numpy as jnp
from jax import lax
from jax.experimental import pallas as pl
from jax.experimental.pallas import tpu as pltpu
from jax.sharding import PartitionSpec as P

highest = lax.Precision.HIGHEST
f32 = jnp.float32
bf16 = jnp.bfloat16
TILE = 128
SIZES = (1, 2, 2, 2, 2, 2)
ORDER = (
    "panels send0 send1 send2", "send3 keep0 send4 send5", "keep1 zm0 keep2 zm1", "zo0 keep3 zm2 zo1",
    "~zo0 keep4 zm3 zo2", "~zo1 ag0 keep5 zm4", "zo3 ~zo2 ag1 g4", "zm5 zo4 ~zo3 ag2",
    "g6 ch0 ~ag1 zo5", "~zo4 ag3 ch1 ~ag2", "ag4 ~zo5 ag5 ch2", "ch3 ~ag3 weights fin0",
    "fin1 fin2 fin3 fin4", "fin5",
)


def dot(a, b):
    return jnp.dot(a, b, precision=highest, preferred_element_type=f32)


def dot_t(a, b):
    return lax.dot_general(a, b, (((0,), (0,)), ((), ())), precision=highest, preferred_element_type=f32)


def dot_nt(a, b):
    return lax.dot_general(a, b, (((1,), (1,)), ((), ())), precision=highest, preferred_element_type=f32)


def split(value):
    high = value.astype(bf16)
    return high, (value - high.astype(f32)).astype(bf16)


def dot3(a, b):
    def product(x, y):
        return jnp.dot(x, y, preferred_element_type=f32)

    return product(a[0], b[0]) + (product(a[0], b[1]) + product(a[1], b[0]))


def flip(value, axis, bit):
    n = lax.axis_size(axis)
    return lax.ppermute(value, axis, [(i, i ^ bit) for i in range(n)])


class Chain:
    def __init__(self):
        self.last = []
        self.waits = []

    def __call__(self, kernel, name, outs, flags, *operands, scratch=()):
        after = self.last + self.waits
        n_in, n_after = len(operands), len(after)
        vmem = pl.BlockSpec(memory_space=pltpu.VMEM)

        def body(*refs):
            skip = 1 + n_in
            kernel(*refs[:skip], *refs[skip + n_after:])

        result = pl.pallas_call(
            body,
            out_shape=[jax.ShapeDtypeStruct(*(o if isinstance(o[0], tuple) else (o, f32))) for o in outs],
            in_specs=[pl.BlockSpec(memory_space=pltpu.SMEM)] + [vmem] * n_in
            + [pl.BlockSpec(memory_space=pl.ANY)] * n_after,
            out_specs=[vmem] * len(outs),
            scratch_shapes=list(scratch),
            name=name,
            compiler_params=pltpu.CompilerParams(vmem_limit_bytes=24 * 2**20),
            cost_estimate=pl.CostEstimate(flops=1000, bytes_accessed=1000, transcendentals=0),
        )(flags, *operands, *after)
        self.last = [result[0]]
        self.waits = []
        return result


def spread_kernel(parts, flags, in_ref, *out_refs):
    part = 0
    for out_ref, high_ref, low_ref in zip(out_refs[::3], out_refs[1::3], out_refs[2::3]):
        rows, columns = out_ref.shape
        for at in range(0, columns, TILE):
            cut = slice(at, at + TILE)
            value = in_ref[pl.ds(part, rows, stride=parts), :]
            out_ref[:, cut] = value
            high_ref[:, cut], low_ref[:, cut] = split(value)
            part += 1


def pick_kernel(which, flags, a_ref, b_ref, out_ref):
    @pl.when(flags[which] != 0)
    def _():
        out_ref[...] = a_ref[...]

    @pl.when(flags[which] == 0)
    def _():
        out_ref[...] = b_ref[...]


def panels_kernel(
    flags, held_ref, other_ref, both_ref, keep_ref, send_ref, keep_high, keep_low, send_high, send_low
):
    width = held_ref.shape[1]
    held, other = held_ref[...], other_ref[...]
    low = flags[1] != 0
    p0, p1 = jnp.where(low, held, other), jnp.where(low, other, held)
    both_ref[:, :width] = p0
    both_ref[:, width:] = p1
    t0, t1 = p0.T, p1.T
    first = flags[2] != 0
    keep, send = jnp.where(first, t0, t1), jnp.where(first, t1, t0)
    keep_ref[...], send_ref[...] = keep, send
    keep_high[...], keep_low[...] = split(keep)
    send_high[...], send_low[...] = split(send)


def product_kernel(flags, panel_high, panel_low, a_high, a_low, *refs):
    columns, out_ref = a_high.shape[1], refs[-1]
    out_ref[:, :columns] = dot3((panel_high[...], panel_low[...]), (a_high[...], a_low[...]))
    if len(refs) > 1:
        out_ref[:, columns:] = dot(refs[0][...], refs[1][...])


def product_add_kernel(flags, panel_high, panel_low, a_high, a_low, came_ref, *refs):
    columns, out_ref = a_high.shape[1], refs[-1]
    product = dot3((panel_high[...], panel_low[...]), (a_high[...], a_low[...]))
    out_ref[:, :columns] = product + came_ref[:, :columns]
    if len(refs) > 1:
        out_ref[:, columns:] = dot(refs[0][...], refs[1][...]) + came_ref[:, columns:]


def share_kernel(flags, keep_ref, other_ref, out_ref):
    width = keep_ref.shape[0]
    first = flags[2] != 0
    keep, other = keep_ref[:, -width:], other_ref[:, -width:]
    out_ref[:width] = jnp.where(first, keep, other)
    out_ref[width:] = jnp.where(first, other, keep)


def gather_kernel(flags, own_ref, other_ref, out_ref):
    width = own_ref.shape[1]
    low = flags[1] != 0
    own, other = own_ref[...], other_ref[...]
    out_ref[:, :width] = jnp.where(low, own, other)
    out_ref[:, width:] = jnp.where(low, other, own)


def add_kernel(flags, a_ref, b_ref, out_ref):
    out_ref[...] = a_ref[...] + b_ref[...]


def eliminate(block, rows_ref, heads_ref):
    size = block.shape[0]
    group = 4
    sub = lax.broadcasted_iota(jnp.int32, (size, size), 0)
    lane = lax.broadcasted_iota(jnp.int32, (size, size), 1)
    left = block
    right = jnp.where(sub == lane, 1.0, 0.0).astype(f32)

    def spread(j):
        return [jnp.broadcast_to(left[:, j + p:j + p + 1], left.shape) for p in range(group)]

    cols = spread(0)
    for j in range(0, size, group):
        at = j % 8
        last = j + group == size
        ahead = [] if last else spread(j + group)
        rows = [left[at + p:at + p + 1] for p in range(group)]
        others = [right[at + p:at + p + 1] for p in range(group)]
        factors = []
        for p in range(group):
            head = cols[p][at + p:at + p + 1]
            factor = cols[p] * (1.0 / head)
            factors.append(factor)
            heads_ref[j + p:j + p + 1, :] = head
            rows_ref[j + p:j + p + 1, :] = others[p]
            for q in range(p + 1, group):
                cols[q] = cols[q] - factor * cols[p][at + q:at + q + 1]
                low = factor[at + q:at + q + 1]
                rows[q] = rows[q] - low * rows[p]
                others[q] = others[q] - low * others[p]
            for q in range(len(ahead)):
                here = at + group + q
                ahead[q] = ahead[q] - factor * cols[p][here:here + 1]
        if last:
            break
        cut = 8 if at + group == 8 else 0
        left, right, cols = left[cut:], right[cut:], [c[cut:] for c in ahead]
        for p in range(group):
            left = left - factors[p][cut:] * rows[p]
            right = right - factors[p][cut:] * others[p]


def factor_kernel(step, flags, *refs):
    if step == 0:
        gram_ref, out_state_ref, out_inv_ref, rows_ref, heads_ref = refs
    else:
        state_ref, inv_ref, out_state_ref, out_inv_ref, rows_ref, heads_ref = refs
    size = out_state_ref.shape[0]
    lo, hi = step * TILE, (step + 1) * TILE
    if step == 0:
        out_state_ref[...] = gram_ref[...]
        sub = lax.broadcasted_iota(jnp.int32, (size, size), 0)
        lane = lax.broadcasted_iota(jnp.int32, (size, size), 1)
        out_inv_ref[...] = jnp.where(sub == lane, 1.0, 0.0).astype(f32)
    else:
        out_state_ref[...] = state_ref[...]
        out_inv_ref[...] = inv_ref[...]
    eliminate(out_state_ref[lo:hi, lo:hi], rows_ref, heads_ref)
    block_inv = rows_ref[...] * lax.rsqrt(heads_ref[...])
    done = dot(block_inv, out_inv_ref[lo:hi, :hi])
    out_inv_ref[lo:hi, :hi] = done
    if hi < size:
        below = dot_nt(out_state_ref[hi:, lo:hi], block_inv)
        out_state_ref[hi:, hi:] = out_state_ref[hi:, hi:] - dot_nt(below, below)
        out_inv_ref[hi:, :hi] = out_inv_ref[hi:, :hi] - dot(below, done)


def weights_kernel(flags, both_ref, inv_ref, high_ref, low_ref):
    rows = both_ref.shape[0]
    width = both_ref.shape[1] // 2
    per_device = high_ref.shape[0] - rows
    inverse = inv_ref[...]
    high, low = split(inverse)
    ortho = split(dot3(split(both_ref[...]), split(inverse.T)))
    first = flags[2] != 0
    mine = inv_ref[pl.ds(pl.multiple_of(flags[5] * per_device, 8), per_device), :]

    def put(place, left, right):
        high_ref[place, :width], low_ref[place, :width] = split(jnp.where(first, left, right))
        high_ref[place, width:], low_ref[place, width:] = split(jnp.where(first, right, left))

    both = dot3(ortho, (high, low))
    put(slice(0, rows), both[:, :width], both[:, width:])
    put(slice(rows, rows + per_device), mine[:, :width], mine[:, width:])


def finish_kernel(flags, a_ref, high_ref, low_ref, first_ref, second_ref, rest_ref, factor_ref):
    rows, columns = a_ref.shape
    width = first_ref.shape[0]
    change = dot3((high_ref[:, :width], low_ref[:, :width]), split(first_ref[:, :columns]))
    change += dot3((high_ref[:, width:], low_ref[:, width:]), split(second_ref[:, :columns]))
    rest_ref[...] = a_ref[...] - change[:rows]
    factor_ref[...] = change[rows:]


def rows_kernel(parts, n, *refs):
    rests, factors, (rest_ref, factor_ref) = refs[:n], refs[n:2 * n], refs[2 * n:]

    def lay(pieces, out_ref):
        part = 0
        for piece in pieces:
            rows = piece.shape[0]
            for at in range(0, piece.shape[1], TILE):
                out_ref[pl.ds(part, rows, stride=parts), :] = piece[:, at:at + TILE]
                part += 1

    lay(rests, rest_ref)

    @pl.when(pl.program_id(0) == 0)
    def _():
        lay(factors, factor_ref)


def in_rows(rests, factors, parts):
    rows, own_rows = rests[0].shape[0], factors[0].shape[0]
    step = min(rows, 128)
    return pl.pallas_call(
        functools.partial(rows_kernel, parts, len(rests)),
        grid=(rows // step,),
        out_shape=[
            jax.ShapeDtypeStruct((rows * parts, TILE), f32),
            jax.ShapeDtypeStruct((own_rows * parts, TILE), f32),
        ],
        in_specs=[pl.BlockSpec((step, v.shape[1]), lambda i: (i, 0)) for v in rests]
        + [pl.BlockSpec(v.shape, lambda i: (0, 0)) for v in factors],
        out_specs=[
            pl.BlockSpec((step * parts, TILE), lambda i: (i, 0)),
            pl.BlockSpec((own_rows * parts, TILE), lambda i: (0, 0)),
        ],
        name="tiles_to_rows",
        compiler_params=pltpu.CompilerParams(vmem_limit_bytes=24 * 2**20),
    )(*rests, *factors)


def local(matrix):
    rows, blocks, _, width = matrix.shape
    parts = blocks * width // TILE
    depth = 2 * width
    n_row, n_col = lax.axis_size("prow"), lax.axis_size("pcol")
    row, col = lax.axis_index("prow"), lax.axis_index("pcol")
    place = row // 2
    line = n_row == 8
    sizes = SIZES if sum(SIZES) == blocks else (blocks,)
    flags = jnp.stack([
        col >= 2, col % 2 == 0, row % 2 == 0, (place == 1) | (place == 2), col, row,
    ]).astype(jnp.int32)
    chain = Chain()
    flat = matrix.reshape(rows * parts, TILE)

    held = matrix[:, 0, 0, :]
    reach = 2
    came = lax.ppermute(held, "pcol", [(0, 2), (1, 3)]) if n_col > 2 else held
    shapes = []
    for count in sizes:
        shape = (rows, count * width)
        shapes += [shape, (shape, bf16), (shape, bf16)]
    cuts = chain(functools.partial(spread_kernel, parts), "rows_to_tiles", shapes, flags, flat)
    cuts = [cuts[3 * k:3 * k + 3] for k in range(len(sizes))]
    held, = chain(functools.partial(pick_kernel, 0), "pick", [held.shape], flags, came, held)
    reach = 4
    while reach < n_col:
        came = lax.ppermute(held, "pcol", [(i, i + reach) for i in range(reach) if i + reach < n_col])
        held = jnp.where((col >= reach) & (col < 2 * reach), came, held)
        reach *= 2
    beside = flip(held, "pcol", 1)

    state = {}

    def in_hop(value):
        return lax.ppermute(value, "prow", [(0, 2), (1, 3), (6, 4), (7, 5)]) if line else None

    def mid_hop(value):
        return lax.ppermute(value, "prow", [(2, 4), (3, 5), (4, 2), (5, 3)]) if line else None

    def out_hop(value):
        return lax.ppermute(value, "prow", [(2, 0), (3, 1), (4, 6), (5, 7)]) if line else None

    def add(name, a, b):
        if b is None:
            return a
        return chain(add_kernel, name, [a.shape], flags, a, b)[0]

    def pick_inner(name, a, b):
        if b is None:
            bit = 2
            while bit < n_row:
                a = a + flip(a, "prow", bit)
                bit *= 2
            return a
        return chain(functools.partial(pick_kernel, 3), name, [a.shape], flags, a, b)[0]

    def run(task):
        if task == "panels":
            cut = (width, rows)
            both, keep, send, *parted = chain(
                panels_kernel, task, [(rows, depth), cut, cut] + [(cut, bf16)] * 4, flags, held, beside
            )
            state.update(both=both, keep=parted[:2], send=parted[2:], keep_more=[keep, held], send_more=[send, held])
        elif task == "g4":
            share, = chain(share_kernel, task, [(depth, width)], flags, state["s", 0], state["r", 0])
            state["gr"] = share, flip(share, "pcol", 1)
        elif task == "g6":
            state["gram"], = chain(gather_kernel, task, [(depth, depth)], flags, *state["gr"])
        elif task.startswith("ch"):
            step = int(task[2:])
            operands = [state["gram"]] if step == 0 else state["factor"]
            state["factor"] = chain(
                functools.partial(factor_kernel, step), f"factor{step}", [(depth, depth)] * 2, flags, *operands,
                scratch=[pltpu.VMEM((TILE, TILE), f32)] * 2,
            )
        elif task == "weights":
            cut = ((rows + depth // n_row, depth), bf16)
            state["weights"] = chain(weights_kernel, task, [cut] * 2, flags, state["both"], state["factor"][1])
        else:
            kind, k = task.rstrip("0123456789"), int(task.lstrip("abcdefghijklmnopqrstuvwxyz"))
            if k >= len(sizes):
                return
            count = (sizes[k] + (k == 0)) * width
            if kind == "send":
                more = state["send_more"] if k == 0 else []
                out, = chain(product_kernel, task, [(width, count)], flags, *state["send"], *cuts[k][1:], *more)
                state["r", k] = flip(out, "prow", 1)
            elif kind == "keep":
                more = state["keep_more"] if k == 0 else []
                out, = chain(product_add_kernel, task, [(width, count)],
                             flags, *state["keep"], *cuts[k][1:], state["r", k], *more)
                state["s", k], state["r", k] = out, in_hop(out)
            elif kind == "zm":
                out = add(task, state["s", k], state["r", k])
                state["s", k], state["r", k] = out, mid_hop(out)
            elif kind == "zo":
                out = add(task, state["s", k], state["r", k])
                state["s", k], state["r", k] = out, out_hop(out)
            elif kind == "ag":
                out = pick_inner(task, state["s", k], state["r", k])
                state["s", k], state["r", k] = out, flip(out, "prow", 1)
            elif kind == "fin":
                state["out", k] = chain(
                    finish_kernel, task, [(rows, sizes[k] * width), (depth // n_row, sizes[k] * width)],
                    flags, cuts[k][0], *state["weights"], state["s", k], state["r", k],
                )

    for task in " ".join(ORDER).split():
        if task[0] != "~":
            run(task)
        elif line and ("r", int(task[-1])) in state:
            chain.waits.append(state["r", int(task[-1])])
    outs = [state["out", k] for k in range(len(sizes))]
    rest, factor = in_rows([o[0] for o in outs], [o[1] for o in outs], parts)
    return (
        factor.reshape(depth // n_row, blocks, 1, width),
        rest.reshape(rows, blocks, 1, width),
    )


def solution(mesh):
    placed = P("prow", None, "pcol", None)
    return jax.shard_map(
        local, mesh=mesh, in_specs=(placed,), out_specs=(placed, placed), check_vma=False
    )
```

```python
import functools

import jax
import jax.numpy as jnp
from jax import lax
from jax.experimental import pallas as pl
from jax.experimental.pallas import tpu as pltpu
from jax.sharding import PartitionSpec as P

highest = lax.Precision.HIGHEST
f32 = jnp.float32
bf16 = jnp.bfloat16
TILE = 128
SIZES = (1, 2, 2, 2, 2, 2)
ORDER = (
    "panels send0 send1 send2", "send3 keep0 send4 send5", "keep1 zm0 keep2 zm1", "zo0 keep3 zm2 zo1",
    "~zo0 keep4 zm3 zo2", "~zo1 ag0 keep5 zm4", "zo3 ~zo2 ag1 g4", "zm5 zo4 ~zo3 ag2",
    "g6 ~ag1 ch0 zo5", "~zo4 ag3 ch1 ~ag2", "ag4 ~zo5 ag5 ch2", "ch3 ~ag3 weights fin0",
    "fin1 fin2 fin3 fin4", "fin5",
)


def dot(a, b):
    return jnp.dot(a, b, precision=highest, preferred_element_type=f32)


def dot_t(a, b):
    return lax.dot_general(a, b, (((0,), (0,)), ((), ())), precision=highest, preferred_element_type=f32)


def dot_nt(a, b):
    return lax.dot_general(a, b, (((1,), (1,)), ((), ())), precision=highest, preferred_element_type=f32)


def split(value):
    high = value.astype(bf16)
    return high, (value - high.astype(f32)).astype(bf16)


def dot3(a, b):
    def product(x, y):
        return jnp.dot(x, y, preferred_element_type=f32)

    return product(a[0], b[0]) + (product(a[0], b[1]) + product(a[1], b[0]))


def flip(value, axis, bit):
    n = lax.axis_size(axis)
    return lax.ppermute(value, axis, [(i, i ^ bit) for i in range(n)])


class Chain:
    def __init__(self):
        self.last = []
        self.waits = []

    def __call__(self, kernel, name, outs, flags, *operands, scratch=()):
        after = self.last + self.waits
        n_in, n_after = len(operands), len(after)
        vmem = pl.BlockSpec(memory_space=pltpu.VMEM)

        def body(*refs):
            skip = 1 + n_in
            kernel(*refs[:skip], *refs[skip + n_after:])

        result = pl.pallas_call(
            body,
            out_shape=[jax.ShapeDtypeStruct(*(o if isinstance(o[0], tuple) else (o, f32))) for o in outs],
            in_specs=[pl.BlockSpec(memory_space=pltpu.SMEM)] + [vmem] * n_in
            + [pl.BlockSpec(memory_space=pl.ANY)] * n_after,
            out_specs=[vmem] * len(outs),
            scratch_shapes=list(scratch),
            name=name,
            compiler_params=pltpu.CompilerParams(vmem_limit_bytes=24 * 2**20),
            cost_estimate=pl.CostEstimate(flops=1000, bytes_accessed=1000, transcendentals=0),
        )(flags, *operands, *after)
        self.last = [result[0]]
        self.waits = []
        return result


def spread_kernel(parts, flags, in_ref, *out_refs):
    part = 0
    for out_ref, high_ref, low_ref in zip(out_refs[::3], out_refs[1::3], out_refs[2::3]):
        rows, columns = out_ref.shape
        for at in range(0, columns, TILE):
            cut = slice(at, at + TILE)
            value = in_ref[pl.ds(part, rows, stride=parts), :]
            out_ref[:, cut] = value
            high_ref[:, cut], low_ref[:, cut] = split(value)
            part += 1


def pick_kernel(which, flags, a_ref, b_ref, out_ref):
    @pl.when(flags[which] != 0)
    def _():
        out_ref[...] = a_ref[...]

    @pl.when(flags[which] == 0)
    def _():
        out_ref[...] = b_ref[...]


def panels_kernel(
    flags, held_ref, other_ref, both_ref, keep_ref, send_ref, keep_high, keep_low, send_high, send_low
):
    width = held_ref.shape[1]
    held, other = held_ref[...], other_ref[...]
    low = flags[1] != 0
    p0, p1 = jnp.where(low, held, other), jnp.where(low, other, held)
    both_ref[:, :width] = p0
    both_ref[:, width:] = p1
    t0, t1 = p0.T, p1.T
    first = flags[2] != 0
    keep, send = jnp.where(first, t0, t1), jnp.where(first, t1, t0)
    keep_ref[...], send_ref[...] = keep, send
    keep_high[...], keep_low[...] = split(keep)
    send_high[...], send_low[...] = split(send)


def product_kernel(flags, panel_high, panel_low, a_high, a_low, *refs):
    columns, out_ref = a_high.shape[1], refs[-1]
    out_ref[:, :columns] = dot3((panel_high[...], panel_low[...]), (a_high[...], a_low[...]))
    if len(refs) > 1:
        out_ref[:, columns:] = dot(refs[0][...], refs[1][...])


def product_add_kernel(flags, panel_high, panel_low, a_high, a_low, came_ref, *refs):
    columns, out_ref = a_high.shape[1], refs[-1]
    product = dot3((panel_high[...], panel_low[...]), (a_high[...], a_low[...]))
    out_ref[:, :columns] = product + came_ref[:, :columns]
    if len(refs) > 1:
        out_ref[:, columns:] = dot(refs[0][...], refs[1][...]) + came_ref[:, columns:]


def share_kernel(flags, keep_ref, other_ref, out_ref):
    width = keep_ref.shape[0]
    first = flags[2] != 0
    keep, other = keep_ref[:, -width:], other_ref[:, -width:]
    out_ref[:width] = jnp.where(first, keep, other)
    out_ref[width:] = jnp.where(first, other, keep)


def gather_kernel(flags, own_ref, other_ref, out_ref):
    width = own_ref.shape[1]
    low = flags[1] != 0
    own, other = own_ref[...], other_ref[...]
    out_ref[:, :width] = jnp.where(low, own, other)
    out_ref[:, width:] = jnp.where(low, other, own)


def add_kernel(flags, a_ref, b_ref, out_ref):
    out_ref[...] = a_ref[...] + b_ref[...]


def eliminate(block, rows_ref, heads_ref):
    size = block.shape[0]
    group = 4
    sub = lax.broadcasted_iota(jnp.int32, (size, size), 0)
    lane = lax.broadcasted_iota(jnp.int32, (size, size), 1)
    left = block
    right = jnp.where(sub == lane, 1.0, 0.0).astype(f32)

    def spread(j):
        return [jnp.broadcast_to(left[:, j + p:j + p + 1], left.shape) for p in range(group)]

    cols = spread(0)
    for j in range(0, size, group):
        at = j % 8
        last = j + group == size
        ahead = [] if last else spread(j + group)
        rows = [left[at + p:at + p + 1] for p in range(group)]
        others = [right[at + p:at + p + 1] for p in range(group)]
        factors = []
        for p in range(group):
            head = cols[p][at + p:at + p + 1]
            factor = cols[p] * (1.0 / head)
            factors.append(factor)
            heads_ref[j + p:j + p + 1, :] = head
            rows_ref[j + p:j + p + 1, :] = others[p]
            for q in range(p + 1, group):
                cols[q] = cols[q] - factor * cols[p][at + q:at + q + 1]
                low = factor[at + q:at + q + 1]
                rows[q] = rows[q] - low * rows[p]
                others[q] = others[q] - low * others[p]
            for q in range(len(ahead)):
                here = at + group + q
                ahead[q] = ahead[q] - factor * cols[p][here:here + 1]
        if last:
            break
        cut = 8 if at + group == 8 else 0
        left, right, cols = left[cut:], right[cut:], [c[cut:] for c in ahead]
        for p in range(group):
            left = left - factors[p][cut:] * rows[p]
            right = right - factors[p][cut:] * others[p]


def factor_kernel(step, flags, *refs):
    if step == 0:
        gram_ref, out_state_ref, out_inv_ref, rows_ref, heads_ref = refs
    else:
        state_ref, inv_ref, out_state_ref, out_inv_ref, rows_ref, heads_ref = refs
    size = out_state_ref.shape[0]
    lo, hi = step * TILE, (step + 1) * TILE
    if step == 0:
        out_state_ref[...] = gram_ref[...]
        sub = lax.broadcasted_iota(jnp.int32, (size, size), 0)
        lane = lax.broadcasted_iota(jnp.int32, (size, size), 1)
        out_inv_ref[...] = jnp.where(sub == lane, 1.0, 0.0).astype(f32)
    else:
        out_state_ref[...] = state_ref[...]
        out_inv_ref[...] = inv_ref[...]
    eliminate(out_state_ref[lo:hi, lo:hi], rows_ref, heads_ref)
    block_inv = rows_ref[...] * lax.rsqrt(heads_ref[...])
    done = dot(block_inv, out_inv_ref[lo:hi, :hi])
    out_inv_ref[lo:hi, :hi] = done
    if hi < size:
        below = dot_nt(out_state_ref[hi:, lo:hi], block_inv)
        out_state_ref[hi:, hi:] = out_state_ref[hi:, hi:] - dot_nt(below, below)
        out_inv_ref[hi:, :hi] = out_inv_ref[hi:, :hi] - dot(below, done)


def weights_kernel(flags, both_ref, inv_ref, high_ref, low_ref):
    rows = both_ref.shape[0]
    width = both_ref.shape[1] // 2
    per_device = high_ref.shape[0] - rows
    inverse = inv_ref[...]
    high, low = split(inverse)
    ortho = split(dot3(split(both_ref[...]), split(inverse.T)))
    first = flags[2] != 0
    mine = inv_ref[pl.ds(pl.multiple_of(flags[5] * per_device, 8), per_device), :]

    def put(place, left, right):
        high_ref[place, :width], low_ref[place, :width] = split(jnp.where(first, left, right))
        high_ref[place, width:], low_ref[place, width:] = split(jnp.where(first, right, left))

    both = dot3(ortho, (high, low))
    put(slice(0, rows), both[:, :width], both[:, width:])
    put(slice(rows, rows + per_device), mine[:, :width], mine[:, width:])


def finish_kernel(flags, a_ref, high_ref, low_ref, first_ref, second_ref, rest_ref, factor_ref):
    rows, columns = a_ref.shape
    width = first_ref.shape[0]
    change = dot3((high_ref[:, :width], low_ref[:, :width]), split(first_ref[:, :columns]))
    change += dot3((high_ref[:, width:], low_ref[:, width:]), split(second_ref[:, :columns]))
    rest_ref[...] = a_ref[...] - change[:rows]
    factor_ref[...] = change[rows:]


def rows_kernel(parts, n, *refs):
    rests, factors, (rest_ref, factor_ref) = refs[:n], refs[n:2 * n], refs[2 * n:]

    def lay(pieces, out_ref):
        part = 0
        for piece in pieces:
            rows = piece.shape[0]
            for at in range(0, piece.shape[1], TILE):
                out_ref[pl.ds(part, rows, stride=parts), :] = piece[:, at:at + TILE]
                part += 1

    lay(rests, rest_ref)

    @pl.when(pl.program_id(0) == 0)
    def _():
        lay(factors, factor_ref)


def in_rows(rests, factors, parts):
    rows, own_rows = rests[0].shape[0], factors[0].shape[0]
    step = min(rows, 128)
    return pl.pallas_call(
        functools.partial(rows_kernel, parts, len(rests)),
        grid=(rows // step,),
        out_shape=[
            jax.ShapeDtypeStruct((rows * parts, TILE), f32),
            jax.ShapeDtypeStruct((own_rows * parts, TILE), f32),
        ],
        in_specs=[pl.BlockSpec((step, v.shape[1]), lambda i: (i, 0)) for v in rests]
        + [pl.BlockSpec(v.shape, lambda i: (0, 0)) for v in factors],
        out_specs=[
            pl.BlockSpec((step * parts, TILE), lambda i: (i, 0)),
            pl.BlockSpec((own_rows * parts, TILE), lambda i: (0, 0)),
        ],
        name="tiles_to_rows",
        compiler_params=pltpu.CompilerParams(vmem_limit_bytes=24 * 2**20),
    )(*rests, *factors)


def local(matrix):
    rows, blocks, _, width = matrix.shape
    parts = blocks * width // TILE
    depth = 2 * width
    n_row, n_col = lax.axis_size("prow"), lax.axis_size("pcol")
    row, col = lax.axis_index("prow"), lax.axis_index("pcol")
    place = row // 2
    line = n_row == 8
    sizes = SIZES if sum(SIZES) == blocks else (blocks,)
    flags = jnp.stack([
        col >= 2, col % 2 == 0, row % 2 == 0, (place == 1) | (place == 2), col, row,
    ]).astype(jnp.int32)
    chain = Chain()
    flat = matrix.reshape(rows * parts, TILE)

    held = matrix[:, 0, 0, :]
    reach = 2
    came = lax.ppermute(held, "pcol", [(0, 2), (1, 3)]) if n_col > 2 else held
    shapes = []
    for count in sizes:
        shape = (rows, count * width)
        shapes += [shape, (shape, bf16), (shape, bf16)]
    cuts = chain(functools.partial(spread_kernel, parts), "rows_to_tiles", shapes, flags, flat)
    cuts = [cuts[3 * k:3 * k + 3] for k in range(len(sizes))]
    held, = chain(functools.partial(pick_kernel, 0), "pick", [held.shape], flags, came, held)
    reach = 4
    while reach < n_col:
        came = lax.ppermute(held, "pcol", [(i, i + reach) for i in range(reach) if i + reach < n_col])
        held = jnp.where((col >= reach) & (col < 2 * reach), came, held)
        reach *= 2
    beside = flip(held, "pcol", 1)

    state = {}

    def in_hop(value):
        return lax.ppermute(value, "prow", [(0, 2), (1, 3), (6, 4), (7, 5)]) if line else None

    def mid_hop(value):
        return lax.ppermute(value, "prow", [(2, 4), (3, 5), (4, 2), (5, 3)]) if line else None

    def out_hop(value):
        return lax.ppermute(value, "prow", [(2, 0), (3, 1), (4, 6), (5, 7)]) if line else None

    def add(name, a, b):
        if b is None:
            return a
        return chain(add_kernel, name, [a.shape], flags, a, b)[0]

    def pick_inner(name, a, b):
        if b is None:
            bit = 2
            while bit < n_row:
                a = a + flip(a, "prow", bit)
                bit *= 2
            return a
        return chain(functools.partial(pick_kernel, 3), name, [a.shape], flags, a, b)[0]

    def run(task):
        if task == "panels":
            cut = (width, rows)
            both, keep, send, *parted = chain(
                panels_kernel, task, [(rows, depth), cut, cut] + [(cut, bf16)] * 4, flags, held, beside
            )
            state.update(both=both, keep=parted[:2], send=parted[2:], keep_more=[keep, held], send_more=[send, held])
        elif task == "g4":
            share, = chain(share_kernel, task, [(depth, width)], flags, state["s", 0], state["r", 0])
            state["gr"] = share, flip(share, "pcol", 1)
        elif task == "g6":
            state["gram"], = chain(gather_kernel, task, [(depth, depth)], flags, *state["gr"])
        elif task.startswith("ch"):
            step = int(task[2:])
            operands = [state["gram"]] if step == 0 else state["factor"]
            state["factor"] = chain(
                functools.partial(factor_kernel, step), f"factor{step}", [(depth, depth)] * 2, flags, *operands,
                scratch=[pltpu.VMEM((TILE, TILE), f32)] * 2,
            )
        elif task == "weights":
            cut = ((rows + depth // n_row, depth), bf16)
            state["weights"] = chain(weights_kernel, task, [cut] * 2, flags, state["both"], state["factor"][1])
        else:
            kind, k = task.rstrip("0123456789"), int(task.lstrip("abcdefghijklmnopqrstuvwxyz"))
            if k >= len(sizes):
                return
            count = (sizes[k] + (k == 0)) * width
            if kind == "send":
                more = state["send_more"] if k == 0 else []
                out, = chain(product_kernel, task, [(width, count)], flags, *state["send"], *cuts[k][1:], *more)
                state["r", k] = flip(out, "prow", 1)
            elif kind == "keep":
                more = state["keep_more"] if k == 0 else []
                out, = chain(product_add_kernel, task, [(width, count)],
                             flags, *state["keep"], *cuts[k][1:], state["r", k], *more)
                state["s", k], state["r", k] = out, in_hop(out)
            elif kind == "zm":
                out = add(task, state["s", k], state["r", k])
                state["s", k], state["r", k] = out, mid_hop(out)
            elif kind == "zo":
                out = add(task, state["s", k], state["r", k])
                state["s", k], state["r", k] = out, out_hop(out)
            elif kind == "ag":
                out = pick_inner(task, state["s", k], state["r", k])
                state["s", k], state["r", k] = out, flip(out, "prow", 1)
            elif kind == "fin":
                state["out", k] = chain(
                    finish_kernel, task, [(rows, sizes[k] * width), (depth // n_row, sizes[k] * width)],
                    flags, cuts[k][0], *state["weights"], state["s", k], state["r", k],
                )

    for task in " ".join(ORDER).split():
        if task[0] != "~":
            run(task)
        elif line and ("r", int(task[-1])) in state:
            chain.waits.append(state["r", int(task[-1])])
    outs = [state["out", k] for k in range(len(sizes))]
    rest, factor = in_rows([o[0] for o in outs], [o[1] for o in outs], parts)
    return (
        factor.reshape(depth // n_row, blocks, 1, width),
        rest.reshape(rows, blocks, 1, width),
    )


def solution(mesh):
    placed = P("prow", None, "pcol", None)
    return jax.shard_map(
        local, mesh=mesh, in_specs=(placed,), out_specs=(placed, placed), check_vma=False
    )
```

```python
import functools

import jax
import jax.numpy as jnp
from jax import lax
from jax.experimental import pallas as pl
from jax.experimental.pallas import tpu as pltpu
from jax.sharding import PartitionSpec as P

highest = lax.Precision.HIGHEST
f32 = jnp.float32
bf16 = jnp.bfloat16
TILE = 128
EXTRA = 32
PIECES = 1
GROUPS = (4, 1, 2, 2, 2)
GROUP_OF = (0, 1, 0, 2, 3, 4)
ORDER = (
    "ka pa send0 kb", "pb send1 send2 send3", "keep0 send4 send5 keep1", "zm0 keep2 zm1 zo0",
    "keep3 zm2 zo1 ~zo0", "keep4 zm3 zo2 ~zo1", "ag0 keep5 zm4 zo3", "~zo2 ~ag0 ag1 zm5",
    "zo4 ~zo3 ag2 g4", "~zo4 ag3 zo5 g6", "ch0 ~ag2 ag4 ch1", "~zo5 ag5 ch2 ch3",
    "weights fin1 fin0 ~ag3", "fin3 ~ag4 fin4",
)


def dot(a, b):
    return jnp.dot(a, b, precision=highest, preferred_element_type=f32)


def dot_t(a, b):
    return lax.dot_general(a, b, (((0,), (0,)), ((), ())), precision=highest, preferred_element_type=f32)


def dot_nt(a, b):
    return lax.dot_general(a, b, (((1,), (1,)), ((), ())), precision=highest, preferred_element_type=f32)


def split(value):
    high = value.astype(bf16)
    return high, (value - high.astype(f32)).astype(bf16)


def dot3(a, b):
    def product(x, y):
        return jnp.dot(x, y, preferred_element_type=f32)

    return product(a[0], b[0]) + (product(a[0], b[1]) + product(a[1], b[0]))


def flip(value, axis, bit):
    n = lax.axis_size(axis)
    return lax.ppermute(value, axis, [(i, i ^ bit) for i in range(n)])


class Chain:
    def __init__(self):
        self.last = []
        self.waits = []

    def __call__(self, kernel, name, outs, flags, *operands, scratch=()):
        after = self.last + self.waits
        n_in, n_after = len(operands), len(after)
        vmem = pl.BlockSpec(memory_space=pltpu.VMEM)

        def body(*refs):
            kernel(refs[0], *refs[1 + n_after:])

        result = pl.pallas_call(
            body,
            out_shape=[jax.ShapeDtypeStruct(*(o if isinstance(o[0], tuple) else (o, f32))) for o in outs],
            in_specs=[pl.BlockSpec(memory_space=pltpu.SMEM)] + [pl.BlockSpec(memory_space=pl.ANY)] * n_after
            + [vmem] * n_in,
            out_specs=[vmem] * len(outs),
            scratch_shapes=list(scratch),
            name=name,
            compiler_params=pltpu.CompilerParams(vmem_limit_bytes=24 * 2**20),
            cost_estimate=pl.CostEstimate(flops=1000, bytes_accessed=1000, transcendentals=0),
        )(flags, *after, *operands)
        self.last = [result[0]]
        self.waits = []
        return result


def spread_kernel(parts, flags, in_ref, *out_refs):
    part = 0
    for out_ref, high_ref, low_ref in zip(out_refs[::3], out_refs[1::3], out_refs[2::3]):
        rows, columns = out_ref.shape
        for at in range(0, columns, TILE):
            cut = slice(at, at + TILE)
            value = in_ref[pl.ds(part, rows, stride=parts), :]
            out_ref[:, cut] = value
            high_ref[:, cut], low_ref[:, cut] = split(value)
            part += 1


def pick_kernel(which, flags, a_ref, b_ref, *out_refs):
    for choice, ref in enumerate((b_ref, a_ref)):
        @pl.when(flags[which] == choice)
        def _():
            at = 0
            for out_ref in out_refs:
                out_ref[...] = ref[at:at + out_ref.shape[0]]
                at += out_ref.shape[0]


def half_panels_kernel(flags, *refs):
    pieces, (keep_high, keep_low, send_high, send_low) = refs[:-4], refs[-4:]
    count = len(pieces) // 2
    held, other = (jnp.concatenate([r[...] for r in part], 0).T for part in (pieces[:count], pieces[count:]))
    same = flags[1] == flags[2]
    keep_high[...], keep_low[...] = split(jnp.where(same, held, other))
    send_high[...], send_low[...] = split(jnp.where(same, other, held))


def joined(refs):
    later = [jnp.concatenate([r[...] for r in part], 0) for part in (refs[2:2 + PIECES], refs[2 + PIECES:])]
    return [jnp.concatenate([r[...], v], 1) for r, v in zip(refs, later)]


def product_kernel(count, kept, flags, *refs):
    highs, lows, (a_high, a_low) = refs[:count], refs[count:2 * count], refs[2 * count:2 * count + 2]
    rest, out_ref = refs[2 * count + 2:-1], refs[-1]
    columns = a_high.shape[1]
    came = rest[0][...] if kept else None
    panel = [jnp.concatenate([r[...] for r in part], 0) for part in (highs, lows)]
    product = dot3(panel, (a_high[...], a_low[...]))
    out_ref[:, :columns] = product + came[:, :columns] if kept else product
    halves = rest[1 if kept else 0:]
    if halves:
        held, other = joined(halves)
        mine = (flags[1] == flags[2]) == kept
        product = dot_t(jnp.where(mine, held, other), held)
        out_ref[:, columns:] = product + came[:, columns:] if kept else product


def share_kernel(flags, keep_ref, other_ref, out_ref):
    width = keep_ref.shape[0]
    first = flags[2] != 0
    keep, other = keep_ref[:, -width:], other_ref[:, -width:]
    out_ref[:width] = jnp.where(first, keep, other)
    out_ref[width:] = jnp.where(first, other, keep)


def gather_kernel(flags, own_ref, other_ref, out_ref):
    width = own_ref.shape[1]
    low = flags[1] != 0
    own, other = own_ref[...], other_ref[...]
    out_ref[:, :width] = jnp.where(low, own, other)
    out_ref[:, width:] = jnp.where(low, other, own)


def add_kernel(flags, a_ref, b_ref, out_ref):
    out_ref[...] = a_ref[...] + b_ref[...]


def eliminate(block, rows_ref, heads_ref):
    size = block.shape[0]
    group = 4
    sub = lax.broadcasted_iota(jnp.int32, (size, size), 0)
    lane = lax.broadcasted_iota(jnp.int32, (size, size), 1)
    left = block
    right = jnp.where(sub == lane, 1.0, 0.0).astype(f32)

    def spread(j):
        return [jnp.broadcast_to(left[:, j + p:j + p + 1], left.shape) for p in range(group)]

    cols = spread(0)
    for j in range(0, size, group):
        at = j % 8
        last = j + group == size
        ahead = [] if last else spread(j + group)
        rows = [left[at + p:at + p + 1] for p in range(group)]
        others = [right[at + p:at + p + 1] for p in range(group)]
        factors = []
        for p in range(group):
            head = cols[p][at + p:at + p + 1]
            factor = cols[p] * (1.0 / head)
            factors.append(factor)
            heads_ref[j + p:j + p + 1, :] = head
            rows_ref[j + p:j + p + 1, :] = others[p]
            for q in range(p + 1, group):
                cols[q] = cols[q] - factor * cols[p][at + q:at + q + 1]
                low = factor[at + q:at + q + 1]
                rows[q] = rows[q] - low * rows[p]
                others[q] = others[q] - low * others[p]
            for q in range(len(ahead)):
                here = at + group + q
                ahead[q] = ahead[q] - factor * cols[p][here:here + 1]
        if last:
            break
        cut = 8 if at + group == 8 else 0
        left, right, cols = left[cut:], right[cut:], [c[cut:] for c in ahead]
        for p in range(group):
            left = left - factors[p][cut:] * rows[p]
            right = right - factors[p][cut:] * others[p]


def factor_kernel(step, flags, *refs):
    if step == 0:
        gram_ref, out_state_ref, out_inv_ref, rows_ref, heads_ref = refs
    else:
        state_ref, inv_ref, out_state_ref, out_inv_ref, rows_ref, heads_ref = refs
    size = out_state_ref.shape[0]
    lo, hi = step * TILE, (step + 1) * TILE
    if step == 0:
        out_state_ref[...] = gram_ref[...]
        sub = lax.broadcasted_iota(jnp.int32, (size, size), 0)
        lane = lax.broadcasted_iota(jnp.int32, (size, size), 1)
        out_inv_ref[...] = jnp.where(sub == lane, 1.0, 0.0).astype(f32)
    else:
        out_state_ref[...] = state_ref[...]
        out_inv_ref[...] = inv_ref[...]
    eliminate(out_state_ref[lo:hi, lo:hi], rows_ref, heads_ref)
    block_inv = rows_ref[...] * lax.rsqrt(heads_ref[...])
    done = dot(block_inv, out_inv_ref[lo:hi, :hi])
    out_inv_ref[lo:hi, :hi] = done
    if hi < size:
        below = dot_nt(out_state_ref[hi:, lo:hi], block_inv)
        out_state_ref[hi:, hi:] = out_state_ref[hi:, hi:] - dot_nt(below, below)
        out_inv_ref[hi:, :hi] = out_inv_ref[hi:, :hi] - dot(below, done)


def weights_kernel(flags, *refs):
    inv_ref, high_ref, low_ref = refs[-3:]
    held, other = joined(refs[:-3])
    rows, width = held.shape
    low_core = flags[1] != 0
    panels = jnp.concatenate([jnp.where(low_core, held, other), jnp.where(low_core, other, held)], 1)
    per_device = high_ref.shape[0] - rows
    inverse = inv_ref[...]
    high, low = split(inverse)
    ortho = split(dot3(split(panels), split(inverse.T)))
    first = flags[2] != 0
    mine = inv_ref[pl.ds(pl.multiple_of(flags[5] * per_device, 8), per_device), :]

    def put(place, left, right):
        high_ref[place, :width], low_ref[place, :width] = split(jnp.where(first, left, right))
        high_ref[place, width:], low_ref[place, width:] = split(jnp.where(first, right, left))

    both = dot3(ortho, (high, low))
    put(slice(0, rows), both[:, :width], both[:, width:])
    put(slice(rows, rows + per_device), mine[:, :width], mine[:, width:])


def finish_kernel(flags, a_ref, high_ref, low_ref, *refs):
    (rest_ref, factor_ref), sums = refs[-2:], refs[:-2]
    rows, columns = a_ref.shape
    count = len(sums) // 2
    first, second = (
        split(jnp.concatenate([r[:, :columns] for r in part], 0)) for part in (sums[:count], sums[count:])
    )
    width = first[0].shape[0]
    change = dot3((high_ref[:, :width], low_ref[:, :width]), first)
    change += dot3((high_ref[:, width:], low_ref[:, width:]), second)
    rest_ref[...] = a_ref[...] - change[:rows]
    factor_ref[...] = change[rows:]


def rows_kernel(parts, n, a_ref, high_ref, low_ref, mine_high, mine_low, first_ref, second_ref, *refs):
    rests, factors, (rest_ref, factor_ref, *sums) = refs[:n], refs[n:2 * n], refs[2 * n:]
    width = first_ref.shape[0]

    @pl.when(pl.program_id(0) == 0)
    def _():
        sums[0][...], sums[1][...] = split(first_ref[...])
        sums[2][...], sums[3][...] = split(second_ref[...])

    def update(high, low):
        change = dot3((high[:, :width], low[:, :width]), (sums[0][...], sums[1][...]))
        return change + dot3((high[:, width:], low[:, width:]), (sums[2][...], sums[3][...]))

    def lay(pieces, out_ref):
        part = 0
        for piece in pieces:
            rows = piece.shape[0]
            for at in range(0, piece.shape[1], TILE):
                out_ref[pl.ds(part, rows, stride=parts), :] = piece[:, at:at + TILE]
                part += 1

    lay([*rests, a_ref[...] - update(high_ref, low_ref)], rest_ref)

    @pl.when(pl.program_id(0) == 0)
    def _():
        lay([*factors, update(mine_high, mine_low)], factor_ref)


def in_rows(last, weights, first, second, rests, factors, parts):
    rows, own_rows = last.shape[0], factors[0].shape[0]
    step = min(rows, 128)
    by_rows = lambda v: pl.BlockSpec((step, v.shape[1]), lambda i: (i, 0))
    whole = lambda v: pl.BlockSpec(v.shape, lambda i: (0, 0))
    mine = pl.BlockSpec((own_rows, weights[0].shape[1]), lambda i: (rows // own_rows, 0))
    return pl.pallas_call(
        functools.partial(rows_kernel, parts, len(rests)),
        grid=(rows // step,),
        out_shape=[
            jax.ShapeDtypeStruct((rows * parts, TILE), f32),
            jax.ShapeDtypeStruct((own_rows * parts, TILE), f32),
        ],
        in_specs=[by_rows(last), by_rows(weights[0]), by_rows(weights[1]), mine, mine, whole(first), whole(second)]
        + [by_rows(v) for v in rests] + [whole(v) for v in factors],
        out_specs=[
            pl.BlockSpec((step * parts, TILE), lambda i: (i, 0)),
            pl.BlockSpec((own_rows * parts, TILE), lambda i: (0, 0)),
        ],
        scratch_shapes=[pltpu.VMEM(first.shape, bf16)] * 4,
        name="tiles_to_rows",
        compiler_params=pltpu.CompilerParams(vmem_limit_bytes=24 * 2**20),
    )(last, *weights, *weights, first, second, *rests, *factors)


def local(matrix):
    rows, blocks, _, width = matrix.shape
    parts = blocks * width // TILE
    depth = 2 * width
    n_row, n_col = lax.axis_size("prow"), lax.axis_size("pcol")
    row, col = lax.axis_index("prow"), lax.axis_index("pcol")
    place = row // 2
    line = n_row == 8
    flags = jnp.stack([
        col >= 2, col % 2 == 0, row % 2 == 0, (place == 1) | (place == 2), col, row,
    ]).astype(jnp.int32)
    chain = Chain()
    flat = matrix.reshape(rows * parts, TILE)

    own = [matrix[:, 0, 0, :width // 2], matrix[:, 0, 0, width // 2:]]
    own[1] = jnp.concatenate([own[1], own[1][:EXTRA]], 0)
    came = [lax.ppermute(v, "pcol", [(0, 2), (1, 3)]) for v in own]
    shapes = []
    for count in GROUPS:
        shape = (rows, count * width)
        shapes += [shape, (shape, bf16), (shape, bf16)]
    cuts = chain(functools.partial(spread_kernel, parts), "rows_to_tiles", shapes, flags, flat)
    cuts = [cuts[3 * k:3 * k + 3] for k in range(len(GROUPS))]

    def bring(which, name):
        pieces = (1, PIECES)[which]
        held = chain(
            functools.partial(pick_kernel, 0), name, [(rows // pieces, width // 2)] * pieces, flags,
            came[which], own[which],
        )
        reach = 4
        while reach < n_col:
            pairs = [(i, i + reach) for i in range(reach) if i + reach < n_col]
            at = (col >= reach) & (col < 2 * reach)
            held = [jnp.where(at, lax.ppermute(v, "pcol", pairs), v) for v in held]
            reach *= 2
        return [*held, *[flip(v, "pcol", 1) for v in held]]

    state = {}

    def in_hop(value):
        return lax.ppermute(value, "prow", [(0, 2), (1, 3), (6, 4), (7, 5)]) if line else None

    def mid_hop(value):
        return lax.ppermute(value, "prow", [(2, 4), (3, 5), (4, 2), (5, 3)]) if line else None

    def out_hop(value):
        return lax.ppermute(value, "prow", [(2, 0), (3, 1), (4, 6), (5, 7)]) if line else None

    def add(name, a, b):
        if b is None:
            return a
        return chain(add_kernel, name, [a.shape], flags, a, b)[0]

    def pick_inner(name, a, b):
        if b is None:
            bit = 2
            while bit < n_row:
                a = a + flip(a, "prow", bit)
                bit *= 2
            return a
        return chain(functools.partial(pick_kernel, 3), name, [a.shape], flags, a, b)[0]

    def run(task):
        if task == "ka" or task == "kb":
            state[task] = bring("ab".index(task[1]), task)
        elif task == "pa" or task == "pb":
            half = ((width // 2, rows), bf16)
            state[task] = chain(half_panels_kernel, task, [half] * 4, flags, *state["k" + task[1]])
        elif task == "g4":
            share, = chain(share_kernel, task, [(depth, width)], flags, state["s", 1], state["r", 1])
            state["gr"] = share, flip(share, "pcol", 1)
        elif task == "g6":
            state["gram"], = chain(gather_kernel, task, [(depth, depth)], flags, *state["gr"])
        elif task.startswith("ch"):
            step = int(task[2:])
            operands = [state["gram"]] if step == 0 else state["factor"]
            state["factor"] = chain(
                functools.partial(factor_kernel, step), f"factor{step}", [(depth, depth)] * 2, flags, *operands,
                scratch=[pltpu.VMEM((TILE, TILE), f32)] * 2,
            )
        elif task == "weights":
            cut = ((rows + depth // n_row, depth), bf16)
            state["weights"] = chain(weights_kernel, task, [cut] * 2, flags, *state["ka"], *state["kb"], state["factor"][1])
        else:
            kind, k = task.rstrip("0123456789"), int(task.lstrip("abcdefghijklmnopqrstuvwxyz"))
            group = GROUP_OF[k]
            lines = width if GROUP_OF.count(group) == 1 else width // 2
            halves = [state[p] for p in (("pa",), ("pa", "pb"), ("pb",))[min(k, 1) if k != 2 else 2]]
            shape = (lines, GROUPS[group] * width + (k == 1) * width)
            more = [*state["ka"], *state["kb"]] if k == 1 else []
            if kind == "send":
                pieces = [p[2] for p in halves] + [p[3] for p in halves]
                out, = chain(functools.partial(product_kernel, len(halves), False), task, [shape],
                             flags, *pieces, *cuts[group][1:], *more)
                state["r", k] = flip(out, "prow", 1)
            elif kind == "keep":
                pieces = [p[0] for p in halves] + [p[1] for p in halves]
                out, = chain(functools.partial(product_kernel, len(halves), True), task, [shape],
                             flags, *pieces, *cuts[group][1:], state["r", k], *more)
                state["s", k], state["r", k] = out, in_hop(out)
            elif kind == "zm":
                out = add(task, state["s", k], state["r", k])
                state["s", k], state["r", k] = out, mid_hop(out)
            elif kind == "zo":
                out = add(task, state["s", k], state["r", k])
                state["s", k], state["r", k] = out, out_hop(out)
            elif kind == "ag":
                out = pick_inner(task, state["s", k], state["r", k])
                state["s", k], state["r", k] = out, flip(out, "prow", 1)
            elif kind == "fin":
                pieces = [j for j, g in enumerate(GROUP_OF) if g == group]
                state["out", group] = chain(
                    finish_kernel, task, [(rows, GROUPS[group] * width), (depth // n_row, GROUPS[group] * width)],
                    flags, cuts[group][0], *state["weights"],
                    *[state["s", j] for j in pieces], *[state["r", j] for j in pieces],
                )

    for task in " ".join(ORDER).split():
        if task[0] != "~":
            run(task)
        elif line and ("r", int(task[-1])) in state:
            chain.waits.append(state["r", int(task[-1])])
    end = len(GROUPS) - 1
    outs = [state["out", k] for k in range(end)]
    k = GROUP_OF.index(end)
    rest, factor = in_rows(
        cuts[end][0], state["weights"], state["s", k], state["r", k],
        [o[0] for o in outs], [o[1] for o in outs], parts,
    )
    return (
        factor.reshape(depth // n_row, blocks, 1, width),
        rest.reshape(rows, blocks, 1, width),
    )


def solution(mesh):
    placed = P("prow", None, "pcol", None)
    return jax.shard_map(
        local, mesh=mesh, in_specs=(placed,), out_specs=(placed, placed), check_vma=False
    )
```

```python
import functools

import jax
import jax.numpy as jnp
from jax import lax
from jax.experimental import pallas as pl
from jax.experimental.pallas import tpu as pltpu
from jax.sharding import PartitionSpec as P

highest = lax.Precision.HIGHEST
f32 = jnp.float32
bf16 = jnp.bfloat16
TILE = 128
EXTRA = 32
PIECES = 1
GROUPS = (4, 1, 2, 2, 2)
GROUP_OF = (0, 1, 0, 2, 3, 4)
ORDER = (
    "ka pa send0 kb", "pb send1 send2 send3", "keep0 send4 send5 keep1", "zm0 keep2 zm1 zo0",
    "keep3 zm2 zo1 ~zo0", "keep4 zm3 zo2 ~zo1", "ag0 keep5 zm4 zo3", "~zo2 ag1 ~ag0 zm5",
    "zo4 ~zo3 ag2 g4", "zo5 ~zo4 ag3 g6", "ch0 ~ag2 ag4 ch1", "~zo5 ag5 ~ag3 ch2",
    "ch3 weights fin1 fin0", "fin3 ~ag4 fin4",
)


def dot(a, b):
    return jnp.dot(a, b, precision=highest, preferred_element_type=f32)


def dot_t(a, b):
    return lax.dot_general(a, b, (((0,), (0,)), ((), ())), precision=highest, preferred_element_type=f32)


def dot_nt(a, b):
    return lax.dot_general(a, b, (((1,), (1,)), ((), ())), precision=highest, preferred_element_type=f32)


def split(value):
    high = value.astype(bf16)
    return high, (value - high.astype(f32)).astype(bf16)


def dot3(a, b):
    def product(x, y):
        return jnp.dot(x, y, preferred_element_type=f32)

    return product(a[0], b[0]) + (product(a[0], b[1]) + product(a[1], b[0]))


def flip(value, axis, bit):
    n = lax.axis_size(axis)
    return lax.ppermute(value, axis, [(i, i ^ bit) for i in range(n)])


class Chain:
    def __init__(self):
        self.last = []
        self.waits = []

    def __call__(self, kernel, name, outs, flags, *operands, scratch=()):
        after = self.last + self.waits
        n_in, n_after = len(operands), len(after)
        vmem = pl.BlockSpec(memory_space=pltpu.VMEM)

        def body(*refs):
            kernel(refs[0], *refs[1 + n_after:])

        result = pl.pallas_call(
            body,
            out_shape=[jax.ShapeDtypeStruct(*(o if isinstance(o[0], tuple) else (o, f32))) for o in outs],
            in_specs=[pl.BlockSpec(memory_space=pltpu.SMEM)] + [pl.BlockSpec(memory_space=pl.ANY)] * n_after
            + [vmem] * n_in,
            out_specs=[vmem] * len(outs),
            scratch_shapes=list(scratch),
            name=name,
            compiler_params=pltpu.CompilerParams(vmem_limit_bytes=24 * 2**20),
            cost_estimate=pl.CostEstimate(flops=1000, bytes_accessed=1000, transcendentals=0),
        )(flags, *after, *operands)
        self.last = [result[0]]
        self.waits = []
        return result


def spread_kernel(parts, flags, in_ref, *out_refs):
    part = 0
    for out_ref, high_ref, low_ref in zip(out_refs[::3], out_refs[1::3], out_refs[2::3]):
        rows, columns = out_ref.shape
        for at in range(0, columns, TILE):
            cut = slice(at, at + TILE)
            value = in_ref[pl.ds(part, rows, stride=parts), :]
            out_ref[:, cut] = value
            high_ref[:, cut], low_ref[:, cut] = split(value)
            part += 1


def pick_kernel(which, flags, a_ref, b_ref, *out_refs):
    for choice, ref in enumerate((b_ref, a_ref)):
        @pl.when(flags[which] == choice)
        def _():
            at = 0
            for out_ref in out_refs:
                out_ref[...] = ref[at:at + out_ref.shape[0]]
                at += out_ref.shape[0]


def half_panels_kernel(flags, *refs):
    pieces, (keep_high, keep_low, send_high, send_low) = refs[:-4], refs[-4:]
    count = len(pieces) // 2
    held, other = (jnp.concatenate([r[...] for r in part], 0).T for part in (pieces[:count], pieces[count:]))
    same = flags[1] == flags[2]
    keep_high[...], keep_low[...] = split(jnp.where(same, held, other))
    send_high[...], send_low[...] = split(jnp.where(same, other, held))


def joined(refs):
    later = [jnp.concatenate([r[...] for r in part], 0) for part in (refs[2:2 + PIECES], refs[2 + PIECES:])]
    return [jnp.concatenate([r[...], v], 1) for r, v in zip(refs, later)]


def product_kernel(count, kept, flags, *refs):
    highs, lows, (a_high, a_low) = refs[:count], refs[count:2 * count], refs[2 * count:2 * count + 2]
    rest, out_ref = refs[2 * count + 2:-1], refs[-1]
    columns = a_high.shape[1]
    came = rest[0][...] if kept else None
    panel = [jnp.concatenate([r[...] for r in part], 0) for part in (highs, lows)]
    product = dot3(panel, (a_high[...], a_low[...]))
    out_ref[:, :columns] = product + came[:, :columns] if kept else product
    halves = rest[1 if kept else 0:]
    if halves:
        held, other = joined(halves)
        mine = (flags[1] == flags[2]) == kept
        product = dot_t(jnp.where(mine, held, other), held)
        out_ref[:, columns:] = product + came[:, columns:] if kept else product


def share_kernel(flags, keep_ref, other_ref, out_ref):
    width = keep_ref.shape[0]
    first = flags[2] != 0
    keep, other = keep_ref[:, -width:], other_ref[:, -width:]
    out_ref[:width] = jnp.where(first, keep, other)
    out_ref[width:] = jnp.where(first, other, keep)


def gather_kernel(flags, own_ref, other_ref, out_ref):
    width = own_ref.shape[1]
    low = flags[1] != 0
    own, other = own_ref[...], other_ref[...]
    out_ref[:, :width] = jnp.where(low, own, other)
    out_ref[:, width:] = jnp.where(low, other, own)


def add_kernel(flags, a_ref, b_ref, out_ref):
    out_ref[...] = a_ref[...] + b_ref[...]


def eliminate(block, rows_ref, heads_ref):
    size = block.shape[0]
    group = 4
    sub = lax.broadcasted_iota(jnp.int32, (size, size), 0)
    lane = lax.broadcasted_iota(jnp.int32, (size, size), 1)
    left = block
    right = jnp.where(sub == lane, 1.0, 0.0).astype(f32)

    def spread(j):
        return [jnp.broadcast_to(left[:, j + p:j + p + 1], left.shape) for p in range(group)]

    cols = spread(0)
    for j in range(0, size, group):
        at = j % 8
        last = j + group == size
        ahead = [] if last else spread(j + group)
        rows = [left[at + p:at + p + 1] for p in range(group)]
        others = [right[at + p:at + p + 1] for p in range(group)]
        factors = []
        for p in range(group):
            head = cols[p][at + p:at + p + 1]
            factor = cols[p] * (1.0 / head)
            factors.append(factor)
            heads_ref[j + p:j + p + 1, :] = head
            rows_ref[j + p:j + p + 1, :] = others[p]
            for q in range(p + 1, group):
                cols[q] = cols[q] - factor * cols[p][at + q:at + q + 1]
                low = factor[at + q:at + q + 1]
                rows[q] = rows[q] - low * rows[p]
                others[q] = others[q] - low * others[p]
            for q in range(len(ahead)):
                here = at + group + q
                ahead[q] = ahead[q] - factor * cols[p][here:here + 1]
        if last:
            break
        cut = 8 if at + group == 8 else 0
        left, right, cols = left[cut:], right[cut:], [c[cut:] for c in ahead]
        for p in range(group):
            left = left - factors[p][cut:] * rows[p]
            right = right - factors[p][cut:] * others[p]


def factor_kernel(step, flags, *refs):
    if step == 0:
        gram_ref, out_state_ref, out_inv_ref, rows_ref, heads_ref = refs
    else:
        state_ref, inv_ref, out_state_ref, out_inv_ref, rows_ref, heads_ref = refs
    size = out_state_ref.shape[0]
    lo, hi = step * TILE, (step + 1) * TILE
    if step == 0:
        out_state_ref[...] = gram_ref[...]
        sub = lax.broadcasted_iota(jnp.int32, (size, size), 0)
        lane = lax.broadcasted_iota(jnp.int32, (size, size), 1)
        out_inv_ref[...] = jnp.where(sub == lane, 1.0, 0.0).astype(f32)
    else:
        out_state_ref[...] = state_ref[...]
        out_inv_ref[...] = inv_ref[...]
    eliminate(out_state_ref[lo:hi, lo:hi], rows_ref, heads_ref)
    block_inv = rows_ref[...] * lax.rsqrt(heads_ref[...])
    done = dot(block_inv, out_inv_ref[lo:hi, :hi])
    out_inv_ref[lo:hi, :hi] = done
    if hi < size:
        below = dot_nt(out_state_ref[hi:, lo:hi], block_inv)
        out_state_ref[hi:, hi:] = out_state_ref[hi:, hi:] - dot_nt(below, below)
        out_inv_ref[hi:, :hi] = out_inv_ref[hi:, :hi] - dot(below, done)


def weights_kernel(flags, *refs):
    inv_ref, high_ref, low_ref = refs[-3:]
    held, other = joined(refs[:-3])
    rows, width = held.shape
    low_core = flags[1] != 0
    panels = jnp.concatenate([jnp.where(low_core, held, other), jnp.where(low_core, other, held)], 1)
    per_device = high_ref.shape[0] - rows
    inverse = inv_ref[...]
    high, low = split(inverse)
    ortho = split(dot3(split(panels), split(inverse.T)))
    first = flags[2] != 0
    mine = inv_ref[pl.ds(pl.multiple_of(flags[5] * per_device, 8), per_device), :]

    def put(place, left, right):
        high_ref[place, :width], low_ref[place, :width] = split(jnp.where(first, left, right))
        high_ref[place, width:], low_ref[place, width:] = split(jnp.where(first, right, left))

    both = dot3(ortho, (high, low))
    put(slice(0, rows), both[:, :width], both[:, width:])
    put(slice(rows, rows + per_device), mine[:, :width], mine[:, width:])


def finish_kernel(flags, a_ref, high_ref, low_ref, *refs):
    (rest_ref, factor_ref), sums = refs[-2:], refs[:-2]
    rows, columns = a_ref.shape
    count = len(sums) // 2
    first, second = (
        split(jnp.concatenate([r[:, :columns] for r in part], 0)) for part in (sums[:count], sums[count:])
    )
    width = first[0].shape[0]
    change = dot3((high_ref[:, :width], low_ref[:, :width]), first)
    change += dot3((high_ref[:, width:], low_ref[:, width:]), second)
    rest_ref[...] = a_ref[...] - change[:rows]
    factor_ref[...] = change[rows:]


def rows_kernel(parts, n, a_ref, high_ref, low_ref, mine_high, mine_low, first_ref, second_ref, *refs):
    rests, factors, (rest_ref, factor_ref, *sums) = refs[:n], refs[n:2 * n], refs[2 * n:]
    width = first_ref.shape[0]

    @pl.when(pl.program_id(0) == 0)
    def _():
        sums[0][...], sums[1][...] = split(first_ref[...])
        sums[2][...], sums[3][...] = split(second_ref[...])

    def update(high, low):
        change = dot3((high[:, :width], low[:, :width]), (sums[0][...], sums[1][...]))
        return change + dot3((high[:, width:], low[:, width:]), (sums[2][...], sums[3][...]))

    def lay(pieces, out_ref):
        part = 0
        for piece in pieces:
            rows = piece.shape[0]
            for at in range(0, piece.shape[1], TILE):
                out_ref[pl.ds(part, rows, stride=parts), :] = piece[:, at:at + TILE]
                part += 1

    lay([*rests, a_ref[...] - update(high_ref, low_ref)], rest_ref)

    @pl.when(pl.program_id(0) == 0)
    def _():
        lay([*factors, update(mine_high, mine_low)], factor_ref)


def in_rows(last, weights, first, second, rests, factors, parts):
    rows, own_rows = last.shape[0], factors[0].shape[0]
    step = min(rows, 128)
    by_rows = lambda v: pl.BlockSpec((step, v.shape[1]), lambda i: (i, 0))
    whole = lambda v: pl.BlockSpec(v.shape, lambda i: (0, 0))
    mine = pl.BlockSpec((own_rows, weights[0].shape[1]), lambda i: (rows // own_rows, 0))
    return pl.pallas_call(
        functools.partial(rows_kernel, parts, len(rests)),
        grid=(rows // step,),
        out_shape=[
            jax.ShapeDtypeStruct((rows * parts, TILE), f32),
            jax.ShapeDtypeStruct((own_rows * parts, TILE), f32),
        ],
        in_specs=[by_rows(last), by_rows(weights[0]), by_rows(weights[1]), mine, mine, whole(first), whole(second)]
        + [by_rows(v) for v in rests] + [whole(v) for v in factors],
        out_specs=[
            pl.BlockSpec((step * parts, TILE), lambda i: (i, 0)),
            pl.BlockSpec((own_rows * parts, TILE), lambda i: (0, 0)),
        ],
        scratch_shapes=[pltpu.VMEM(first.shape, bf16)] * 4,
        name="tiles_to_rows",
        compiler_params=pltpu.CompilerParams(vmem_limit_bytes=24 * 2**20),
    )(last, *weights, *weights, first, second, *rests, *factors)


def local(matrix):
    rows, blocks, _, width = matrix.shape
    parts = blocks * width // TILE
    depth = 2 * width
    n_row, n_col = lax.axis_size("prow"), lax.axis_size("pcol")
    row, col = lax.axis_index("prow"), lax.axis_index("pcol")
    place = row // 2
    line = n_row == 8
    flags = jnp.stack([
        col >= 2, col % 2 == 0, row % 2 == 0, (place == 1) | (place == 2), col, row,
    ]).astype(jnp.int32)
    chain = Chain()
    flat = matrix.reshape(rows * parts, TILE)

    own = [matrix[:, 0, 0, :width // 2], matrix[:, 0, 0, width // 2:]]
    own[1] = jnp.concatenate([own[1], own[1][:EXTRA]], 0)
    came = [lax.ppermute(v, "pcol", [(0, 2), (1, 3)]) for v in own]
    shapes = []
    for count in GROUPS:
        shape = (rows, count * width)
        shapes += [shape, (shape, bf16), (shape, bf16)]
    cuts = chain(functools.partial(spread_kernel, parts), "rows_to_tiles", shapes, flags, flat)
    cuts = [cuts[3 * k:3 * k + 3] for k in range(len(GROUPS))]

    def bring(which, name):
        pieces = (1, PIECES)[which]
        held = chain(
            functools.partial(pick_kernel, 0), name, [(rows // pieces, width // 2)] * pieces, flags,
            came[which], own[which],
        )
        reach = 4
        while reach < n_col:
            pairs = [(i, i + reach) for i in range(reach) if i + reach < n_col]
            at = (col >= reach) & (col < 2 * reach)
            held = [jnp.where(at, lax.ppermute(v, "pcol", pairs), v) for v in held]
            reach *= 2
        return [*held, *[flip(v, "pcol", 1) for v in held]]

    state = {}

    def in_hop(value):
        return lax.ppermute(value, "prow", [(0, 2), (1, 3), (6, 4), (7, 5)]) if line else None

    def mid_hop(value):
        return lax.ppermute(value, "prow", [(2, 4), (3, 5), (4, 2), (5, 3)]) if line else None

    def out_hop(value):
        return lax.ppermute(value, "prow", [(2, 0), (3, 1), (4, 6), (5, 7)]) if line else None

    def add(name, a, b):
        if b is None:
            return a
        return chain(add_kernel, name, [a.shape], flags, a, b)[0]

    def pick_inner(name, a, b):
        if b is None:
            bit = 2
            while bit < n_row:
                a = a + flip(a, "prow", bit)
                bit *= 2
            return a
        return chain(functools.partial(pick_kernel, 3), name, [a.shape], flags, a, b)[0]

    def run(task):
        if task == "ka" or task == "kb":
            state[task] = bring("ab".index(task[1]), task)
        elif task == "pa" or task == "pb":
            half = ((width // 2, rows), bf16)
            state[task] = chain(half_panels_kernel, task, [half] * 4, flags, *state["k" + task[1]])
        elif task == "g4":
            share, = chain(share_kernel, task, [(depth, width)], flags, state["s", 1], state["r", 1])
            state["gr"] = share, flip(share, "pcol", 1)
        elif task == "g6":
            state["gram"], = chain(gather_kernel, task, [(depth, depth)], flags, *state["gr"])
        elif task.startswith("ch"):
            step = int(task[2:])
            operands = [state["gram"]] if step == 0 else state["factor"]
            state["factor"] = chain(
                functools.partial(factor_kernel, step), f"factor{step}", [(depth, depth)] * 2, flags, *operands,
                scratch=[pltpu.VMEM((TILE, TILE), f32)] * 2,
            )
        elif task == "weights":
            cut = ((rows + depth // n_row, depth), bf16)
            state["weights"] = chain(weights_kernel, task, [cut] * 2, flags, *state["ka"], *state["kb"], state["factor"][1])
        else:
            kind, k = task.rstrip("0123456789"), int(task.lstrip("abcdefghijklmnopqrstuvwxyz"))
            group = GROUP_OF[k]
            lines = width if GROUP_OF.count(group) == 1 else width // 2
            halves = [state[p] for p in (("pa",), ("pa", "pb"), ("pb",))[min(k, 1) if k != 2 else 2]]
            shape = (lines, GROUPS[group] * width + (k == 1) * width)
            more = [*state["ka"], *state["kb"]] if k == 1 else []
            if kind == "send":
                pieces = [p[2] for p in halves] + [p[3] for p in halves]
                out, = chain(functools.partial(product_kernel, len(halves), False), task, [shape],
                             flags, *pieces, *cuts[group][1:], *more)
                state["r", k] = flip(out, "prow", 1)
            elif kind == "keep":
                pieces = [p[0] for p in halves] + [p[1] for p in halves]
                out, = chain(functools.partial(product_kernel, len(halves), True), task, [shape],
                             flags, *pieces, *cuts[group][1:], state["r", k], *more)
                state["s", k], state["r", k] = out, in_hop(out)
            elif kind == "zm":
                out = add(task, state["s", k], state["r", k])
                state["s", k], state["r", k] = out, mid_hop(out)
            elif kind == "zo":
                out = add(task, state["s", k], state["r", k])
                state["s", k], state["r", k] = out, out_hop(out)
            elif kind == "ag":
                out = pick_inner(task, state["s", k], state["r", k])
                state["s", k], state["r", k] = out, flip(out, "prow", 1)
            elif kind == "fin":
                pieces = [j for j, g in enumerate(GROUP_OF) if g == group]
                state["out", group] = chain(
                    finish_kernel, task, [(rows, GROUPS[group] * width), (depth // n_row, GROUPS[group] * width)],
                    flags, cuts[group][0], *state["weights"],
                    *[state["s", j] for j in pieces], *[state["r", j] for j in pieces],
                )

    for task in " ".join(ORDER).split():
        if task[0] != "~":
            run(task)
        elif line and ("r", int(task[-1])) in state:
            chain.waits.append(state["r", int(task[-1])])
    end = len(GROUPS) - 1
    outs = [state["out", k] for k in range(end)]
    k = GROUP_OF.index(end)
    rest, factor = in_rows(
        cuts[end][0], state["weights"], state["s", k], state["r", k],
        [o[0] for o in outs], [o[1] for o in outs], parts,
    )
    return (
        factor.reshape(depth // n_row, blocks, 1, width),
        rest.reshape(rows, blocks, 1, width),
    )


def solution(mesh):
    placed = P("prow", None, "pcol", None)
    return jax.shard_map(
        local, mesh=mesh, in_specs=(placed,), out_specs=(placed, placed), check_vma=False
    )
```

```python
import functools

import jax
import jax.numpy as jnp
from jax import lax
from jax.experimental import pallas as pl
from jax.experimental.pallas import tpu as pltpu
from jax.sharding import PartitionSpec as P

highest = lax.Precision.HIGHEST
f32 = jnp.float32
bf16 = jnp.bfloat16
TILE = 128
EXTRA = 32
PIECES = 1
GROUPS = (4, 1, 2, 2, 2)
GROUP_OF = (0, 1, 0, 2, 3, 4)
ORDER = (
    "ka pa send0 kb", "pb send1 send2 send3", "keep0 send4 send5 keep1", "zm0 keep2 zm1 zo0",
    "keep3 zm2 zo1 ~zo0", "keep4 zm3 zo2 ~zo1", "ag0 keep5 zm4 zo3", "~zo2 ag1 ~ag0 zm5",
    "zo4 ~zo3 ag2 g4", "zo5 ~zo4 ag3 g6", "ch0 ~ag2 ag4 ch1", "~zo5 ag5 ~ag3 ch2",
    "ch3 weights fin1 fin0", "fin3 ~ag4 fin4",
)


def dot(a, b):
    return jnp.dot(a, b, precision=highest, preferred_element_type=f32)


def dot_t(a, b):
    return lax.dot_general(a, b, (((0,), (0,)), ((), ())), precision=highest, preferred_element_type=f32)


def dot_nt(a, b):
    return lax.dot_general(a, b, (((1,), (1,)), ((), ())), precision=highest, preferred_element_type=f32)


def split(value):
    high = value.astype(bf16)
    return high, (value - high.astype(f32)).astype(bf16)


def dot3(a, b):
    def product(x, y):
        return jnp.dot(x, y, preferred_element_type=f32)

    return product(a[0], b[0]) + (product(a[0], b[1]) + product(a[1], b[0]))


def flip(value, axis, bit):
    n = lax.axis_size(axis)
    return lax.ppermute(value, axis, [(i, i ^ bit) for i in range(n)])


class Chain:
    def __init__(self):
        self.last = []
        self.waits = []

    def __call__(self, kernel, name, outs, flags, *operands, scratch=(), limit=12):
        after = self.last + self.waits
        n_in, n_after = len(operands), len(after)
        vmem = pl.BlockSpec(memory_space=pltpu.VMEM)

        def body(*refs):
            kernel(refs[0], *refs[1 + n_after:])

        result = pl.pallas_call(
            body,
            out_shape=[jax.ShapeDtypeStruct(*(o if isinstance(o[0], tuple) else (o, f32))) for o in outs],
            in_specs=[pl.BlockSpec(memory_space=pltpu.SMEM)] + [pl.BlockSpec(memory_space=pl.ANY)] * n_after
            + [vmem] * n_in,
            out_specs=[vmem] * len(outs),
            scratch_shapes=list(scratch),
            name=name,
            compiler_params=pltpu.CompilerParams(vmem_limit_bytes=limit * 2**20),
            cost_estimate=pl.CostEstimate(flops=1000, bytes_accessed=1000, transcendentals=0),
        )(flags, *after, *operands)
        self.last = [result[0]]
        self.waits = []
        return result


def spread_kernel(parts, flags, in_ref, *out_refs):
    part = 0
    for out_ref, high_ref, low_ref in zip(out_refs[::3], out_refs[1::3], out_refs[2::3]):
        rows, columns = out_ref.shape
        for at in range(0, columns, TILE):
            cut = slice(at, at + TILE)
            value = in_ref[pl.ds(part, rows, stride=parts), :]
            out_ref[:, cut] = value
            high_ref[:, cut], low_ref[:, cut] = split(value)
            part += 1


def pick_kernel(which, flags, a_ref, b_ref, *out_refs):
    for choice, ref in enumerate((b_ref, a_ref)):
        @pl.when(flags[which] == choice)
        def _():
            at = 0
            for out_ref in out_refs:
                out_ref[...] = ref[at:at + out_ref.shape[0]]
                at += out_ref.shape[0]


def half_panels_kernel(flags, *refs):
    pieces, (keep_high, keep_low, send_high, send_low) = refs[:-4], refs[-4:]
    count = len(pieces) // 2
    held, other = (jnp.concatenate([r[...] for r in part], 0).T for part in (pieces[:count], pieces[count:]))
    same = flags[1] == flags[2]
    keep_high[...], keep_low[...] = split(jnp.where(same, held, other))
    send_high[...], send_low[...] = split(jnp.where(same, other, held))


def joined(refs):
    later = [jnp.concatenate([r[...] for r in part], 0) for part in (refs[2:2 + PIECES], refs[2 + PIECES:])]
    return [jnp.concatenate([r[...], v], 1) for r, v in zip(refs, later)]


def product_kernel(count, kept, flags, *refs):
    highs, lows, (a_high, a_low) = refs[:count], refs[count:2 * count], refs[2 * count:2 * count + 2]
    rest, out_ref = refs[2 * count + 2:-1], refs[-1]
    columns = a_high.shape[1]
    came = rest[0][...] if kept else None
    panel = [jnp.concatenate([r[...] for r in part], 0) for part in (highs, lows)]
    product = dot3(panel, (a_high[...], a_low[...]))
    out_ref[:, :columns] = product + came[:, :columns] if kept else product
    halves = rest[1 if kept else 0:]
    if halves:
        held, other = joined(halves)
        mine = (flags[1] == flags[2]) == kept
        product = dot_t(jnp.where(mine, held, other), held)
        out_ref[:, columns:] = product + came[:, columns:] if kept else product


def share_kernel(flags, keep_ref, other_ref, out_ref):
    width = keep_ref.shape[0]
    first = flags[2] != 0
    keep, other = keep_ref[:, -width:], other_ref[:, -width:]
    out_ref[:width] = jnp.where(first, keep, other)
    out_ref[width:] = jnp.where(first, other, keep)


def gather_kernel(flags, own_ref, other_ref, out_ref):
    width = own_ref.shape[1]
    low = flags[1] != 0
    own, other = own_ref[...], other_ref[...]
    out_ref[:, :width] = jnp.where(low, own, other)
    out_ref[:, width:] = jnp.where(low, other, own)


def add_kernel(flags, a_ref, b_ref, out_ref):
    out_ref[...] = a_ref[...] + b_ref[...]


def eliminate(block, rows_ref, heads_ref):
    size = block.shape[0]
    group = 4
    sub = lax.broadcasted_iota(jnp.int32, (size, size), 0)
    lane = lax.broadcasted_iota(jnp.int32, (size, size), 1)
    left = block
    right = jnp.where(sub == lane, 1.0, 0.0).astype(f32)

    def spread(j):
        return [jnp.broadcast_to(left[:, j + p:j + p + 1], left.shape) for p in range(group)]

    cols = spread(0)
    for j in range(0, size, group):
        at = j % 8
        last = j + group == size
        ahead = [] if last else spread(j + group)
        rows = [left[at + p:at + p + 1] for p in range(group)]
        others = [right[at + p:at + p + 1] for p in range(group)]
        factors = []
        for p in range(group):
            head = cols[p][at + p:at + p + 1]
            factor = cols[p] * (1.0 / head)
            factors.append(factor)
            heads_ref[j + p:j + p + 1, :] = head
            rows_ref[j + p:j + p + 1, :] = others[p]
            for q in range(p + 1, group):
                cols[q] = cols[q] - factor * cols[p][at + q:at + q + 1]
                low = factor[at + q:at + q + 1]
                rows[q] = rows[q] - low * rows[p]
                others[q] = others[q] - low * others[p]
            for q in range(len(ahead)):
                here = at + group + q
                ahead[q] = ahead[q] - factor * cols[p][here:here + 1]
        if last:
            break
        cut = 8 if at + group == 8 else 0
        left, right, cols = left[cut:], right[cut:], [c[cut:] for c in ahead]
        for p in range(group):
            left = left - factors[p][cut:] * rows[p]
            right = right - factors[p][cut:] * others[p]


def factor_kernel(step, flags, *refs):
    if step == 0:
        gram_ref, out_state_ref, out_inv_ref, rows_ref, heads_ref = refs
    else:
        state_ref, inv_ref, out_state_ref, out_inv_ref, rows_ref, heads_ref = refs
    size = out_state_ref.shape[0]
    lo, hi = step * TILE, (step + 1) * TILE
    if step == 0:
        out_state_ref[...] = gram_ref[...]
        sub = lax.broadcasted_iota(jnp.int32, (size, size), 0)
        lane = lax.broadcasted_iota(jnp.int32, (size, size), 1)
        out_inv_ref[...] = jnp.where(sub == lane, 1.0, 0.0).astype(f32)
    else:
        out_state_ref[...] = state_ref[...]
        out_inv_ref[...] = inv_ref[...]
    eliminate(out_state_ref[lo:hi, lo:hi], rows_ref, heads_ref)
    block_inv = rows_ref[...] * lax.rsqrt(heads_ref[...])
    done = dot(block_inv, out_inv_ref[lo:hi, :hi])
    out_inv_ref[lo:hi, :hi] = done
    if hi < size:
        below = dot_nt(out_state_ref[hi:, lo:hi], block_inv)
        out_state_ref[hi:, hi:] = out_state_ref[hi:, hi:] - dot_nt(below, below)
        out_inv_ref[hi:, :hi] = out_inv_ref[hi:, :hi] - dot(below, done)


def weights_kernel(flags, *refs):
    inv_ref, high_ref, low_ref = refs[-3:]
    held, other = joined(refs[:-3])
    rows, width = held.shape
    low_core = flags[1] != 0
    panels = jnp.concatenate([jnp.where(low_core, held, other), jnp.where(low_core, other, held)], 1)
    per_device = high_ref.shape[0] - rows
    inverse = inv_ref[...]
    high, low = split(inverse)
    ortho = split(dot3(split(panels), split(inverse.T)))
    first = flags[2] != 0
    mine = inv_ref[pl.ds(pl.multiple_of(flags[5] * per_device, 8), per_device), :]

    def put(place, left, right):
        high_ref[place, :width], low_ref[place, :width] = split(jnp.where(first, left, right))
        high_ref[place, width:], low_ref[place, width:] = split(jnp.where(first, right, left))

    both = dot3(ortho, (high, low))
    put(slice(0, rows), both[:, :width], both[:, width:])
    put(slice(rows, rows + per_device), mine[:, :width], mine[:, width:])


def finish_kernel(flags, a_ref, high_ref, low_ref, *refs):
    (rest_ref, factor_ref), sums = refs[-2:], refs[:-2]
    rows, columns = a_ref.shape
    count = len(sums) // 2
    first, second = (
        split(jnp.concatenate([r[:, :columns] for r in part], 0)) for part in (sums[:count], sums[count:])
    )
    width = first[0].shape[0]
    change = dot3((high_ref[:, :width], low_ref[:, :width]), first)
    change += dot3((high_ref[:, width:], low_ref[:, width:]), second)
    rest_ref[...] = a_ref[...] - change[:rows]
    factor_ref[...] = change[rows:]


def rows_kernel(parts, n, a_ref, high_ref, low_ref, mine_high, mine_low, first_ref, second_ref, *refs):
    rests, factors, (rest_ref, factor_ref, *sums) = refs[:n], refs[n:2 * n], refs[2 * n:]
    width = first_ref.shape[0]

    @pl.when(pl.program_id(0) == 0)
    def _():
        sums[0][...], sums[1][...] = split(first_ref[...])
        sums[2][...], sums[3][...] = split(second_ref[...])

    def update(high, low):
        change = dot3((high[:, :width], low[:, :width]), (sums[0][...], sums[1][...]))
        return change + dot3((high[:, width:], low[:, width:]), (sums[2][...], sums[3][...]))

    def lay(pieces, out_ref):
        part = 0
        for piece in pieces:
            rows = piece.shape[0]
            for at in range(0, piece.shape[1], TILE):
                out_ref[pl.ds(part, rows, stride=parts), :] = piece[:, at:at + TILE]
                part += 1

    lay([*rests, a_ref[...] - update(high_ref, low_ref)], rest_ref)

    @pl.when(pl.program_id(0) == 0)
    def _():
        lay([*factors, update(mine_high, mine_low)], factor_ref)


def in_rows(last, weights, first, second, rests, factors, parts):
    rows, own_rows = last.shape[0], factors[0].shape[0]
    step = min(rows, 128)
    by_rows = lambda v: pl.BlockSpec((step, v.shape[1]), lambda i: (i, 0))
    whole = lambda v: pl.BlockSpec(v.shape, lambda i: (0, 0))
    mine = pl.BlockSpec((own_rows, weights[0].shape[1]), lambda i: (rows // own_rows, 0))
    return pl.pallas_call(
        functools.partial(rows_kernel, parts, len(rests)),
        grid=(rows // step,),
        out_shape=[
            jax.ShapeDtypeStruct((rows * parts, TILE), f32),
            jax.ShapeDtypeStruct((own_rows * parts, TILE), f32),
        ],
        in_specs=[by_rows(last), by_rows(weights[0]), by_rows(weights[1]), mine, mine, whole(first), whole(second)]
        + [by_rows(v) for v in rests] + [whole(v) for v in factors],
        out_specs=[
            pl.BlockSpec((step * parts, TILE), lambda i: (i, 0)),
            pl.BlockSpec((own_rows * parts, TILE), lambda i: (0, 0)),
        ],
        scratch_shapes=[pltpu.VMEM(first.shape, bf16)] * 4,
        name="tiles_to_rows",
        compiler_params=pltpu.CompilerParams(vmem_limit_bytes=24 * 2**20),
    )(last, *weights, *weights, first, second, *rests, *factors)


def local(matrix):
    rows, blocks, _, width = matrix.shape
    parts = blocks * width // TILE
    depth = 2 * width
    n_row, n_col = lax.axis_size("prow"), lax.axis_size("pcol")
    row, col = lax.axis_index("prow"), lax.axis_index("pcol")
    place = row // 2
    line = n_row == 8
    flags = jnp.stack([
        col >= 2, col % 2 == 0, row % 2 == 0, (place == 1) | (place == 2), col, row,
    ]).astype(jnp.int32)
    chain = Chain()
    flat = matrix.reshape(rows * parts, TILE)

    own = [matrix[:, 0, 0, :width // 2], matrix[:, 0, 0, width // 2:]]
    own[1] = jnp.concatenate([own[1], own[1][:EXTRA]], 0)
    came = [lax.ppermute(v, "pcol", [(0, 2), (1, 3)]) for v in own]
    shapes = []
    for count in GROUPS:
        shape = (rows, count * width)
        shapes += [shape, (shape, bf16), (shape, bf16)]
    cuts = chain(functools.partial(spread_kernel, parts), "rows_to_tiles", shapes, flags, flat, limit=24)
    cuts = [cuts[3 * k:3 * k + 3] for k in range(len(GROUPS))]

    def bring(which, name):
        pieces = (1, PIECES)[which]
        held = chain(
            functools.partial(pick_kernel, 0), name, [(rows // pieces, width // 2)] * pieces, flags,
            came[which], own[which],
        )
        reach = 4
        while reach < n_col:
            pairs = [(i, i + reach) for i in range(reach) if i + reach < n_col]
            at = (col >= reach) & (col < 2 * reach)
            held = [jnp.where(at, lax.ppermute(v, "pcol", pairs), v) for v in held]
            reach *= 2
        return [*held, *[flip(v, "pcol", 1) for v in held]]

    state = {}

    def in_hop(value):
        return lax.ppermute(value, "prow", [(0, 2), (1, 3), (6, 4), (7, 5)]) if line else None

    def mid_hop(value):
        return lax.ppermute(value, "prow", [(2, 4), (3, 5), (4, 2), (5, 3)]) if line else None

    def out_hop(value):
        return lax.ppermute(value, "prow", [(2, 0), (3, 1), (4, 6), (5, 7)]) if line else None

    def add(name, a, b):
        if b is None:
            return a
        return chain(add_kernel, name, [a.shape], flags, a, b)[0]

    def pick_inner(name, a, b):
        if b is None:
            bit = 2
            while bit < n_row:
                a = a + flip(a, "prow", bit)
                bit *= 2
            return a
        return chain(functools.partial(pick_kernel, 3), name, [a.shape], flags, a, b)[0]

    def run(task):
        if task == "ka" or task == "kb":
            state[task] = bring("ab".index(task[1]), task)
        elif task == "pa" or task == "pb":
            half = ((width // 2, rows), bf16)
            state[task] = chain(half_panels_kernel, task, [half] * 4, flags, *state["k" + task[1]])
        elif task == "g4":
            share, = chain(share_kernel, task, [(depth, width)], flags, state["s", 1], state["r", 1])
            state["gr"] = share, flip(share, "pcol", 1)
        elif task == "g6":
            state["gram"], = chain(gather_kernel, task, [(depth, depth)], flags, *state["gr"])
        elif task.startswith("ch"):
            step = int(task[2:])
            operands = [state["gram"]] if step == 0 else state["factor"]
            state["factor"] = chain(
                functools.partial(factor_kernel, step), f"factor{step}", [(depth, depth)] * 2, flags, *operands,
                scratch=[pltpu.VMEM((TILE, TILE), f32)] * 2,
            )
        elif task == "weights":
            cut = ((rows + depth // n_row, depth), bf16)
            state["weights"] = chain(weights_kernel, task, [cut] * 2, flags, *state["ka"], *state["kb"], state["factor"][1])
        else:
            kind, k = task.rstrip("0123456789"), int(task.lstrip("abcdefghijklmnopqrstuvwxyz"))
            group = GROUP_OF[k]
            lines = width if GROUP_OF.count(group) == 1 else width // 2
            halves = [state[p] for p in (("pa",), ("pa", "pb"), ("pb",))[min(k, 1) if k != 2 else 2]]
            shape = (lines, GROUPS[group] * width + (k == 1) * width)
            more = [*state["ka"], *state["kb"]] if k == 1 else []
            if kind == "send":
                pieces = [p[2] for p in halves] + [p[3] for p in halves]
                out, = chain(functools.partial(product_kernel, len(halves), False), task, [shape],
                             flags, *pieces, *cuts[group][1:], *more)
                state["r", k] = flip(out, "prow", 1)
            elif kind == "keep":
                pieces = [p[0] for p in halves] + [p[1] for p in halves]
                out, = chain(functools.partial(product_kernel, len(halves), True), task, [shape],
                             flags, *pieces, *cuts[group][1:], state["r", k], *more)
                state["s", k], state["r", k] = out, in_hop(out)
            elif kind == "zm":
                out = add(task, state["s", k], state["r", k])
                state["s", k], state["r", k] = out, mid_hop(out)
            elif kind == "zo":
                out = add(task, state["s", k], state["r", k])
                state["s", k], state["r", k] = out, out_hop(out)
            elif kind == "ag":
                out = pick_inner(task, state["s", k], state["r", k])
                state["s", k], state["r", k] = out, flip(out, "prow", 1)
            elif kind == "fin":
                pieces = [j for j, g in enumerate(GROUP_OF) if g == group]
                state["out", group] = chain(
                    finish_kernel, task, [(rows, GROUPS[group] * width), (depth // n_row, GROUPS[group] * width)],
                    flags, cuts[group][0], *state["weights"],
                    *[state["s", j] for j in pieces], *[state["r", j] for j in pieces],
                )

    for task in " ".join(ORDER).split():
        if task[0] != "~":
            run(task)
        elif line and ("r", int(task[-1])) in state:
            chain.waits.append(state["r", int(task[-1])])
    end = len(GROUPS) - 1
    outs = [state["out", k] for k in range(end)]
    k = GROUP_OF.index(end)
    rest, factor = in_rows(
        cuts[end][0], state["weights"], state["s", k], state["r", k],
        [o[0] for o in outs], [o[1] for o in outs], parts,
    )
    return (
        factor.reshape(depth // n_row, blocks, 1, width),
        rest.reshape(rows, blocks, 1, width),
    )


def solution(mesh):
    placed = P("prow", None, "pcol", None)
    return jax.shard_map(
        local, mesh=mesh, in_specs=(placed,), out_specs=(placed, placed), check_vma=False
    )
```

```python
import functools

import jax
import jax.numpy as jnp
from jax import lax
from jax.experimental import pallas as pl
from jax.experimental.pallas import tpu as pltpu
from jax.sharding import PartitionSpec as P

highest = lax.Precision.HIGHEST
f32 = jnp.float32
bf16 = jnp.bfloat16
TILE = 128
EXTRA = 32
PIECES = 1
GROUPS = (4, 1, 2, 2, 2)
GROUP_OF = (0, 1, 0, 2, 3, 4)
ORDER = (
    "ka pa send0 kb", "pb send1 send2 send3", "keep0 send4 send5 keep1", "zm0 keep2 zm1 ~send3",
    "zo0 keep3 zm2 zo1", "~zo0 keep4 zm3 zo2", "~zo1 ag0 keep5 zm4", "zo3 ~zo2 ag1 ~ag0",
    "zm5 zo4 ~zo3 ag2", "g4 ~zo4 ag3 zo5", "g6 ch0 ~ag2 ag4", "ch1 ~zo5 ag5 ch2",
    "~ag3 ch3 weights fin1", "fin0 fin3 ~ag4 fin4",
)


def dot(a, b):
    return jnp.dot(a, b, precision=highest, preferred_element_type=f32)


def dot_t(a, b):
    return lax.dot_general(a, b, (((0,), (0,)), ((), ())), precision=highest, preferred_element_type=f32)


def dot_nt(a, b):
    return lax.dot_general(a, b, (((1,), (1,)), ((), ())), precision=highest, preferred_element_type=f32)


def split(value):
    high = value.astype(bf16)
    return high, (value - high.astype(f32)).astype(bf16)


def dot3(a, b):
    def product(x, y):
        return jnp.dot(x, y, preferred_element_type=f32)

    return product(a[0], b[0]) + (product(a[0], b[1]) + product(a[1], b[0]))


def flip(value, axis, bit):
    n = lax.axis_size(axis)
    return lax.ppermute(value, axis, [(i, i ^ bit) for i in range(n)])


class Chain:
    def __init__(self):
        self.last = []
        self.waits = []

    def __call__(self, kernel, name, outs, flags, *operands, scratch=()):
        after = self.last + self.waits
        n_in, n_after = len(operands), len(after)
        vmem = pl.BlockSpec(memory_space=pltpu.VMEM)

        def body(*refs):
            kernel(refs[0], *refs[1 + n_after:])

        result = pl.pallas_call(
            body,
            out_shape=[jax.ShapeDtypeStruct(*(o if isinstance(o[0], tuple) else (o, f32))) for o in outs],
            in_specs=[pl.BlockSpec(memory_space=pltpu.SMEM)] + [pl.BlockSpec(memory_space=pl.ANY)] * n_after
            + [vmem] * n_in,
            out_specs=[vmem] * len(outs),
            scratch_shapes=list(scratch),
            name=name,
            compiler_params=pltpu.CompilerParams(vmem_limit_bytes=24 * 2**20),
            cost_estimate=pl.CostEstimate(flops=1000, bytes_accessed=1000, transcendentals=0),
        )(flags, *after, *operands)
        self.last = [result[0]]
        self.waits = []
        return result


def spread_kernel(parts, flags, in_ref, *out_refs):
    part = 0
    for out_ref, high_ref, low_ref in zip(out_refs[::3], out_refs[1::3], out_refs[2::3]):
        rows, columns = out_ref.shape
        for at in range(0, columns, TILE):
            cut = slice(at, at + TILE)
            value = in_ref[pl.ds(part, rows, stride=parts), :]
            out_ref[:, cut] = value
            high_ref[:, cut], low_ref[:, cut] = split(value)
            part += 1


def pick_kernel(which, flags, a_ref, b_ref, *out_refs):
    for choice, ref in enumerate((b_ref, a_ref)):
        @pl.when(flags[which] == choice)
        def _():
            at = 0
            for out_ref in out_refs:
                out_ref[...] = ref[at:at + out_ref.shape[0]]
                at += out_ref.shape[0]


def half_panels_kernel(flags, *refs):
    pieces, (keep_high, keep_low, send_high, send_low) = refs[:-4], refs[-4:]
    count = len(pieces) // 2
    held, other = (jnp.concatenate([r[...] for r in part], 0).T for part in (pieces[:count], pieces[count:]))
    same = flags[1] == flags[2]
    keep_high[...], keep_low[...] = split(jnp.where(same, held, other))
    send_high[...], send_low[...] = split(jnp.where(same, other, held))


def joined(refs):
    later = [jnp.concatenate([r[...] for r in part], 0) for part in (refs[2:2 + PIECES], refs[2 + PIECES:])]
    return [jnp.concatenate([r[...], v], 1) for r, v in zip(refs, later)]


def product_kernel(count, kept, flags, *refs):
    highs, lows, (a_high, a_low) = refs[:count], refs[count:2 * count], refs[2 * count:2 * count + 2]
    rest, out_ref = refs[2 * count + 2:-1], refs[-1]
    columns = a_high.shape[1]
    came = rest[0][...] if kept else None
    panel = [jnp.concatenate([r[...] for r in part], 0) for part in (highs, lows)]
    product = dot3(panel, (a_high[...], a_low[...]))
    out_ref[:, :columns] = product + came[:, :columns] if kept else product
    halves = rest[1 if kept else 0:]
    if halves:
        held, other = joined(halves)
        mine = (flags[1] == flags[2]) == kept
        product = dot_t(jnp.where(mine, held, other), held)
        out_ref[:, columns:] = product + came[:, columns:] if kept else product


def share_kernel(flags, keep_ref, other_ref, out_ref):
    width = keep_ref.shape[0]
    first = flags[2] != 0
    keep, other = keep_ref[:, -width:], other_ref[:, -width:]
    out_ref[:width] = jnp.where(first, keep, other)
    out_ref[width:] = jnp.where(first, other, keep)


def gather_kernel(flags, own_ref, other_ref, out_ref):
    width = own_ref.shape[1]
    low = flags[1] != 0
    own, other = own_ref[...], other_ref[...]
    out_ref[:, :width] = jnp.where(low, own, other)
    out_ref[:, width:] = jnp.where(low, other, own)


def add_kernel(flags, a_ref, b_ref, out_ref):
    out_ref[...] = a_ref[...] + b_ref[...]


def eliminate(block, rows_ref, heads_ref):
    size = block.shape[0]
    group = 4
    sub = lax.broadcasted_iota(jnp.int32, (size, size), 0)
    lane = lax.broadcasted_iota(jnp.int32, (size, size), 1)
    left = block
    right = jnp.where(sub == lane, 1.0, 0.0).astype(f32)

    def spread(j):
        return [jnp.broadcast_to(left[:, j + p:j + p + 1], left.shape) for p in range(group)]

    cols = spread(0)
    for j in range(0, size, group):
        at = j % 8
        last = j + group == size
        ahead = [] if last else spread(j + group)
        rows = [left[at + p:at + p + 1] for p in range(group)]
        others = [right[at + p:at + p + 1] for p in range(group)]
        factors = []
        for p in range(group):
            head = cols[p][at + p:at + p + 1]
            factor = cols[p] * (1.0 / head)
            factors.append(factor)
            heads_ref[j + p:j + p + 1, :] = head
            rows_ref[j + p:j + p + 1, :] = others[p]
            for q in range(p + 1, group):
                cols[q] = cols[q] - factor * cols[p][at + q:at + q + 1]
                low = factor[at + q:at + q + 1]
                rows[q] = rows[q] - low * rows[p]
                others[q] = others[q] - low * others[p]
            for q in range(len(ahead)):
                here = at + group + q
                ahead[q] = ahead[q] - factor * cols[p][here:here + 1]
        if last:
            break
        cut = 8 if at + group == 8 else 0
        left, right, cols = left[cut:], right[cut:], [c[cut:] for c in ahead]
        for p in range(group):
            left = left - factors[p][cut:] * rows[p]
            right = right - factors[p][cut:] * others[p]


def factor_kernel(step, flags, *refs):
    if step == 0:
        gram_ref, out_state_ref, out_inv_ref, rows_ref, heads_ref = refs
    else:
        state_ref, inv_ref, out_state_ref, out_inv_ref, rows_ref, heads_ref = refs
    size = out_state_ref.shape[0]
    lo, hi = step * TILE, (step + 1) * TILE
    if step == 0:
        out_state_ref[...] = gram_ref[...]
        sub = lax.broadcasted_iota(jnp.int32, (size, size), 0)
        lane = lax.broadcasted_iota(jnp.int32, (size, size), 1)
        out_inv_ref[...] = jnp.where(sub == lane, 1.0, 0.0).astype(f32)
    else:
        out_state_ref[...] = state_ref[...]
        out_inv_ref[...] = inv_ref[...]
    eliminate(out_state_ref[lo:hi, lo:hi], rows_ref, heads_ref)
    block_inv = rows_ref[...] * lax.rsqrt(heads_ref[...])
    done = dot(block_inv, out_inv_ref[lo:hi, :hi])
    out_inv_ref[lo:hi, :hi] = done
    if hi < size:
        below = dot_nt(out_state_ref[hi:, lo:hi], block_inv)
        out_state_ref[hi:, hi:] = out_state_ref[hi:, hi:] - dot_nt(below, below)
        out_inv_ref[hi:, :hi] = out_inv_ref[hi:, :hi] - dot(below, done)


def weights_kernel(flags, *refs):
    inv_ref, high_ref, low_ref = refs[-3:]
    held, other = joined(refs[:-3])
    rows, width = held.shape
    low_core = flags[1] != 0
    panels = jnp.concatenate([jnp.where(low_core, held, other), jnp.where(low_core, other, held)], 1)
    per_device = high_ref.shape[0] - rows
    inverse = inv_ref[...]
    high, low = split(inverse)
    ortho = split(dot3(split(panels), split(inverse.T)))
    first = flags[2] != 0
    mine = inv_ref[pl.ds(pl.multiple_of(flags[5] * per_device, 8), per_device), :]

    def put(place, left, right):
        high_ref[place, :width], low_ref[place, :width] = split(jnp.where(first, left, right))
        high_ref[place, width:], low_ref[place, width:] = split(jnp.where(first, right, left))

    both = dot3(ortho, (high, low))
    put(slice(0, rows), both[:, :width], both[:, width:])
    put(slice(rows, rows + per_device), mine[:, :width], mine[:, width:])


def finish_kernel(flags, a_ref, high_ref, low_ref, *refs):
    (rest_ref, factor_ref), sums = refs[-2:], refs[:-2]
    rows, columns = a_ref.shape
    count = len(sums) // 2
    first, second = (
        split(jnp.concatenate([r[:, :columns] for r in part], 0)) for part in (sums[:count], sums[count:])
    )
    width = first[0].shape[0]
    change = dot3((high_ref[:, :width], low_ref[:, :width]), first)
    change += dot3((high_ref[:, width:], low_ref[:, width:]), second)
    rest_ref[...] = a_ref[...] - change[:rows]
    factor_ref[...] = change[rows:]


def rows_kernel(parts, n, a_ref, high_ref, low_ref, mine_high, mine_low, first_ref, second_ref, *refs):
    rests, factors, (rest_ref, factor_ref, *sums) = refs[:n], refs[n:2 * n], refs[2 * n:]
    width = first_ref.shape[0]

    @pl.when(pl.program_id(0) == 0)
    def _():
        sums[0][...], sums[1][...] = split(first_ref[...])
        sums[2][...], sums[3][...] = split(second_ref[...])

    def update(high, low):
        change = dot3((high[:, :width], low[:, :width]), (sums[0][...], sums[1][...]))
        return change + dot3((high[:, width:], low[:, width:]), (sums[2][...], sums[3][...]))

    def lay(pieces, out_ref):
        part = 0
        for piece in pieces:
            rows = piece.shape[0]
            for at in range(0, piece.shape[1], TILE):
                out_ref[pl.ds(part, rows, stride=parts), :] = piece[:, at:at + TILE]
                part += 1

    lay([*rests, a_ref[...] - update(high_ref, low_ref)], rest_ref)

    @pl.when(pl.program_id(0) == 0)
    def _():
        lay([*factors, update(mine_high, mine_low)], factor_ref)


def in_rows(last, weights, first, second, rests, factors, parts):
    rows, own_rows = last.shape[0], factors[0].shape[0]
    step = min(rows, 128)
    by_rows = lambda v: pl.BlockSpec((step, v.shape[1]), lambda i: (i, 0))
    whole = lambda v: pl.BlockSpec(v.shape, lambda i: (0, 0))
    mine = pl.BlockSpec((own_rows, weights[0].shape[1]), lambda i: (rows // own_rows, 0))
    return pl.pallas_call(
        functools.partial(rows_kernel, parts, len(rests)),
        grid=(rows // step,),
        out_shape=[
            jax.ShapeDtypeStruct((rows * parts, TILE), f32),
            jax.ShapeDtypeStruct((own_rows * parts, TILE), f32),
        ],
        in_specs=[by_rows(last), by_rows(weights[0]), by_rows(weights[1]), mine, mine, whole(first), whole(second)]
        + [by_rows(v) for v in rests] + [whole(v) for v in factors],
        out_specs=[
            pl.BlockSpec((step * parts, TILE), lambda i: (i, 0)),
            pl.BlockSpec((own_rows * parts, TILE), lambda i: (0, 0)),
        ],
        scratch_shapes=[pltpu.VMEM(first.shape, bf16)] * 4,
        name="tiles_to_rows",
        compiler_params=pltpu.CompilerParams(vmem_limit_bytes=24 * 2**20),
    )(last, *weights, *weights, first, second, *rests, *factors)


def local(matrix):
    rows, blocks, _, width = matrix.shape
    parts = blocks * width // TILE
    depth = 2 * width
    n_row, n_col = lax.axis_size("prow"), lax.axis_size("pcol")
    row, col = lax.axis_index("prow"), lax.axis_index("pcol")
    place = row // 2
    line = n_row == 8
    flags = jnp.stack([
        col >= 2, col % 2 == 0, row % 2 == 0, (place == 1) | (place == 2), col, row,
    ]).astype(jnp.int32)
    chain = Chain()
    flat = matrix.reshape(rows * parts, TILE)

    own = [matrix[:, 0, 0, :width // 2], matrix[:, 0, 0, width // 2:]]
    own[1] = jnp.concatenate([own[1], own[1][:EXTRA]], 0)
    came = [lax.ppermute(v, "pcol", [(0, 2), (1, 3)]) for v in own]
    shapes = []
    for count in GROUPS:
        shape = (rows, count * width)
        shapes += [shape, (shape, bf16), (shape, bf16)]
    cuts = chain(functools.partial(spread_kernel, parts), "rows_to_tiles", shapes, flags, flat)
    cuts = [cuts[3 * k:3 * k + 3] for k in range(len(GROUPS))]

    def bring(which, name):
        pieces = (1, PIECES)[which]
        held = chain(
            functools.partial(pick_kernel, 0), name, [(rows // pieces, width // 2)] * pieces, flags,
            came[which], own[which],
        )
        reach = 4
        while reach < n_col:
            pairs = [(i, i + reach) for i in range(reach) if i + reach < n_col]
            at = (col >= reach) & (col < 2 * reach)
            held = [jnp.where(at, lax.ppermute(v, "pcol", pairs), v) for v in held]
            reach *= 2
        return [*held, *[flip(v, "pcol", 1) for v in held]]

    state = {}

    def in_hop(value):
        return lax.ppermute(value, "prow", [(0, 2), (1, 3), (6, 4), (7, 5)]) if line else None

    def mid_hop(value):
        return lax.ppermute(value, "prow", [(2, 4), (3, 5), (4, 2), (5, 3)]) if line else None

    def out_hop(value):
        return lax.ppermute(value, "prow", [(2, 0), (3, 1), (4, 6), (5, 7)]) if line else None

    def add(name, a, b):
        if b is None:
            return a
        return chain(add_kernel, name, [a.shape], flags, a, b)[0]

    def pick_inner(name, a, b):
        if b is None:
            bit = 2
            while bit < n_row:
                a = a + flip(a, "prow", bit)
                bit *= 2
            return a
        return chain(functools.partial(pick_kernel, 3), name, [a.shape], flags, a, b)[0]

    def run(task):
        if task == "ka" or task == "kb":
            state[task] = bring("ab".index(task[1]), task)
        elif task == "pa" or task == "pb":
            half = ((width // 2, rows), bf16)
            state[task] = chain(half_panels_kernel, task, [half] * 4, flags, *state["k" + task[1]])
        elif task == "g4":
            share, = chain(share_kernel, task, [(depth, width)], flags, state["s", 1], state["r", 1])
            state["gr"] = share, flip(share, "pcol", 1)
        elif task == "g6":
            state["gram"], = chain(gather_kernel, task, [(depth, depth)], flags, *state["gr"])
        elif task.startswith("ch"):
            step = int(task[2:])
            operands = [state["gram"]] if step == 0 else state["factor"]
            state["factor"] = chain(
                functools.partial(factor_kernel, step), f"factor{step}", [(depth, depth)] * 2, flags, *operands,
                scratch=[pltpu.VMEM((TILE, TILE), f32)] * 2,
            )
        elif task == "weights":
            cut = ((rows + depth // n_row, depth), bf16)
            state["weights"] = chain(weights_kernel, task, [cut] * 2, flags, *state["ka"], *state["kb"], state["factor"][1])
        else:
            kind, k = task.rstrip("0123456789"), int(task.lstrip("abcdefghijklmnopqrstuvwxyz"))
            group = GROUP_OF[k]
            lines = width if GROUP_OF.count(group) == 1 else width // 2
            halves = [state[p] for p in (("pa",), ("pa", "pb"), ("pb",))[min(k, 1) if k != 2 else 2]]
            shape = (lines, GROUPS[group] * width + (k == 1) * width)
            more = [*state["ka"], *state["kb"]] if k == 1 else []
            if kind == "send":
                pieces = [p[2] for p in halves] + [p[3] for p in halves]
                out, = chain(functools.partial(product_kernel, len(halves), False), task, [shape],
                             flags, *pieces, *cuts[group][1:], *more)
                state["r", k] = flip(out, "prow", 1)
            elif kind == "keep":
                pieces = [p[0] for p in halves] + [p[1] for p in halves]
                out, = chain(functools.partial(product_kernel, len(halves), True), task, [shape],
                             flags, *pieces, *cuts[group][1:], state["r", k], *more)
                state["s", k], state["r", k] = out, in_hop(out)
            elif kind == "zm":
                out = add(task, state["s", k], state["r", k])
                state["s", k], state["r", k] = out, mid_hop(out)
            elif kind == "zo":
                out = add(task, state["s", k], state["r", k])
                state["s", k], state["r", k] = out, out_hop(out)
            elif kind == "ag":
                out = pick_inner(task, state["s", k], state["r", k])
                state["s", k], state["r", k] = out, flip(out, "prow", 1)
            elif kind == "fin":
                pieces = [j for j, g in enumerate(GROUP_OF) if g == group]
                state["out", group] = chain(
                    finish_kernel, task, [(rows, GROUPS[group] * width), (depth // n_row, GROUPS[group] * width)],
                    flags, cuts[group][0], *state["weights"],
                    *[state["s", j] for j in pieces], *[state["r", j] for j in pieces],
                )

    for task in " ".join(ORDER).split():
        if task[0] != "~":
            run(task)
        elif line and ("r", int(task[-1])) in state:
            chain.waits.append(state["r", int(task[-1])])
    end = len(GROUPS) - 1
    outs = [state["out", k] for k in range(end)]
    k = GROUP_OF.index(end)
    rest, factor = in_rows(
        cuts[end][0], state["weights"], state["s", k], state["r", k],
        [o[0] for o in outs], [o[1] for o in outs], parts,
    )
    return (
        factor.reshape(depth // n_row, blocks, 1, width),
        rest.reshape(rows, blocks, 1, width),
    )


def solution(mesh):
    placed = P("prow", None, "pcol", None)
    return jax.shard_map(
        local, mesh=mesh, in_specs=(placed,), out_specs=(placed, placed), check_vma=False
    )
```

```python
import functools

import jax
import jax.numpy as jnp
from jax import lax
from jax.experimental import pallas as pl
from jax.experimental.pallas import tpu as pltpu
from jax.sharding import PartitionSpec as P

highest = lax.Precision.HIGHEST
f32 = jnp.float32
bf16 = jnp.bfloat16
TILE = 128
EXTRA = 32
PIECES = 1
GROUPS = (4, 1, 2, 2, 2)
GROUP_OF = (0, 1, 0, 2, 3, 4)
ORDER = (
    "ka pa send0 kb", "pb send1 send2 send3", "keep0 send4 send5 keep1", "zm0 keep2 zm1 zo0",
    "keep3 zm2 zo1 ~zo0", "keep4 zm3 zo2 ~zo1", "ag0 keep5 zm4 zo3", "~zo2 ag1 ~ag0 zm5",
    "zo4 ~zo3 ag2 g4", "~zo4 ag3 zo5 g6", "ch0 ~ag2 ag4 ch1", "~zo5 ag5 ch2 ~ag3",
    "ch3 weights fin1 fin0", "fin3 ~ag4 fin4",
)


def dot(a, b):
    return jnp.dot(a, b, precision=highest, preferred_element_type=f32)


def dot_t(a, b):
    return lax.dot_general(a, b, (((0,), (0,)), ((), ())), precision=highest, preferred_element_type=f32)


def dot_nt(a, b):
    return lax.dot_general(a, b, (((1,), (1,)), ((), ())), precision=highest, preferred_element_type=f32)


def split(value):
    high = value.astype(bf16)
    return high, (value - high.astype(f32)).astype(bf16)


def dot3(a, b):
    def product(x, y):
        return jnp.dot(x, y, preferred_element_type=f32)

    return product(a[0], b[0]) + (product(a[0], b[1]) + product(a[1], b[0]))


def flip(value, axis, bit):
    n = lax.axis_size(axis)
    return lax.ppermute(value, axis, [(i, i ^ bit) for i in range(n)])


class Chain:
    def __init__(self):
        self.last = []
        self.waits = []

    def __call__(self, kernel, name, outs, flags, *operands, scratch=()):
        after = self.last + self.waits
        n_in, n_after = len(operands), len(after)
        vmem = pl.BlockSpec(memory_space=pltpu.VMEM)

        def body(*refs):
            kernel(refs[0], *refs[1 + n_after:])

        result = pl.pallas_call(
            body,
            out_shape=[jax.ShapeDtypeStruct(*(o if isinstance(o[0], tuple) else (o, f32))) for o in outs],
            in_specs=[pl.BlockSpec(memory_space=pltpu.SMEM)] + [pl.BlockSpec(memory_space=pl.ANY)] * n_after
            + [vmem] * n_in,
            out_specs=[vmem] * len(outs),
            scratch_shapes=list(scratch),
            name=name,
            compiler_params=pltpu.CompilerParams(vmem_limit_bytes=24 * 2**20),
            cost_estimate=pl.CostEstimate(flops=1000, bytes_accessed=1000, transcendentals=0),
        )(flags, *after, *operands)
        self.last = [result[0]]
        self.waits = []
        return result


def spread_kernel(parts, flags, in_ref, *out_refs):
    part = 0
    for out_ref, high_ref, low_ref in zip(out_refs[::3], out_refs[1::3], out_refs[2::3]):
        rows, columns = out_ref.shape
        for at in range(0, columns, TILE):
            cut = slice(at, at + TILE)
            value = in_ref[pl.ds(part, rows, stride=parts), :]
            out_ref[:, cut] = value
            high_ref[:, cut], low_ref[:, cut] = split(value)
            part += 1


def pick_kernel(which, flags, a_ref, b_ref, *out_refs):
    for choice, ref in enumerate((b_ref, a_ref)):
        @pl.when(flags[which] == choice)
        def _():
            at = 0
            for out_ref in out_refs:
                out_ref[...] = ref[at:at + out_ref.shape[0]]
                at += out_ref.shape[0]


def half_panels_kernel(flags, *refs):
    pieces, (keep_high, keep_low, send_high, send_low) = refs[:-4], refs[-4:]
    count = len(pieces) // 2
    held, other = (jnp.concatenate([r[...] for r in part], 0).T for part in (pieces[:count], pieces[count:]))
    same = flags[1] == flags[2]
    keep_high[...], keep_low[...] = split(jnp.where(same, held, other))
    send_high[...], send_low[...] = split(jnp.where(same, other, held))


def joined(refs):
    later = [jnp.concatenate([r[...] for r in part], 0) for part in (refs[2:2 + PIECES], refs[2 + PIECES:])]
    return [jnp.concatenate([r[...], v], 1) for r, v in zip(refs, later)]


def product_kernel(count, kept, flags, *refs):
    highs, lows, (a_high, a_low) = refs[:count], refs[count:2 * count], refs[2 * count:2 * count + 2]
    rest, out_ref = refs[2 * count + 2:-1], refs[-1]
    columns = a_high.shape[1]
    came = rest[0][...] if kept else None
    panel = [jnp.concatenate([r[...] for r in part], 0) for part in (highs, lows)]
    product = dot3(panel, (a_high[...], a_low[...]))
    out_ref[:, :columns] = product + came[:, :columns] if kept else product
    halves = rest[1 if kept else 0:]
    if halves:
        held, other = joined(halves)
        mine = (flags[1] == flags[2]) == kept
        product = dot_t(jnp.where(mine, held, other), held)
        out_ref[:, columns:] = product + came[:, columns:] if kept else product


def share_kernel(flags, keep_ref, other_ref, out_ref):
    width = keep_ref.shape[0]
    first = flags[2] != 0
    keep, other = keep_ref[:, -width:], other_ref[:, -width:]
    out_ref[:width] = jnp.where(first, keep, other)
    out_ref[width:] = jnp.where(first, other, keep)


def gather_kernel(flags, own_ref, other_ref, out_ref):
    width = own_ref.shape[1]
    low = flags[1] != 0
    own, other = own_ref[...], other_ref[...]
    out_ref[:, :width] = jnp.where(low, own, other)
    out_ref[:, width:] = jnp.where(low, other, own)


def add_kernel(flags, a_ref, b_ref, out_ref):
    out_ref[...] = a_ref[...] + b_ref[...]


def eliminate(block, rows_ref, heads_ref):
    size = block.shape[0]
    group = 4
    sub = lax.broadcasted_iota(jnp.int32, (size, size), 0)
    lane = lax.broadcasted_iota(jnp.int32, (size, size), 1)
    left = block
    right = jnp.where(sub == lane, 1.0, 0.0).astype(f32)

    def spread(j):
        return [jnp.broadcast_to(left[:, j + p:j + p + 1], left.shape) for p in range(group)]

    cols = spread(0)
    for j in range(0, size, group):
        at = j % 8
        last = j + group == size
        ahead = [] if last else spread(j + group)
        rows = [left[at + p:at + p + 1] for p in range(group)]
        others = [right[at + p:at + p + 1] for p in range(group)]
        factors = []
        for p in range(group):
            head = cols[p][at + p:at + p + 1]
            factor = cols[p] * (1.0 / head)
            factors.append(factor)
            heads_ref[j + p:j + p + 1, :] = head
            rows_ref[j + p:j + p + 1, :] = others[p]
            for q in range(p + 1, group):
                cols[q] = cols[q] - factor * cols[p][at + q:at + q + 1]
                low = factor[at + q:at + q + 1]
                rows[q] = rows[q] - low * rows[p]
                others[q] = others[q] - low * others[p]
            for q in range(len(ahead)):
                here = at + group + q
                ahead[q] = ahead[q] - factor * cols[p][here:here + 1]
        if last:
            break
        cut = 8 if at + group == 8 else 0
        left, right, cols = left[cut:], right[cut:], [c[cut:] for c in ahead]
        for p in range(group):
            left = left - factors[p][cut:] * rows[p]
            right = right - factors[p][cut:] * others[p]


def factor_kernel(step, flags, *refs):
    if step == 0:
        gram_ref, out_state_ref, out_inv_ref, rows_ref, heads_ref = refs
    else:
        state_ref, inv_ref, out_state_ref, out_inv_ref, rows_ref, heads_ref = refs
    size = out_state_ref.shape[0]
    lo, hi = step * TILE, (step + 1) * TILE
    if step == 0:
        out_state_ref[...] = gram_ref[...]
        sub = lax.broadcasted_iota(jnp.int32, (size, size), 0)
        lane = lax.broadcasted_iota(jnp.int32, (size, size), 1)
        out_inv_ref[...] = jnp.where(sub == lane, 1.0, 0.0).astype(f32)
    else:
        out_state_ref[...] = state_ref[...]
        out_inv_ref[...] = inv_ref[...]
    eliminate(out_state_ref[lo:hi, lo:hi], rows_ref, heads_ref)
    block_inv = rows_ref[...] * lax.rsqrt(heads_ref[...])
    done = dot(block_inv, out_inv_ref[lo:hi, :hi])
    out_inv_ref[lo:hi, :hi] = done
    if hi < size:
        below = dot_nt(out_state_ref[hi:, lo:hi], block_inv)
        out_state_ref[hi:, hi:] = out_state_ref[hi:, hi:] - dot_nt(below, below)
        out_inv_ref[hi:, :hi] = out_inv_ref[hi:, :hi] - dot(below, done)


def weights_kernel(flags, *refs):
    inv_ref, high_ref, low_ref = refs[-3:]
    held, other = joined(refs[:-3])
    rows, width = held.shape
    low_core = flags[1] != 0
    panels = jnp.concatenate([jnp.where(low_core, held, other), jnp.where(low_core, other, held)], 1)
    per_device = high_ref.shape[0] - rows
    inverse = inv_ref[...]
    high, low = split(inverse)
    ortho = split(dot3(split(panels), split(inverse.T)))
    first = flags[2] != 0
    mine = inv_ref[pl.ds(pl.multiple_of(flags[5] * per_device, 8), per_device), :]

    def put(place, left, right):
        high_ref[place, :width], low_ref[place, :width] = split(jnp.where(first, left, right))
        high_ref[place, width:], low_ref[place, width:] = split(jnp.where(first, right, left))

    both = dot3(ortho, (high, low))
    put(slice(0, rows), both[:, :width], both[:, width:])
    put(slice(rows, rows + per_device), mine[:, :width], mine[:, width:])


def finish_kernel(flags, a_ref, high_ref, low_ref, *refs):
    (rest_ref, factor_ref), sums = refs[-2:], refs[:-2]
    rows, columns = a_ref.shape
    count = len(sums) // 2
    first, second = (
        split(jnp.concatenate([r[:, :columns] for r in part], 0)) for part in (sums[:count], sums[count:])
    )
    width = first[0].shape[0]
    change = dot3((high_ref[:, :width], low_ref[:, :width]), first)
    change += dot3((high_ref[:, width:], low_ref[:, width:]), second)
    rest_ref[...] = a_ref[...] - change[:rows]
    factor_ref[...] = change[rows:]


def rows_kernel(parts, n, a_ref, high_ref, low_ref, mine_high, mine_low, first_ref, second_ref, *refs):
    rests, factors, (rest_ref, factor_ref, *sums) = refs[:n], refs[n:2 * n], refs[2 * n:]
    width = first_ref.shape[0]

    @pl.when(pl.program_id(0) == 0)
    def _():
        sums[0][...], sums[1][...] = split(first_ref[...])
        sums[2][...], sums[3][...] = split(second_ref[...])

    def update(high, low):
        change = dot3((high[:, :width], low[:, :width]), (sums[0][...], sums[1][...]))
        return change + dot3((high[:, width:], low[:, width:]), (sums[2][...], sums[3][...]))

    def lay(pieces, out_ref):
        part = 0
        for piece in pieces:
            rows = piece.shape[0]
            for at in range(0, piece.shape[1], TILE):
                out_ref[pl.ds(part, rows, stride=parts), :] = piece[:, at:at + TILE]
                part += 1

    lay([*rests, a_ref[...] - update(high_ref, low_ref)], rest_ref)

    @pl.when(pl.program_id(0) == 0)
    def _():
        lay([*factors, update(mine_high, mine_low)], factor_ref)


def in_rows(last, weights, first, second, rests, factors, parts):
    rows, own_rows = last.shape[0], factors[0].shape[0]
    step = min(rows, 128)
    by_rows = lambda v: pl.BlockSpec((step, v.shape[1]), lambda i: (i, 0))
    whole = lambda v: pl.BlockSpec(v.shape, lambda i: (0, 0))
    mine = pl.BlockSpec((own_rows, weights[0].shape[1]), lambda i: (rows // own_rows, 0))
    return pl.pallas_call(
        functools.partial(rows_kernel, parts, len(rests)),
        grid=(rows // step,),
        out_shape=[
            jax.ShapeDtypeStruct((rows * parts, TILE), f32),
            jax.ShapeDtypeStruct((own_rows * parts, TILE), f32),
        ],
        in_specs=[by_rows(last), by_rows(weights[0]), by_rows(weights[1]), mine, mine, whole(first), whole(second)]
        + [by_rows(v) for v in rests] + [whole(v) for v in factors],
        out_specs=[
            pl.BlockSpec((step * parts, TILE), lambda i: (i, 0)),
            pl.BlockSpec((own_rows * parts, TILE), lambda i: (0, 0)),
        ],
        scratch_shapes=[pltpu.VMEM(first.shape, bf16)] * 4,
        name="tiles_to_rows",
        compiler_params=pltpu.CompilerParams(vmem_limit_bytes=24 * 2**20),
    )(last, *weights, *weights, first, second, *rests, *factors)


def local(matrix):
    rows, blocks, _, width = matrix.shape
    parts = blocks * width // TILE
    depth = 2 * width
    n_row, n_col = lax.axis_size("prow"), lax.axis_size("pcol")
    row, col = lax.axis_index("prow"), lax.axis_index("pcol")
    place = row // 2
    line = n_row == 8
    flags = jnp.stack([
        col >= 2, col % 2 == 0, row % 2 == 0, (place == 1) | (place == 2), col, row,
    ]).astype(jnp.int32)
    chain = Chain()
    flat = matrix.reshape(rows * parts, TILE)

    own = [matrix[:, 0, 0, :width // 2], matrix[:, 0, 0, width // 2:]]
    own[1] = jnp.concatenate([own[1], own[1][:EXTRA]], 0)
    came = [lax.ppermute(v, "pcol", [(0, 2), (1, 3)]) for v in own]
    shapes = []
    for count in GROUPS:
        shape = (rows, count * width)
        shapes += [shape, (shape, bf16), (shape, bf16)]
    cuts = chain(functools.partial(spread_kernel, parts), "rows_to_tiles", shapes, flags, flat)
    cuts = [cuts[3 * k:3 * k + 3] for k in range(len(GROUPS))]

    def bring(which, name):
        pieces = (1, PIECES)[which]
        held = chain(
            functools.partial(pick_kernel, 0), name, [(rows // pieces, width // 2)] * pieces, flags,
            came[which], own[which],
        )
        reach = 4
        while reach < n_col:
            pairs = [(i, i + reach) for i in range(reach) if i + reach < n_col]
            at = (col >= reach) & (col < 2 * reach)
            held = [jnp.where(at, lax.ppermute(v, "pcol", pairs), v) for v in held]
            reach *= 2
        return [*held, *[flip(v, "pcol", 1) for v in held]]

    state = {}

    def in_hop(value):
        return lax.ppermute(value, "prow", [(0, 2), (1, 3), (6, 4), (7, 5)]) if line else None

    def mid_hop(value):
        return lax.ppermute(value, "prow", [(2, 4), (3, 5), (4, 2), (5, 3)]) if line else None

    def out_hop(value):
        return lax.ppermute(value, "prow", [(2, 0), (3, 1), (4, 6), (5, 7)]) if line else None

    def add(name, a, b):
        if b is None:
            return a
        return chain(add_kernel, name, [a.shape], flags, a, b)[0]

    def pick_inner(name, a, b):
        if b is None:
            bit = 2
            while bit < n_row:
                a = a + flip(a, "prow", bit)
                bit *= 2
            return a
        return chain(functools.partial(pick_kernel, 3), name, [a.shape], flags, a, b)[0]

    def run(task):
        if task == "ka" or task == "kb":
            state[task] = bring("ab".index(task[1]), task)
        elif task == "pa" or task == "pb":
            half = ((width // 2, rows), bf16)
            state[task] = chain(half_panels_kernel, task, [half] * 4, flags, *state["k" + task[1]])
        elif task == "g4":
            share, = chain(share_kernel, task, [(depth, width)], flags, state["s", 1], state["r", 1])
            state["gr"] = share, flip(share, "pcol", 1)
        elif task == "g6":
            state["gram"], = chain(gather_kernel, task, [(depth, depth)], flags, *state["gr"])
        elif task.startswith("ch"):
            step = int(task[2:])
            operands = [state["gram"]] if step == 0 else state["factor"]
            state["factor"] = chain(
                functools.partial(factor_kernel, step), f"factor{step}", [(depth, depth)] * 2, flags, *operands,
                scratch=[pltpu.VMEM((TILE, TILE), f32)] * 2,
            )
        elif task == "weights":
            cut = ((rows + depth // n_row, depth), bf16)
            state["weights"] = chain(weights_kernel, task, [cut] * 2, flags, *state["ka"], *state["kb"], state["factor"][1])
        else:
            kind, k = task.rstrip("0123456789"), int(task.lstrip("abcdefghijklmnopqrstuvwxyz"))
            group = GROUP_OF[k]
            lines = width if GROUP_OF.count(group) == 1 else width // 2
            halves = [state[p] for p in (("pa",), ("pa", "pb"), ("pb",))[min(k, 1) if k != 2 else 2]]
            shape = (lines, GROUPS[group] * width + (k == 1) * width)
            more = [*state["ka"], *state["kb"]] if k == 1 else []
            if kind == "send":
                pieces = [p[2] for p in halves] + [p[3] for p in halves]
                out, = chain(functools.partial(product_kernel, len(halves), False), task, [shape],
                             flags, *pieces, *cuts[group][1:], *more)
                state["r", k] = flip(out, "prow", 1)
            elif kind == "keep":
                pieces = [p[0] for p in halves] + [p[1] for p in halves]
                out, = chain(functools.partial(product_kernel, len(halves), True), task, [shape],
                             flags, *pieces, *cuts[group][1:], state["r", k], *more)
                state["s", k], state["r", k] = out, in_hop(out)
            elif kind == "zm":
                out = add(task, state["s", k], state["r", k])
                state["s", k], state["r", k] = out, mid_hop(out)
            elif kind == "zo":
                out = add(task, state["s", k], state["r", k])
                state["s", k], state["r", k] = out, out_hop(out)
            elif kind == "ag":
                out = pick_inner(task, state["s", k], state["r", k])
                state["s", k], state["r", k] = out, flip(out, "prow", 1)
            elif kind == "fin":
                pieces = [j for j, g in enumerate(GROUP_OF) if g == group]
                state["out", group] = chain(
                    finish_kernel, task, [(rows, GROUPS[group] * width), (depth // n_row, GROUPS[group] * width)],
                    flags, cuts[group][0], *state["weights"],
                    *[state["s", j] for j in pieces], *[state["r", j] for j in pieces],
                )

    for task in " ".join(ORDER).split():
        if task[0] != "~":
            run(task)
        elif line and ("r", int(task[-1])) in state:
            chain.waits.append(state["r", int(task[-1])])
    end = len(GROUPS) - 1
    outs = [state["out", k] for k in range(end)]
    k = GROUP_OF.index(end)
    rest, factor = in_rows(
        cuts[end][0], state["weights"], state["s", k], state["r", k],
        [o[0] for o in outs], [o[1] for o in outs], parts,
    )
    return (
        factor.reshape(depth // n_row, blocks, 1, width),
        rest.reshape(rows, blocks, 1, width),
    )


def solution(mesh):
    placed = P("prow", None, "pcol", None)
    return jax.shard_map(
        local, mesh=mesh, in_specs=(placed,), out_specs=(placed, placed), check_vma=False
    )
```
